32 devices in a mesh: rows: 4 (over x, core), seq: 8 (over z, y).
Axes of the slice: x: 2, y: 2, z: 4, core: 2. Of those that a mesh axis runs over, the one named last changes fastest.
Arguments:
- tokens: bfloat16 [2, 4, 1152, 512], P(None, 'rows', 'seq'), may hold values from -6 to 6
- segments: int32 [2, 4, 1152], P(None, 'rows', 'seq'), may hold values from 0 to 24, as said below
- cotangent: bfloat16 [2, 4, 1152, 512], P(None, 'rows', 'seq'), may hold values from -6 to 6
- gain_attn: bfloat16 [512], replicated, may hold values from 0.5 to 1.5
- w_query: bfloat16 [512, 512], replicated, may hold values from -0.25 to 0.25
- w_key: bfloat16 [512, 512], replicated, may hold values from -0.25 to 0.25
- w_value: bfloat16 [512, 512], replicated, may hold values from -0.25 to 0.25
- conv_key: bfloat16 [1536, 512], replicated, may hold values from -0.15625 to 0.15625
- conv_value: bfloat16 [1536, 512], replicated, may hold values from -0.15625 to 0.15625
- w_out: bfloat16 [512, 512], replicated, may hold values from -1 to 1
- gain_ffn: bfloat16 [512], replicated, may hold values from 0.5 to 1.5
- w_up: bfloat16 [512, 2048], replicated, may hold values from -0.25 to 0.25
- w_down: bfloat16 [2048, 512], replicated, may hold values from -0.125 to 0.125
Outputs:
- layer_out: bfloat16 [2, 4, 1152, 512], P(None, 'rows', 'seq')
- grad_tokens: bfloat16 [2, 4, 1152, 512], P(None, 'rows', 'seq')
- grad_gain_attn: float32 [512], replicated
- grad_w_query: float32 [512, 512], replicated
- grad_w_key: float32 [512, 512], replicated
- grad_w_value: float32 [512, 512], replicated
- grad_conv_key: float32 [1536, 512], replicated
- grad_conv_value: float32 [1536, 512], replicated
- grad_w_out: float32 [512, 512], replicated
- grad_gain_ffn: float32 [512], replicated
- grad_w_up: float32 [512, 2048], replicated
- grad_w_down: float32 [2048, 512], replicated
The draws below stay inside these ranges and needn't reach their ends.
Inputs may be any that keep to these rules, and one draw needn't show every extreme that they name: `segments`: along each row document numbers start at 0 at the first position, never fall and rise by at most one from a position to the next; a document may begin at any position.
All inputs are finite; a program needn't handle non-finite values.
Results may differ from the reference program's by a relative error of at most 0.015.
Values may be sent and summed in bfloat16 or wider, within the bound.
No kernel may reach another device: no remote copies, remote signals or barrier semaphores. Data moves between devices by JAX's collectives and lax.ppermute only.
A program may use at most 192 MiB of HBM per device.

```python
import math
import jax
import jax.numpy as jnp
from jax import lax

D = 512
HEADS = 8
HEAD_DIM = 64
FF = 2048
MB = 2
ROWS_DEV = 1
SHARD = 144
ROWS = 4
LEN = 1152


def position_ranks(row_key):
    order = jax.random.permutation(row_key, LEN - 1)
    return jnp.argsort(order).astype(jnp.int32)


def draw_segments(key, part):
    key = jax.random.fold_in(key, 11)
    rows_all = MB * ROWS
    pick_key, start_key, end_key, edge_key, order_key = jax.random.split(key, 5)
    positions = jnp.arange(LEN, dtype=jnp.int32)
    long_start = jax.random.randint(start_key, (rows_all, 1), 1, SHARD)
    long_end = jax.random.randint(end_key, (rows_all, 1), LEN - SHARD + 1, LEN)
    long_starts = (positions[None, :] == long_start) | (positions[None, :] == long_end)
    cuts = min(24, LEN // 8)
    edge = SHARD * jax.random.randint(edge_key, (rows_all, 1), 1, LEN // SHARD)
    ranks = jax.vmap(position_ranks)(jax.random.split(order_key, rows_all))
    ranks_full = jnp.concatenate([jnp.full((rows_all, 1), LEN, jnp.int32), ranks], axis=1)
    is_edge = positions[None, :] == edge
    edge_rank = jnp.sum(jnp.where(is_edge, ranks_full, 0), axis=1, keepdims=True)
    limit = cuts - 1 + (edge_rank < cuts - 1).astype(jnp.int32)
    many_starts = (ranks_full < limit) | is_edge
    group_count = ROWS // ROWS_DEV
    chosen = jax.random.randint(pick_key, (group_count,), 0, MB * ROWS_DEV)
    row_ids = jnp.arange(rows_all, dtype=jnp.int32)
    batch_index = row_ids // ROWS
    row_index = row_ids % ROWS
    member = batch_index * ROWS_DEV + row_index % ROWS_DEV
    group_of = row_index // ROWS_DEV
    group_match = group_of[:, None] == jnp.arange(group_count, dtype=jnp.int32)[None, :]
    chosen_here = jnp.sum(jnp.where(group_match, chosen[None, :], 0), axis=1)
    is_long = chosen_here == member
    starts = jnp.where(is_long[:, None], long_starts, many_starts).astype(jnp.int32)
    return jnp.cumsum(starts, axis=1).astype(jnp.int32).reshape(MB, ROWS, LEN)


def levels(own_key, dims, shards, low, top_value):
    loudness = 1.0
    for dim, parts in shards:
        steps = jax.random.uniform(jax.random.fold_in(jax.random.fold_in(own_key, 6), dim), (parts,), jnp.float32, low / len(shards), top_value / len(shards))
        loudness = loudness * jnp.repeat(jnp.exp(steps), dims[dim] // parts).reshape((-1,) + (1,) * (len(dims) - 1 - dim))
    return loudness


def bell_draw(key, dims, width, most, pieces=(), held_as=jnp.bfloat16):
    values = width * jax.random.normal(key, dims, jnp.float32)
    if pieces:
        values = values * levels(key, dims, pieces, -0.22, 0.18)
    return jnp.clip(values, -most, most).astype(held_as)


def setup_inputs(seed: int = 0) -> dict:
    arg_keys = jax.random.split(jax.random.key(seed), 14)
    return {
        "tokens": bell_draw(arg_keys[0], (MB, ROWS, LEN, D), 1.0, 6.0, ((1, 4), (2, 8))),
        "segments": draw_segments(jax.random.fold_in(arg_keys[13], 71), 0),
        "cotangent": bell_draw(arg_keys[2], (MB, ROWS, LEN, D), 1.0, 6.0, ((1, 4), (2, 8))),
        "gain_attn": jnp.clip(1.0 + 0.1 * jax.random.normal(arg_keys[3], (D,), jnp.float32), 0.5, 1.5).astype(jnp.bfloat16),
        "w_query": bell_draw(arg_keys[4], (D, D), D ** -0.5, 0.25),
        "w_key": bell_draw(arg_keys[5], (D, D), D ** -0.5, 0.25),
        "w_value": bell_draw(arg_keys[6], (D, D), D ** -0.5, 0.25),
        "conv_key": bell_draw(arg_keys[7], (3 * D, D), (3 * D) ** -0.5, 0.15625),
        "conv_value": bell_draw(arg_keys[8], (3 * D, D), (3 * D) ** -0.5, 0.15625),
        "w_out": bell_draw(arg_keys[9], (D, D), (D // 16) ** -0.5, 1.0),
        "gain_ffn": jnp.clip(1.0 + 0.1 * jax.random.normal(arg_keys[10], (D,), jnp.float32), 0.5, 1.5).astype(jnp.bfloat16),
        "w_up": bell_draw(arg_keys[11], (D, FF), D ** -0.5, 0.25),
        "w_down": bell_draw(arg_keys[12], (FF, D), FF ** -0.5, 0.125),
    }


EPSILON = 1e-05
MASKED_OUT = -1e+30

@jax.custom_vjp
def low(v):
    return lax.optimization_barrier(v.astype(jnp.bfloat16)).astype(jnp.float32)

@jax.custom_vjp
def low_back(v):
    return v

def low_keep(v):
    return (low(v), None)

def low_pass(kept, grad):
    return (grad,)

def back_keep(v):
    return (v, None)

def back_low(kept, grad):
    return (low(grad),)
low.defvjp(low_keep, low_pass)
low_back.defvjp(back_keep, back_low)

def matmul(operand, matrix):
    return jnp.dot(operand, matrix, precision=lax.Precision.HIGHEST)

def normalize(values):
    average = lax.optimization_barrier(jnp.mean(values, axis=-1, keepdims=True))
    centred = values - average
    variance = lax.optimization_barrier(jnp.mean(centred * centred, axis=-1, keepdims=True))
    return centred * lax.rsqrt(variance + EPSILON)

def attend(queries, key_rows, value_rows, packed_key, packed_value, segment_row, slot_segment):
    length = queries.shape[0]
    block_len = math.gcd(length, 512)
    block_count = length // block_len
    slot_total = packed_key.shape[0]
    key_heads = packed_key.reshape(slot_total, HEADS, HEAD_DIM)
    value_heads = packed_value.reshape(slot_total, HEADS, HEAD_DIM)
    slot_end = 3 * jnp.arange(slot_total, dtype=jnp.int32) + 2
    positions = jnp.arange(length, dtype=jnp.int32)
    score_scale = HEAD_DIM ** (-0.5)

    def query_block(inputs):
        query_part, key_part, value_part, segment_part, place_part = inputs
        scores = low_back(jnp.einsum('qhe,jhe->hqj', query_part, key_heads, precision=lax.Precision.HIGHEST) * score_scale)
        own_score = low_back(lax.optimization_barrier(jnp.sum(query_part * key_part, axis=-1)).T * score_scale)
        visible_now = (slot_end[None, :] <= place_part[:, None]) & (slot_segment[None, :] == segment_part[:, None])
        masked = jnp.where(visible_now[None], scores, MASKED_OUT)
        log_total = jax.nn.logsumexp(jnp.concatenate([masked, own_score[..., None]], axis=-1), axis=-1)
        weight = low(jnp.exp(masked - log_total[..., None]))
        own_weight = low(jnp.exp(own_score - log_total))
        result = jnp.einsum('hqj,jhe->qhe', weight, value_heads, precision=lax.Precision.HIGHEST)
        return result + own_weight.T[..., None] * value_part
    blocks_out = lax.map(jax.checkpoint(query_block), (queries.reshape(block_count, block_len, HEADS, HEAD_DIM), key_rows.reshape(block_count, block_len, HEADS, HEAD_DIM), value_rows.reshape(block_count, block_len, HEADS, HEAD_DIM), segment_row.reshape(block_count, block_len), positions.reshape(block_count, block_len)))
    return blocks_out.reshape(length, HEADS * HEAD_DIM)

def layer_forward(token_row, segment_row, gain_attn, w_query, w_key, w_value, conv_key, conv_value, w_out, gain_ffn, w_up, w_down):
    normed = low(normalize(token_row) * gain_attn)
    queries = low(low_back(matmul(normed, w_query)))
    key_rows = low(low_back(matmul(normed, w_key)))
    value_rows = low(low_back(matmul(normed, w_value)))
    slot_segment = segment_row[2::3]
    in_window = (segment_row.reshape(-1, 3) == slot_segment[:, None]).astype(jnp.float32)[..., None]
    key_window = (key_rows.reshape(-1, 3, D) * in_window).reshape(-1, 3 * D)
    value_window = (value_rows.reshape(-1, 3, D) * in_window).reshape(-1, 3 * D)
    packed_key = low(low_back(matmul(key_window, conv_key)))
    packed_value = low(low_back(matmul(value_window, conv_value)))
    attended = low(low_back(attend(queries, key_rows, value_rows, packed_key, packed_value, segment_row, slot_segment)))
    hidden = token_row + low_back(matmul(attended, w_out))
    normed_ffn = low(normalize(hidden) * gain_ffn)
    expanded = low_back(matmul(normed_ffn, w_up))
    activated = low(jax.nn.gelu(expanded))
    return hidden + low_back(matmul(activated, w_down))

def reference(tokens, segments, cotangent, gain_attn, w_query, w_key, w_value, conv_key, conv_value, w_out, gain_ffn, w_up, w_down):
    params = tuple((parameter.astype(jnp.float32) for parameter in (gain_attn, w_query, w_key, w_value, conv_key, conv_value, w_out, gain_ffn, w_up, w_down)))
    row_total = MB * ROWS
    all_tokens = tokens.reshape(row_total, LEN, D).astype(jnp.float32)
    all_segments = segments.reshape(row_total, LEN)
    all_cotangents = cotangent.reshape(row_total, LEN, D).astype(jnp.float32)

    def one_row(totals, inputs):
        token_row, segment_row, cotangent_row = inputs

        def forward(tokens_in, *weights):
            return layer_forward(tokens_in, segment_row, *weights)
        out_row, pullback = jax.vjp(forward, token_row, *params)
        gradients = pullback(cotangent_row)
        summed = tuple((total_part + grad_part for total_part, grad_part in zip(totals, gradients[1:])))
        return (summed, (out_row.astype(jnp.bfloat16), gradients[0].astype(jnp.bfloat16)))
    zero_grads = tuple((jnp.zeros_like(parameter) for parameter in params))
    totals, (layer_outputs, token_grads) = lax.scan(one_row, zero_grads, (all_tokens, all_segments, all_cotangents))
    return (layer_outputs.reshape(MB, ROWS, LEN, D), token_grads.reshape(MB, ROWS, LEN, D), totals[0], totals[1], totals[2], totals[3], totals[4], totals[5], totals[6], totals[7], totals[8], totals[9])
```

```python
import functools

import jax
import jax.numpy as jnp
from jax import lax
from jax.experimental import pallas as pl
from jax.experimental.pallas import tpu as pltpu
from jax.sharding import PartitionSpec as P

HEADS = 8
HEAD_DIM = 64
LANES = 128
GROUPS = HEADS * HEAD_DIM // LANES
EPSILON = 1e-05
MASKED_OUT = -1e30
SCALE = HEAD_DIM ** (-0.5)
GELU_SCALE = 0.7978845608028654
GELU_CUBIC = 0.044715
SCATTER_BITS = 5
EXTRA_ROWS = 16
VMEM_LIMIT = 60 * 1024 * 1024

BF16 = jnp.bfloat16
F32 = jnp.float32


def dot(left, right):
    return jnp.dot(left, right, preferred_element_type=F32)


def dot_nt(left, right):
    return lax.dot_general(left, right, (((1,), (1,)), ((), ())), preferred_element_type=F32)


def dot_tn(left, right):
    return lax.dot_general(left, right, (((0,), (0,)), ((), ())), preferred_element_type=F32)


def normalize(values):
    average = jnp.mean(values, axis=-1, keepdims=True)
    centred = values - average
    variance = jnp.mean(centred * centred, axis=-1, keepdims=True)
    inverse_dev = lax.rsqrt(variance + EPSILON)
    return centred * inverse_dev, inverse_dev


def normalize_back(grad_normed, unit, inverse_dev, gain):
    grad_unit = grad_normed * gain
    first_mean = jnp.mean(grad_unit, axis=-1, keepdims=True)
    second_mean = jnp.mean(grad_unit * unit, axis=-1, keepdims=True)
    return inverse_dev * (grad_unit - first_mean - unit * second_mean)


class Plan:
    def __init__(self, mesh):
        self.n_rows = mesh.shape["rows"]
        self.n_seq = mesh.shape["seq"]
        rows = [("rows", 1 << i) for i in range(self.n_rows.bit_length() - 1)]
        seq = [("seq", 1 << i) for i in range(self.n_seq.bit_length() - 1)]
        kept = max(0, min(len(seq), SCATTER_BITS - len(rows)))
        self.seq_block = 1 << kept
        self.blocks = self.n_rows * self.seq_block
        core, others = rows[:1], rows[1:]
        low, high = seq[:1], seq[1:kept] if kept else []
        low = low[:kept]
        self.core = core[0]
        self.first = others + low
        self.second = low + others
        self.tail = high
        self.rest = seq[kept:]
        bits = [1 << i for i in range(len(seq))]
        self.key_order = bits[::-1]
        self.value_order = bits[:1] + bits[:0:-1]

    def mask(self, bit):
        axis, value = bit
        return value * self.seq_block if axis == "rows" else value

    def relative(self, order, position):
        result = 0
        for number, bit in enumerate(order):
            if position >> (len(order) - 1 - number) & 1:
                result |= self.mask(bit)
        return result

    def seq_relative(self, order, position):
        result = 0
        for number, bit in enumerate(order):
            if position >> number & 1:
                result |= bit
        return result

    def swap(self, array, bit):
        axis, value = bit
        size = self.n_rows if axis == "rows" else self.n_seq
        return lax.ppermute(array, axis, [(i, i ^ value) for i in range(size)])


def order_matrix(length, transposed):
    slots = length // 3
    rows = lax.broadcasted_iota(jnp.int32, (length, length), 1 if transposed else 0)
    columns = lax.broadcasted_iota(jnp.int32, (length, length), 0 if transposed else 1)
    tap = (rows >= slots).astype(jnp.int32) + (rows >= 2 * slots).astype(jnp.int32)
    return (columns == 3 * (rows - tap * slots) + tap).astype(BF16)


def window_masks(segment_column, slots):
    last = segment_column[2 * slots :]
    return [(segment_column[i * slots : (i + 1) * slots] == last).astype(F32) for i in range(3)]


def call(kernel, name, outs, scratch=(), flops=0, bytes_accessed=0, smem=0, anywhere=()):
    def space(number):
        if number < smem:
            return pltpu.SMEM
        return pl.ANY if number in anywhere else pltpu.VMEM

    def specs(count):
        return [pl.BlockSpec(memory_space=space(number)) for number in range(count)]

    def run(*operands):
        return pl.pallas_call(
            kernel,
            name=name,
            out_shape=[jax.ShapeDtypeStruct(shape, dtype) for shape, dtype in outs],
            in_specs=specs(len(operands)),
            out_specs=[pl.BlockSpec(memory_space=pltpu.VMEM)] * len(outs),
            scratch_shapes=list(scratch),
            compiler_params=pltpu.CompilerParams(vmem_limit_bytes=VMEM_LIMIT),
            cost_estimate=pl.CostEstimate(
                flops=flops, bytes_accessed=bytes_accessed, transcendentals=0
            ),
        )(*operands)

    return run


def project_kernel(
    tokens, gain, w_query, w_key, w_value, conv_key, conv_value, segment_column, extra,
    x_out, normed_out, query_out, key_out, value_out, packed_key, packed_value,
):
    batch, length, width = tokens.shape
    slots = length // 3
    order = order_matrix(length, False)
    rows = [dot(order, tokens[b]) for b in range(batch)]
    x = jnp.concatenate(rows, axis=0)
    x_out[...] = x
    unit, _ = normalize(x)
    normed = (unit * gain[...].astype(F32)).astype(BF16)
    normed_out[...] = normed
    query_out[...] = dot(normed, w_query[...]).astype(BF16)
    for matrix, conv, flat_out, packed_out in (
        (w_key, conv_key, key_out, packed_key),
        (w_value, conv_value, value_out, packed_value),
    ):
        flat = dot(normed, matrix[...]).astype(BF16)
        flat_out[...] = flat
        taps = [[], [], []]
        for b in range(batch):
            masks = window_masks(segment_column[b], slots)
            for i in range(3):
                start = b * length + i * slots
                part = flat[start : start + slots].astype(F32) * masks[i]
                taps[i].append(part.astype(BF16))
        total = None
        for i in range(3):
            term = dot(jnp.concatenate(taps[i], axis=0), conv[i * width : (i + 1) * width, :])
            total = term if total is None else total + term
        packed_out[0 : batch * slots, :] = total.astype(BF16)
    packed_key[batch * slots :, :] = extra[...]


def layer_kernel(
    plan, keep_prob,
    place, x_in, cotangent, query_in, key_in, value_in, keys_near, keys_far, values_near, values_far,
    segment_column, w_out, gain_ffn, w_up, w_down,
    layer_out, d_hidden_out, normed_ffn_out, activated_out, d_expanded_out, cotangent_out,
    attended_out, d_branch_out, d_query_out, d_key_own, d_value_own, d_packed_key, d_packed_value,
    gain_grad,
    all_keys, all_values, all_extra, bias, statistics, prob_keep, expanded_sum, d_normed_sum,
    d_attended, copied,
):
    batch, length, width = cotangent.shape
    slots = length // 3
    n_seq = plan.n_seq
    half = n_seq // 2
    total_slots = slots * n_seq
    own_place = place[0]
    key_position = {plan.seq_relative(plan.key_order, p): p for p in range(n_seq)}
    copies = []

    def fetch(source, target):
        copies.append(pltpu.make_async_copy(source, target, copied.at[len(copies)]))
        copies[-1].start()

    for p in range(n_seq):
        keys = keys_near.at[p] if p < half else keys_far.at[p - half]
        values = values_near.at[p] if p < half else values_far.at[p - half]
        q = key_position[plan.seq_relative(plan.value_order, p)]
        fetch(keys.at[pl.ds(batch * slots, EXTRA_ROWS), :], all_extra.at[p])
        for b in range(batch):
            rows = pl.ds(b * slots, slots)
            fetch(keys.at[rows, :], all_keys.at[b, pl.ds(p * slots, slots), :])
            fetch(values.at[rows, :], all_values.at[b, pl.ds(q * slots, slots), :])
    for copy in copies:
        copy.wait()

    segment_rows = jnp.zeros((EXTRA_ROWS, total_slots), F32)
    slot_lane = lax.broadcasted_iota(jnp.int32, (1, total_slots), 1)
    slot_end = jnp.zeros((1, total_slots), jnp.int32)
    select_row = lax.broadcasted_iota(jnp.int32, (LANES, total_slots), 0)
    select_lane = lax.broadcasted_iota(jnp.int32, (LANES, total_slots), 1)
    for p in range(n_seq):
        selected = (select_lane == select_row + p * slots) & (select_row < slots)
        segment_rows += dot(all_extra[p, :, 0:LANES], selected.astype(BF16))
        owner = plan.seq_relative(plan.key_order, p) ^ own_place
        here = (slot_lane >= p * slots) & (slot_lane < (p + 1) * slots)
        slot_end = jnp.where(here, length * owner - length * p + 3 * slot_lane + 2, slot_end)
    row = lax.broadcasted_iota(jnp.int32, (length, 1), 0)
    tap = (row >= slots).astype(jnp.int32) + (row >= 2 * slots).astype(jnp.int32)
    query_place = length * own_place + 3 * (row - tap * slots) + tap
    causal = slot_end <= query_place
    for b in range(batch):
        matching = segment_rows[b : b + 1, :] == segment_column[b]
        bias[b] = jnp.where(causal & matching, 0.0, MASKED_OUT)

    low_lane = lax.broadcasted_iota(jnp.int32, (length, LANES), 1) < HEAD_DIM

    def stacked(part):
        zero = jnp.zeros_like(part)
        return jnp.concatenate(
            [jnp.where(low_lane, part, zero), jnp.where(low_lane, zero, part)], axis=0
        )

    def twice(part):
        return jnp.concatenate([part, part], axis=0)

    def merged(part):
        return jnp.where(low_lane, part[:length], part[length:])

    def rows_of(b):
        return pl.ds(pl.multiple_of(b * length, 16), length)

    def lanes_of(g):
        return pl.ds(pl.multiple_of(g * LANES, LANES), LANES)

    def scaled_queries(b, g):
        part = query_in[rows_of(b), lanes_of(g)].astype(F32) * SCALE
        return stacked(part).astype(BF16)

    def attend(number, carry):
        b, g = number // GROUPS, number % GROUPS
        rows, lanes = rows_of(b), lanes_of(g)
        queries = scaled_queries(b, g)
        own_key = twice(key_in[rows, lanes].astype(F32))
        scores = dot_nt(queries, all_keys[b, :, lanes]) + twice(bias[b])
        own_score = jnp.sum(queries.astype(F32) * own_key, axis=-1, keepdims=True)
        top = jnp.maximum(own_score, jnp.max(scores, axis=-1, keepdims=True))
        raised = jnp.exp(scores - top)
        own_raised = jnp.exp(own_score - top)
        inverse = 1.0 / (own_raised + jnp.sum(raised, axis=-1, keepdims=True))
        prob = raised * inverse
        own_prob = own_raised * inverse
        if keep_prob:
            prob_keep[number] = prob
        statistics[number, :, 0:1] = own_prob
        statistics[number, :, 1:2] = top - jnp.log(inverse)
        result = dot(prob.astype(BF16), all_values[b, :, lanes])
        own_value = twice(value_in[rows, lanes].astype(F32))
        result += own_prob.astype(BF16).astype(F32) * own_value
        attended_out[rows, lanes] = merged(result).astype(BF16)
        return carry

    lax.fori_loop(0, batch * GROUPS, attend, 0)

    x = x_in[...]
    hidden = x + dot(attended_out[...], w_out[...])
    unit, inverse_dev = normalize(hidden)
    gain = gain_ffn[...].astype(F32)
    normed_ffn_out[...] = (unit * gain).astype(BF16)
    order = order_matrix(length, False)
    for b in range(batch):
        cotangent_out[b * length : (b + 1) * length, :] = dot(order, cotangent[b]).astype(BF16)
    expanded_sum[...] = hidden
    d_normed_sum[...] = jnp.zeros_like(d_normed_sum)
    chunk = width
    total_width = w_up.shape[1]

    def feed(number, carry):
        columns = pl.ds(pl.multiple_of(number * chunk, chunk), chunk)
        expanded = dot(normed_ffn_out[...], w_up[:, columns])
        square = expanded * expanded
        curve = jnp.tanh(GELU_SCALE * expanded * (1.0 + GELU_CUBIC * square))
        activated = (0.5 * expanded * (1.0 + curve)).astype(BF16)
        activated_out[:, columns] = activated
        slope = 0.5 * (1.0 + curve) + 0.5 * expanded * (1.0 - curve * curve) * (
            GELU_SCALE * (1.0 + 3.0 * GELU_CUBIC * square)
        )
        expanded_sum[...] += dot(activated, w_down[columns, :])
        d_activated = dot_nt(cotangent_out[...], w_down[columns, :])
        d_expanded = (d_activated * slope).astype(BF16)
        d_expanded_out[:, columns] = d_expanded
        d_normed_sum[...] += dot_nt(d_expanded, w_up[:, columns])
        return carry

    lax.fori_loop(0, total_width // chunk, feed, 0)

    unorder = order_matrix(length, True)
    for b in range(batch):
        part = expanded_sum[b * length : (b + 1) * length, :].astype(BF16)
        layer_out[b] = dot(unorder, part).astype(BF16)
    d_normed = d_normed_sum[...]
    gain_grad[...] = jnp.sum(d_normed * unit, axis=0, keepdims=True)
    d_hidden = cotangent_out[...].astype(F32) + normalize_back(d_normed, unit, inverse_dev, gain)
    d_hidden_out[...] = d_hidden
    d_branch = d_hidden.astype(BF16)
    d_branch_out[...] = d_branch
    d_attended[...] = dot_nt(d_branch, w_out[...]).astype(BF16)

    value_spot = [key_position[plan.seq_relative(plan.value_order, p)] for p in range(n_seq)]

    def attend_back(number, carry):
        b, g = number // GROUPS, number % GROUPS
        rows, lanes = rows_of(b), lanes_of(g)
        queries = scaled_queries(b, g)
        own_prob = statistics[number, :, 0:1]
        if keep_prob:
            prob = prob_keep[number]
        else:
            scores = dot_nt(queries, all_keys[b, :, lanes]) + twice(bias[b])
            prob = jnp.exp(scores - statistics[number, :, 1:2])
        grads = stacked(d_attended[rows, lanes])
        own_value = twice(value_in[rows, lanes].astype(F32))
        own_key = twice(key_in[rows, lanes].astype(F32))
        prob_grad = dot_nt(grads, all_values[b, :, lanes])
        own_prob_grad = jnp.sum(grads.astype(F32) * own_value, axis=-1, keepdims=True)
        delta = own_prob * own_prob_grad + jnp.sum(prob * prob_grad, axis=-1, keepdims=True)
        d_score = (prob * (prob_grad - delta)).astype(BF16)
        d_own = (own_prob * (own_prob_grad - delta)).astype(BF16).astype(F32)
        own_low = own_prob.astype(BF16).astype(F32)
        d_query = merged(dot(d_score, all_keys[b, :, lanes]) + d_own * own_key) * SCALE
        d_query_out[rows, lanes] = d_query.astype(BF16)
        d_key_own[rows, lanes] = merged(d_own * queries.astype(F32))
        d_value_own[rows, lanes] = merged(own_low * grads.astype(F32))
        key_sums = dot_tn(d_score, queries).astype(BF16)
        value_sums = dot_tn(prob.astype(BF16), grads).astype(BF16)
        for p in range(n_seq):
            d_packed_key[p, pl.ds(pl.multiple_of(b * slots, 16), slots), lanes] = key_sums[
                p * slots : (p + 1) * slots
            ]
            q = value_spot[p]
            d_packed_value[p, pl.ds(pl.multiple_of(b * slots, 16), slots), lanes] = value_sums[
                q * slots : (q + 1) * slots
            ]
        return carry

    lax.fori_loop(0, batch * GROUPS, attend_back, 0)


def spread(plan, place, order, parts, send, keep, offset):
    rows_block = sum(rows for _, rows in parts)
    half = plan.blocks // 2
    for target, core in ((send, 1), (keep, 0)):
        for p in range(half):
            block = plan.relative(order, core * half + p) ^ place
            start = offset + p * rows_block
            for source, rows in parts:
                target[start : start + rows, :] = source[
                    pl.ds(pl.multiple_of(block * rows, 16), rows), :
                ]
                start += rows


def ffn_grad_kernel(
    plan, order_a, order_b,
    place, activated, cotangent, normed_ffn, d_expanded, attended, d_branch,
    send, keep,
    down_rows, up_rows, out_rows,
):
    width = cotangent.shape[1]
    chunk = 512
    for c in range(activated.shape[1] // chunk):
        columns = slice(c * chunk, (c + 1) * chunk)
        down_rows[columns, :] = dot_tn(activated[:, columns], cotangent[...]).astype(BF16)
        up_rows[c] = dot_tn(normed_ffn[...], d_expanded[:, columns]).astype(BF16)
    out_rows[...] = dot_tn(attended[...], d_branch[...]).astype(BF16)
    mine = place[1]
    down_block = activated.shape[1] // plan.blocks
    thin = width // plan.blocks
    rows_a = down_block + thin
    spread(plan, mine, order_a, ((down_rows, down_block), (out_rows, thin)), send, keep, 0)
    ups = tuple((up_rows.at[c], thin) for c in range(activated.shape[1] // chunk))
    spread(plan, mine, order_b, ups, send, keep, rows_a * plan.blocks // 2)


def tail_kernel(
    plan, order_a, order_b,
    place, d_packed_key, d_packed_value, x_in, normed, d_query, key_in, value_in,
    d_key_own, d_value_own, d_hidden, segment_column, gain, w_query, w_key, w_value,
    conv_key, conv_value, gain_ffn_grad,
    send, keep, grad_tokens,
    key_conv_rows, value_conv_rows, key_rows, value_rows, query_rows, gain_rows,
):
    batch, length, width = grad_tokens.shape
    slots = length // 3
    masks = [window_masks(segment_column[b], slots) for b in range(batch)]
    grads = []
    for d_packed, flat, conv, own, conv_rows, rows_out in (
        (d_packed_key, key_in, conv_key, d_key_own, key_conv_rows, key_rows),
        (d_packed_value, value_in, conv_value, d_value_own, value_conv_rows, value_rows),
    ):
        back = d_packed[...]
        pieces = [[None] * 3 for _ in range(batch)]
        for i in range(3):
            taps = []
            from_tap = dot_nt(back, conv[i * width : (i + 1) * width, :])
            for b in range(batch):
                start = b * length + i * slots
                part = flat[start : start + slots, :].astype(F32) * masks[b][i]
                taps.append(part.astype(BF16))
                pieces[b][i] = from_tap[b * slots : (b + 1) * slots] * masks[b][i]
            window = jnp.concatenate(taps, axis=0)
            conv_rows[i * width : (i + 1) * width, :] = dot_tn(window, back).astype(BF16)
        whole = jnp.concatenate([piece for row in pieces for piece in row], axis=0)
        d_flat = (whole + own[...]).astype(BF16)
        grads.append(d_flat)
        rows_out[...] = dot_tn(normed[...], d_flat).astype(BF16)
    query_rows[...] = dot_tn(normed[...], d_query[...]).astype(BF16)
    d_normed = (
        dot_nt(d_query[...], w_query[...])
        + dot_nt(grads[0], w_key[...])
        + dot_nt(grads[1], w_value[...])
    )
    unit, inverse_dev = normalize(x_in[...])
    gain_grad = jnp.sum(d_normed * unit, axis=0, keepdims=True)
    d_input = normalize_back(d_normed, unit, inverse_dev, gain[...].astype(F32))
    result = (d_hidden[...] + d_input).astype(BF16)
    unorder = order_matrix(length, True)
    for b in range(batch):
        part = result[b * length : (b + 1) * length, :]
        grad_tokens[b] = dot(unorder, part).astype(BF16)
    row = lax.broadcasted_iota(jnp.int32, (EXTRA_ROWS, width), 0)
    gains = jnp.where(row == 0, gain_grad, jnp.where(row == 1, gain_ffn_grad[...], 0.0))
    for p in range(plan.blocks):
        gain_rows[p * EXTRA_ROWS : (p + 1) * EXTRA_ROWS, :] = gains.astype(BF16)
    mine = place[1]
    conv_block = 3 * width // plan.blocks
    thin = width // plan.blocks
    rows_a = conv_block + 2 * thin
    spread(
        plan, mine, order_a,
        ((key_conv_rows, conv_block), (key_rows, thin), (query_rows, thin)), send, keep, 0,
    )
    spread(
        plan, mine, order_b,
        ((value_conv_rows, conv_block), (value_rows, thin), (gain_rows, EXTRA_ROWS)),
        send, keep, rows_a * plan.blocks // 2,
    )


def unspread(plan, place, order, parts, near, far, offset):
    rows_block = sum(rows for _, rows, _ in parts)
    half = plan.blocks // 2
    for source, core in ((near, 0), (far, 1)):
        for p in range(half):
            block = plan.relative(order, core * half + p) ^ place
            start = offset + p * rows_block
            for target, rows, columns in parts:
                part = source[start : start + rows, :].astype(F32)
                spot = pl.ds(pl.multiple_of(block * rows, 16), rows)
                target[spot, columns] = part
                start += rows


def ffn_finish_kernel(plan, order_a, order_b, place, near, far, grad_down, grad_up, grad_out):
    width = grad_out.shape[1]
    down_block = grad_down.shape[0] // plan.blocks
    thin = width // plan.blocks
    everything = slice(None)
    unspread(
        plan, place[1], order_a,
        ((grad_down, down_block, everything), (grad_out, thin, everything)), near, far, 0,
    )
    ups = tuple(
        (grad_up, thin, slice(c * width, (c + 1) * width)) for c in range(grad_up.shape[1] // width)
    )
    unspread(plan, place[1], order_b, ups, near, far, (down_block + thin) * plan.blocks // 2)


def tail_finish_kernel(
    plan, order_a, order_b, place, near, far,
    grad_conv_key, grad_key, grad_query, grad_conv_value, grad_value, grad_gains,
):
    width = grad_key.shape[1]
    conv_block = grad_conv_key.shape[0] // plan.blocks
    thin = width // plan.blocks
    everything = slice(None)
    unspread(
        plan, place[1], order_a,
        (
            (grad_conv_key, conv_block, everything),
            (grad_key, thin, everything),
            (grad_query, thin, everything),
        ),
        near, far, 0,
    )
    offset = (conv_block + 2 * thin) * plan.blocks // 2
    rows_block = conv_block + thin + EXTRA_ROWS
    half = plan.blocks // 2
    for source, core in ((near, 0), (far, 1)):
        for p in range(half):
            block = plan.relative(order_b, core * half + p) ^ place[1]
            start = offset + p * rows_block
            grad_conv_value[pl.ds(pl.multiple_of(block * conv_block, 16), conv_block), :] = source[
                start : start + conv_block, :
            ].astype(F32)
            start += conv_block
            grad_value[pl.ds(pl.multiple_of(block * thin, 16), thin), :] = source[
                start : start + thin, :
            ].astype(F32)
    start = offset + conv_block + thin
    grad_gains[...] = near[start : start + EXTRA_ROWS, :].astype(F32)


def add(left, right):
    return (left.astype(F32) + right.astype(F32)).astype(BF16)


def gather_row(plan, array, order):
    held = array[None]
    for number, bit in enumerate(order):
        arrived = plan.swap(held, ("seq", bit))
        if number == len(order) - 1:
            return held, arrived
        held = jnp.concatenate([held, arrived], axis=0)


def scatter_row(plan, array, order):
    held = array
    for bit in reversed(order):
        half = held.shape[0] // 2
        held = add(held[:half], plan.swap(held[half:], ("seq", bit)))
    return held[0]


def halve(plan, array, bit):
    half = array.shape[0] // 2
    return add(array[:half], plan.swap(array[half:], bit))


def reduce_blocks(plan, send, keep, split, first_a, first_b):
    total = add(keep, plan.swap(send, plan.core))
    part_a, part_b = total[:split], total[split:]
    for bit_a, bit_b in zip(first_a, first_b):
        part_a = halve(plan, part_a, bit_a)
        part_b = halve(plan, part_b, bit_b)
    for bit in plan.tail:
        half_a, half_b = part_a.shape[0] // 2, part_b.shape[0] // 2
        arrived = plan.swap(jnp.concatenate([part_a[half_a:], part_b[half_b:]], axis=0), bit)
        part_a = add(part_a[:half_a], arrived[:half_a])
        part_b = add(part_b[:half_b], arrived[half_a:])
    for bit in plan.rest:
        arrived = plan.swap(jnp.concatenate([part_a, part_b], axis=0), bit)
        part_a = add(part_a, arrived[: part_a.shape[0]])
        part_b = add(part_b, arrived[part_a.shape[0] :])
    return part_a, part_b


def gather_blocks(plan, part_a, part_b, first_a, first_b):
    for bit in reversed(plan.tail):
        arrived = plan.swap(jnp.concatenate([part_a, part_b], axis=0), bit)
        rows = part_a.shape[0]
        part_a = jnp.concatenate([part_a, arrived[:rows]], axis=0)
        part_b = jnp.concatenate([part_b, arrived[rows:]], axis=0)
    for bit_a, bit_b in zip(reversed(first_a), reversed(first_b)):
        far_a, far_b = plan.swap(part_a, bit_a), plan.swap(part_b, bit_b)
        part_a = jnp.concatenate([part_a, far_a], axis=0)
        part_b = jnp.concatenate([part_b, far_b], axis=0)
    near = jnp.concatenate([part_a, part_b], axis=0)
    return near, plan.swap(near, plan.core)


def body(
    plan, tokens, segments, cotangent, gain_attn, w_query, w_key, w_value, conv_key, conv_value,
    w_out, gain_ffn, w_up, w_down,
):
    batch, _, length, width = tokens.shape
    slots = length // 3
    positions = batch * length
    tokens, segments, cotangent = tokens[:, 0], segments[:, 0], cotangent[:, 0]
    gain_attn, gain_ffn = gain_attn[None], gain_ffn[None]
    seq_place = lax.axis_index("seq").astype(jnp.int32)
    block_place = lax.axis_index("rows").astype(jnp.int32) * plan.seq_block + lax.rem(
        seq_place, jnp.int32(plan.seq_block)
    )
    place = jnp.stack([seq_place, block_place])
    grouped = segments.reshape(batch, slots, 3)
    segment_column = grouped.transpose(0, 2, 1).reshape(batch, length, 1).astype(F32)
    extra = jnp.pad(
        grouped[:, :, 2].astype(BF16), ((0, EXTRA_ROWS - batch), (0, width - slots))
    )
    flat = ((positions, width), BF16)
    flat32 = ((positions, width), F32)
    x, normed, queries, key_rows, value_rows, packed_key, packed_value = call(
        project_kernel,
        "project",
        [flat32] + [flat] * 4
        + [((batch * slots + EXTRA_ROWS, width), BF16), ((batch * slots, width), BF16)],
        flops=2 * positions * width * width * 5,
        bytes_accessed=2 * width * width * 9,
    )(
        tokens, gain_attn, w_query, w_key, w_value, conv_key, conv_value, segment_column, extra
    )
    keys_near, keys_far = gather_row(plan, packed_key, plan.key_order)
    values_near, values_far = gather_row(plan, packed_value, plan.value_order)

    total_slots = slots * plan.n_seq
    keep_prob = total_slots <= 768
    wide = ((positions, w_up.shape[1]), BF16)
    steps = batch * GROUPS
    packed_shape = ((plan.n_seq, batch * slots, width), BF16)
    (
        layer_out, d_hidden, normed_ffn, activated, d_expanded, cotangent_rows, attended, d_branch,
        d_query, d_key_own, d_value_own, d_packed_key, d_packed_value, gain_ffn_grad,
    ) = call(
        functools.partial(layer_kernel, plan, keep_prob),
        "layer",
        [
            ((batch, length, width), BF16), flat32, flat, wide, wide, flat, flat, flat,
            flat, flat32, flat32, packed_shape, packed_shape, ((1, width), F32),
        ],
        scratch=[
            pltpu.VMEM((batch, total_slots, width), BF16),
            pltpu.VMEM((batch, total_slots, width), BF16),
            pltpu.VMEM((plan.n_seq, EXTRA_ROWS, width), BF16),
            pltpu.VMEM((batch, length, total_slots), F32),
            pltpu.VMEM((steps, 2 * length, LANES), F32),
            pltpu.VMEM((steps if keep_prob else 1, 2 * length, total_slots), F32),
            pltpu.VMEM((positions, width), F32),
            pltpu.VMEM((positions, width), F32),
            pltpu.VMEM((positions, width), BF16),
            pltpu.SemaphoreType.DMA((plan.n_seq * (1 + 2 * batch),)),
        ],
        flops=2 * positions * width * width * 24,
        bytes_accessed=2 * width * width * 20,
        smem=1,
        anywhere=(6, 7, 8, 9),
    )(
        place, x, cotangent, queries, key_rows, value_rows, keys_near, keys_far, values_near,
        values_far, segment_column, w_out, gain_ffn, w_up, w_down,
    )

    core = [plan.core]
    order_a, order_b = core + plan.first + plan.tail, core + plan.second + plan.tail
    half = plan.blocks // 2
    thin = width // plan.blocks
    down_block = w_down.shape[0] // plan.blocks
    chunks = w_up.shape[1] // width
    rows_a, rows_b = down_block + thin, chunks * thin
    buffer = ((half * (rows_a + rows_b), width), BF16)
    ffn_send, ffn_keep = call(
        functools.partial(ffn_grad_kernel, plan, order_a, order_b),
        "ffn_grads",
        [buffer, buffer],
        scratch=[
            pltpu.VMEM((w_down.shape[0], width), BF16),
            pltpu.VMEM((chunks, width, width), BF16),
            pltpu.VMEM((width, width), BF16),
        ],
        flops=2 * positions * width * width * 9,
        bytes_accessed=2 * width * width * 18,
        smem=1,
    )(place, activated, cotangent_rows, normed_ffn, d_expanded, attended, d_branch)
    own_key_grad = scatter_row(plan, d_packed_key, plan.key_order)
    own_value_grad = scatter_row(plan, d_packed_value, plan.value_order)
    ffn_a, ffn_b = reduce_blocks(
        plan, ffn_send, ffn_keep, half * rows_a, plan.first, plan.second
    )

    conv_block = conv_key.shape[0] // plan.blocks
    tail_a, tail_b = conv_block + 2 * thin, conv_block + thin + EXTRA_ROWS
    tail_buffer = ((half * (tail_a + tail_b), width), BF16)
    square = pltpu.VMEM((width, width), BF16)
    tail_send, tail_keep, grad_tokens = call(
        functools.partial(tail_kernel, plan, order_b, order_a),
        "tail",
        [tail_buffer, tail_buffer, ((batch, length, width), BF16)],
        scratch=[
            pltpu.VMEM(conv_key.shape, BF16), pltpu.VMEM(conv_value.shape, BF16),
            square, square, square, pltpu.VMEM((plan.blocks * EXTRA_ROWS, width), BF16),
        ],
        flops=2 * positions * width * width * 10,
        bytes_accessed=2 * width * width * 18,
        smem=1,
    )(
        place, own_key_grad, own_value_grad, x, normed, d_query, key_rows, value_rows,
        d_key_own, d_value_own, d_hidden, segment_column, gain_attn, w_query, w_key, w_value,
        conv_key, conv_value, gain_ffn_grad,
    )
    ffn_near, ffn_far = gather_blocks(plan, ffn_a, ffn_b, plan.first, plan.second)
    tail_first, tail_second = reduce_blocks(
        plan, tail_send, tail_keep, half * tail_a, plan.second, plan.first
    )
    tail_near, tail_far = gather_blocks(
        plan, tail_first, tail_second, plan.second, plan.first
    )
    matrix = ((width, width), F32)
    grad_down, grad_up, grad_out = call(
        functools.partial(ffn_finish_kernel, plan, order_a, order_b),
        "ffn_finish",
        [(w_down.shape, F32), (w_up.shape, F32), matrix],
        bytes_accessed=6 * width * width * 9,
        smem=1,
    )(place, ffn_near, ffn_far)
    grad_conv_key, grad_key, grad_query, grad_conv_value, grad_value, grad_gains = call(
        functools.partial(tail_finish_kernel, plan, order_b, order_a),
        "tail_finish",
        [(conv_key.shape, F32), matrix, matrix, (conv_value.shape, F32), matrix]
        + [((EXTRA_ROWS, width), F32)],
        bytes_accessed=6 * width * width * 9,
        smem=1,
    )(place, tail_near, tail_far)
    return (
        layer_out[:, None], grad_tokens[:, None], grad_gains[0], grad_query, grad_key, grad_value,
        grad_conv_key, grad_conv_value, grad_out, grad_gains[1], grad_up, grad_down,
    )


def solution(mesh):
    packed = P(None, "rows", "seq", None)
    in_specs = (packed, P(None, "rows", "seq"), packed) + (P(),) * 10
    out_specs = (packed, packed) + (P(),) * 10
    return jax.shard_map(
        functools.partial(body, Plan(mesh)),
        mesh=mesh, in_specs=in_specs, out_specs=out_specs, check_vma=False,
    )
```

```python
import functools

import jax
import jax.numpy as jnp
from jax import lax
from jax.experimental import pallas as pl
from jax.experimental.pallas import tpu as pltpu
from jax.sharding import PartitionSpec as P

HEADS = 8
HEAD_DIM = 64
LANES = 128
GROUPS = HEADS * HEAD_DIM // LANES
EPSILON = 1e-05
MASKED_OUT = -1e30
SCALE = HEAD_DIM ** (-0.5)
GELU_SCALE = 0.7978845608028654
GELU_CUBIC = 0.044715
SCATTER_BITS = 5
EXTRA_ROWS = 16
VMEM_SMALL = 28 * 1024 * 1024
VMEM_LARGE = 60 * 1024 * 1024
SHORT_ROW = 768

BF16 = jnp.bfloat16
F32 = jnp.float32


def dot(left, right):
    return jnp.dot(left, right, preferred_element_type=F32)


def dot_nt(left, right):
    return lax.dot_general(left, right, (((1,), (1,)), ((), ())), preferred_element_type=F32)


def dot_tn(left, right):
    return lax.dot_general(left, right, (((0,), (0,)), ((), ())), preferred_element_type=F32)


def normalize(values):
    average = jnp.mean(values, axis=-1, keepdims=True)
    centred = values - average
    variance = jnp.mean(centred * centred, axis=-1, keepdims=True)
    inverse_dev = lax.rsqrt(variance + EPSILON)
    return centred * inverse_dev, inverse_dev


def normalize_back(grad_normed, unit, inverse_dev, gain):
    grad_unit = grad_normed * gain
    first_mean = jnp.mean(grad_unit, axis=-1, keepdims=True)
    second_mean = jnp.mean(grad_unit * unit, axis=-1, keepdims=True)
    return inverse_dev * (grad_unit - first_mean - unit * second_mean)


class Plan:
    def __init__(self, mesh):
        self.n_rows = mesh.shape["rows"]
        self.n_seq = mesh.shape["seq"]
        rows = [("rows", 1 << i) for i in range(self.n_rows.bit_length() - 1)]
        seq = [("seq", 1 << i) for i in range(self.n_seq.bit_length() - 1)]
        kept = max(0, min(len(seq), SCATTER_BITS - len(rows)))
        self.seq_block = 1 << kept
        self.blocks = self.n_rows * self.seq_block
        core, others = rows[:1], rows[1:]
        low, high = seq[:1], seq[1:kept] if kept else []
        low = low[:kept]
        self.core = core[0]
        self.first = others + low
        self.second = low + others
        self.tail = high
        self.rest = seq[kept:]
        bits = [1 << i for i in range(len(seq))]
        self.key_order = bits[::-1]
        self.value_order = bits[:1] + bits[:0:-1]

    def mask(self, bit):
        axis, value = bit
        return value * self.seq_block if axis == "rows" else value

    def relative(self, order, position):
        result = 0
        for number, bit in enumerate(order):
            if position >> (len(order) - 1 - number) & 1:
                result |= self.mask(bit)
        return result

    def seq_relative(self, order, position):
        result = 0
        for number, bit in enumerate(order):
            if position >> number & 1:
                result |= bit
        return result

    def swap(self, array, bit):
        axis, value = bit
        size = self.n_rows if axis == "rows" else self.n_seq
        return lax.ppermute(array, axis, [(i, i ^ value) for i in range(size)])


def order_matrix(length, transposed):
    slots = length // 3
    rows = lax.broadcasted_iota(jnp.int32, (length, length), 1 if transposed else 0)
    columns = lax.broadcasted_iota(jnp.int32, (length, length), 0 if transposed else 1)
    tap = (rows >= slots).astype(jnp.int32) + (rows >= 2 * slots).astype(jnp.int32)
    return (columns == 3 * (rows - tap * slots) + tap).astype(BF16)


def window_masks(segment_column, slots):
    last = segment_column[2 * slots :]
    return [(segment_column[i * slots : (i + 1) * slots] == last).astype(F32) for i in range(3)]


def fetch_all(pairs, arrived):
    copies = [
        pltpu.make_async_copy(source, target, arrived.at[number])
        for number, (source, target) in enumerate(pairs)
    ]
    for copy in copies:
        copy.start()

    def ready(number):
        copies[number].wait()
        return pairs[number][1]

    return ready


def call(
    kernel, name, outs, scratch=(), flops=0, bytes_accessed=0, anywhere=(), out_anywhere=(), aliases=None,
    vmem=VMEM_SMALL,
):
    def spec(number, places):
        return pl.BlockSpec(memory_space=pltpu.HBM if number in places else pltpu.VMEM)

    def run(*operands):
        operands = [
            pltpu.with_memory_space_constraint(operand, pltpu.HBM) if number in anywhere else operand
            for number, operand in enumerate(operands)
        ]
        return pl.pallas_call(
            kernel,
            name=name,
            out_shape=[jax.ShapeDtypeStruct(shape, dtype) for shape, dtype in outs],
            in_specs=[spec(number, anywhere) for number in range(len(operands))],
            out_specs=[spec(number, out_anywhere) for number in range(len(outs))],
            scratch_shapes=list(scratch),
            input_output_aliases=aliases or {},
            compiler_params=pltpu.CompilerParams(vmem_limit_bytes=vmem),
            cost_estimate=pl.CostEstimate(
                flops=flops, bytes_accessed=bytes_accessed, transcendentals=0
            ),
        )(*operands)

    return run


def own_places(plan):
    seq = lax.axis_index("seq")
    return seq, lax.axis_index("rows") * plan.seq_block + lax.rem(seq, plan.seq_block)


def read_segments(order, segments, batch):
    length = order.shape[0]
    rows = [segments[b].astype(F32) for b in range(batch)]
    rows = jnp.concatenate(rows + [jnp.zeros((EXTRA_ROWS - batch, length), F32)], axis=0)
    columns = dot_nt(order, rows.astype(BF16))
    return rows, [columns[:, b : b + 1] for b in range(batch)]


def project_kernel(
    tokens_far, gain_far, segments_far, w_query, w_key, w_value, conv_key, conv_value,
    x_out, normed_out, query_out, key_out, value_out, packed_key, packed_value, segment_out,
    query_here, key_here, value_here, conv_key_here, conv_value_here, tokens, gain, segments,
    arrived,
):
    ready = fetch_all(
        [
            (tokens_far, tokens), (segments_far, segments), (gain_far, gain), (w_key, key_here), (conv_key, conv_key_here), (w_value, value_here),
            (conv_value, conv_value_here), (w_query, query_here),
        ],
        arrived,
    )
    batch, _, length, width = tokens.shape
    slots = length // 3
    order = order_matrix(length, False)
    for number in range(3):
        ready(number)
    rows = [dot(order, tokens[b, 0]) for b in range(batch)]
    segment_rows, segment_columns = read_segments(order, segments, batch)
    for b in range(batch):
        x_out[b] = rows[b]
        segment_out[b] = segment_columns[b]
    last = lax.broadcasted_iota(jnp.int32, (length, width), 0)
    slot = lax.broadcasted_iota(jnp.int32, (length, width), 1)
    extra = dot(segment_rows.astype(BF16), (last == 3 * slot + 2).astype(BF16)).astype(BF16)
    unit, _ = normalize(jnp.concatenate(rows, axis=0))
    normed = (unit * gain[...].astype(F32).reshape(1, width)).astype(BF16)

    def put(target, values):
        for b in range(batch):
            target[b] = values[b * length : (b + 1) * length]

    put(normed_out, normed)
    for number, flat_out, packed_out in ((3, key_out, packed_key), (5, value_out, packed_value)):
        flat = dot(normed, ready(number)[...]).astype(BF16)
        put(flat_out, flat)
        taps = [[], [], []]
        for b in range(batch):
            masks = window_masks(segment_columns[b], slots)
            for i in range(3):
                start = b * length + i * slots
                part = flat[start : start + slots].astype(F32) * masks[i]
                taps[i].append(part.astype(BF16))
        conv = ready(number + 1)
        total = None
        for i in range(3):
            term = dot(jnp.concatenate(taps[i], axis=0), conv[i * width : (i + 1) * width, :])
            total = term if total is None else total + term
        for b in range(batch):
            packed_out[b, 0:slots, :] = total[b * slots : (b + 1) * slots].astype(BF16)
            if number == 3:
                packed_out[b, slots:, :] = extra
    put(query_out, dot(normed, ready(7)[...]).astype(BF16))


def layer_kernel(
    plan, short, number_mb,
    x_in, cotangent, query_in, key_in, value_in, segment_column, gain_ffn,
    keys_near, keys_far, values_near, values_far, w_out, w_up, w_down,
    layer_out, d_hidden_out, normed_ffn_out, activated_out, d_expanded_out, cotangent_out,
    attended_out, d_branch_out, d_query_out, d_key_own, d_value_own, d_packed_key, d_packed_value,
    gain_grad,
    all_keys, all_values, all_extra, bias, statistics, prob_keep, expanded_sum, d_normed_sum,
    d_attended,
):
    _, _, length, width = cotangent.shape
    x_in, query_in, key_in, value_in = (
        ref.at[number_mb] for ref in (x_in, query_in, key_in, value_in)
    )
    slots = length // 3
    n_seq = plan.n_seq
    half = n_seq // 2
    total_slots = slots * n_seq
    own_place = lax.axis_index("seq")
    key_position = {plan.seq_relative(plan.key_order, p): p for p in range(n_seq)}
    for p in range(n_seq):
        keys = keys_near.at[p] if p < half else keys_far.at[p - half]
        values = values_near.at[p] if p < half else values_far.at[p - half]
        q = key_position[plan.seq_relative(plan.value_order, p)]
        all_keys[p * slots : (p + 1) * slots, :] = keys[0:slots, :]
        all_extra[p] = keys[slots:, 0:LANES]
        all_values[q * slots : (q + 1) * slots, :] = values[...]

    segment_rows = jnp.zeros((EXTRA_ROWS, total_slots), F32)
    slot_lane = lax.broadcasted_iota(jnp.int32, (1, total_slots), 1)
    slot_end = jnp.zeros((1, total_slots), jnp.int32)
    select_row = lax.broadcasted_iota(jnp.int32, (LANES, total_slots), 0)
    select_lane = lax.broadcasted_iota(jnp.int32, (LANES, total_slots), 1)
    for p in range(n_seq):
        selected = (select_lane == select_row + p * slots) & (select_row < slots)
        segment_rows += dot(all_extra[p], selected.astype(BF16))
        owner = plan.seq_relative(plan.key_order, p) ^ own_place
        here = (slot_lane >= p * slots) & (slot_lane < (p + 1) * slots)
        slot_end = jnp.where(here, length * owner - length * p + 3 * slot_lane + 2, slot_end)
    row = lax.broadcasted_iota(jnp.int32, (length, 1), 0)
    tap = (row >= slots).astype(jnp.int32) + (row >= 2 * slots).astype(jnp.int32)
    query_place = length * own_place + 3 * (row - tap * slots) + tap
    matching = segment_rows[number_mb : number_mb + 1, :] == segment_column[number_mb]
    bias[...] = jnp.where((slot_end <= query_place) & matching, 0.0, MASKED_OUT)

    low_lane = lax.broadcasted_iota(jnp.int32, (length, LANES), 1) < HEAD_DIM

    def stacked(part):
        zero = jnp.zeros_like(part)
        return jnp.concatenate(
            [jnp.where(low_lane, part, zero), jnp.where(low_lane, zero, part)], axis=0
        )

    def twice(part):
        return jnp.concatenate([part, part], axis=0)

    def merged(part):
        return jnp.where(low_lane, part[:length], part[length:])

    def lanes_of(g):
        return pl.ds(pl.multiple_of(g * LANES, LANES), LANES)

    def scaled_queries(g):
        part = query_in[:, lanes_of(g)].astype(F32) * SCALE
        return stacked(part).astype(BF16)

    def attend(number, carry):
        lanes = lanes_of(number)
        queries = scaled_queries(number)
        own_key = twice(key_in[:, lanes].astype(F32))
        scores = dot_nt(queries, all_keys[:, lanes]) + twice(bias[...])
        own_score = jnp.sum(queries.astype(F32) * own_key, axis=-1, keepdims=True)
        top = jnp.maximum(own_score, jnp.max(scores, axis=-1, keepdims=True))
        raised = jnp.exp(scores - top)
        own_raised = jnp.exp(own_score - top)
        inverse = 1.0 / (own_raised + jnp.sum(raised, axis=-1, keepdims=True))
        prob = raised * inverse
        own_prob = own_raised * inverse
        if short:
            prob_keep[number] = prob
        statistics[number, :, 0:1] = own_prob
        statistics[number, :, 1:2] = top - jnp.log(inverse)
        result = dot(prob.astype(BF16), all_values[:, lanes])
        own_value = twice(value_in[:, lanes].astype(F32))
        result += own_prob.astype(BF16).astype(F32) * own_value
        attended_out[:, lanes] = merged(result).astype(BF16)
        return carry

    lax.fori_loop(0, GROUPS, attend, 0, unroll=short)

    x = x_in[...]
    hidden = x + dot(attended_out[...], w_out[...])
    unit, inverse_dev = normalize(hidden)
    gain = gain_ffn[...].astype(F32).reshape(1, width)
    normed_ffn_out[...] = (unit * gain).astype(BF16)
    order = order_matrix(length, False)
    cotangent_out[...] = dot(order, cotangent[number_mb, 0]).astype(BF16)
    expanded_sum[...] = hidden
    d_normed_sum[...] = jnp.zeros_like(d_normed_sum)
    chunk = width
    total_width = w_up.shape[1]

    def feed(number, carry):
        columns = pl.ds(pl.multiple_of(number * chunk, chunk), chunk)
        expanded = dot(normed_ffn_out[...], w_up[:, columns])
        square = expanded * expanded
        curve = jnp.tanh(GELU_SCALE * expanded * (1.0 + GELU_CUBIC * square))
        activated = (0.5 * expanded * (1.0 + curve)).astype(BF16)
        activated_out[:, columns] = activated
        slope = 0.5 * (1.0 + curve) + 0.5 * expanded * (1.0 - curve * curve) * (
            GELU_SCALE * (1.0 + 3.0 * GELU_CUBIC * square)
        )
        expanded_sum[...] += dot(activated, w_down[columns, :])
        d_activated = dot_nt(cotangent_out[...], w_down[columns, :])
        d_expanded = (d_activated * slope).astype(BF16)
        d_expanded_out[:, columns] = d_expanded
        d_normed_sum[...] += dot_nt(d_expanded, w_up[:, columns])
        return carry

    lax.fori_loop(0, total_width // chunk, feed, 0, unroll=True)

    unorder = order_matrix(length, True)
    layer_out[...] = dot(unorder, expanded_sum[...].astype(BF16)).astype(BF16)
    d_normed = d_normed_sum[...]
    gain_grad[...] = jnp.sum(d_normed * unit, axis=0, keepdims=True)
    d_hidden = cotangent_out[...].astype(F32) + normalize_back(d_normed, unit, inverse_dev, gain)
    d_hidden_out[...] = d_hidden
    d_branch = d_hidden.astype(BF16)
    d_branch_out[...] = d_branch
    d_attended[...] = dot_nt(d_branch, w_out[...]).astype(BF16)

    value_spot = [key_position[plan.seq_relative(plan.value_order, p)] for p in range(n_seq)]

    def attend_back(number, carry):
        lanes = lanes_of(number)
        queries = scaled_queries(number)
        own_prob = statistics[number, :, 0:1]
        if short:
            prob = prob_keep[number]
        else:
            scores = dot_nt(queries, all_keys[:, lanes]) + twice(bias[...])
            prob = jnp.exp(scores - statistics[number, :, 1:2])
        grads = stacked(d_attended[:, lanes])
        own_value = twice(value_in[:, lanes].astype(F32))
        own_key = twice(key_in[:, lanes].astype(F32))
        prob_grad = dot_nt(grads, all_values[:, lanes])
        own_prob_grad = jnp.sum(grads.astype(F32) * own_value, axis=-1, keepdims=True)
        delta = own_prob * own_prob_grad + jnp.sum(prob * prob_grad, axis=-1, keepdims=True)
        d_score = (prob * (prob_grad - delta)).astype(BF16)
        d_own = (own_prob * (own_prob_grad - delta)).astype(BF16).astype(F32)
        own_low = own_prob.astype(BF16).astype(F32)
        d_query = merged(dot(d_score, all_keys[:, lanes]) + d_own * own_key) * SCALE
        d_query_out[:, lanes] = d_query.astype(BF16)
        d_key_own[:, lanes] = merged(d_own * queries.astype(F32))
        d_value_own[:, lanes] = merged(own_low * grads.astype(F32))
        key_sums = dot_tn(d_score, queries).astype(BF16)
        value_sums = dot_tn(prob.astype(BF16), grads).astype(BF16)
        for p in range(n_seq):
            d_packed_key[p, :, lanes] = key_sums[p * slots : (p + 1) * slots]
            q = value_spot[p]
            d_packed_value[p, :, lanes] = value_sums[q * slots : (q + 1) * slots]
        return carry

    lax.fori_loop(0, GROUPS, attend_back, 0, unroll=short)


def spread(plan, place, order, parts, send, keep, offset):
    rows_block = sum(rows for _, rows in parts)
    half = plan.blocks // 2
    for target, core in ((send, 1), (keep, 0)):
        for p in range(half):
            block = plan.relative(order, core * half + p) ^ place
            start = offset + p * rows_block
            for source, rows in parts:
                target[start : start + rows, :] = source[
                    pl.ds(pl.multiple_of(block * rows, 16), rows), :
                ]
                start += rows


def ffn_grad_kernel(
    plan, order_a, order_b, batch, *refs,
):
    operands, refs = refs[: 7 * batch], refs[7 * batch :]
    activated, cotangent, normed_ffn, d_expanded, attended, d_branch, d_query = (
        operands[i * batch : (i + 1) * batch] for i in range(7)
    )
    normed_in, send, keep, down_rows, up_rows, out_rows, query_rows = refs
    width = cotangent[0].shape[1]
    wide = activated[0].shape[1]
    chunk = 512

    def joined(parts, columns=slice(None)):
        return jnp.concatenate([part[:, columns] for part in parts], axis=0)

    for c in range(wide // chunk):
        columns = slice(c * chunk, (c + 1) * chunk)
        down_rows[columns, :] = dot_tn(joined(activated, columns), joined(cotangent)).astype(BF16)
        up_rows[c] = dot_tn(joined(normed_ffn), joined(d_expanded, columns)).astype(BF16)
    out_rows[...] = dot_tn(joined(attended), joined(d_branch)).astype(BF16)
    normed = [normed_in.at[b] for b in range(batch)]
    query_rows[...] = dot_tn(joined(normed), joined(d_query)).astype(BF16)
    _, mine = own_places(plan)
    down_block = wide // plan.blocks
    thin = width // plan.blocks
    rows_a = down_block + thin
    spread(plan, mine, order_a, ((down_rows, down_block), (out_rows, thin)), send, keep, 0)
    ups = tuple((up_rows.at[c], thin) for c in range(wide // chunk)) + ((query_rows, thin),)
    spread(plan, mine, order_b, ups, send, keep, rows_a * plan.blocks // 2)


def tail_kernel(
    plan, order_a, order_b, batch,
    x_in, normed_in, key_in, value_in, segment_column, gain, *refs,
):
    per_batch, refs = refs[: 7 * batch], refs[7 * batch :]
    d_packed_key, d_packed_value, d_query, d_key_own, d_value_own, d_hidden, gain_ffn_grad = (
        per_batch[i * batch : (i + 1) * batch] for i in range(7)
    )
    (
        w_query, w_key, w_value, conv_key, conv_value,
        send, keep, grad_tokens,
        key_conv_rows, value_conv_rows, key_rows, value_rows,
    ) = refs
    _, length, width = x_in.shape
    slots = length // 3

    def joined(parts):
        return jnp.concatenate([parts[b][...] for b in range(batch)], axis=0)

    masks = [window_masks(segment_column[b], slots) for b in range(batch)]
    normed = joined(normed_in)
    d_queries = joined(d_query)
    grads = []
    for conv, d_packed, flat, own, conv_rows, rows_out in (
        (conv_key, d_packed_key, key_in, d_key_own, key_conv_rows, key_rows),
        (conv_value, d_packed_value, value_in, d_value_own, value_conv_rows, value_rows),
    ):
        back = joined(d_packed)
        pieces = [[None] * 3 for _ in range(batch)]
        for i in range(3):
            taps = []
            from_tap = dot_nt(back, conv[i * width : (i + 1) * width, :])
            for b in range(batch):
                part = flat[b, i * slots : (i + 1) * slots, :].astype(F32) * masks[b][i]
                taps.append(part.astype(BF16))
                pieces[b][i] = from_tap[b * slots : (b + 1) * slots] * masks[b][i]
            window = jnp.concatenate(taps, axis=0)
            conv_rows[i * width : (i + 1) * width, :] = dot_tn(window, back).astype(BF16)
        whole = jnp.concatenate([piece for row in pieces for piece in row], axis=0)
        d_flat = (whole + joined(own)).astype(BF16)
        grads.append(d_flat)
        rows_out[...] = dot_tn(normed, d_flat).astype(BF16)
    d_normed = (
        dot_nt(d_queries, w_query[...])
        + dot_nt(grads[0], w_key[...])
        + dot_nt(grads[1], w_value[...])
    )
    unit, inverse_dev = normalize(joined(x_in))
    gain_grad = jnp.sum(d_normed * unit, axis=0, keepdims=True)
    d_input = normalize_back(d_normed, unit, inverse_dev, gain[...].astype(F32).reshape(1, width))
    result = (joined(d_hidden) + d_input).astype(BF16)
    unorder = order_matrix(length, True)
    for b in range(batch):
        part = result[b * length : (b + 1) * length, :]
        grad_tokens[b, 0] = dot(unorder, part).astype(BF16)
    ffn_grad = sum(part[...] for part in gain_ffn_grad)
    row = lax.broadcasted_iota(jnp.int32, (EXTRA_ROWS, width), 0)
    gains = jnp.where(row == 0, gain_grad, jnp.where(row == 1, ffn_grad, 0.0))
    _, mine = own_places(plan)
    conv_block = 3 * width // plan.blocks
    thin = width // plan.blocks
    rows_a = conv_block + thin
    spread(
        plan, mine, order_a, ((key_conv_rows, conv_block), (key_rows, thin)), send, keep, 0
    )
    spread(
        plan, mine, order_b, ((value_conv_rows, conv_block), (value_rows, thin)), send, keep,
        rows_a * plan.blocks // 2,
    )
    keep[rows_a * plan.blocks :, :] = gains.astype(BF16)
    send[rows_a * plan.blocks :, :] = gains.astype(BF16)


def finish_kernel(plan, layouts, core, count, *refs):
    blocks, refs = refs[0], refs[1 + core * count :]
    targets, (stage, sent) = refs[:count], refs[count:]
    _, mine = own_places(plan)
    half = plan.blocks // 2
    copies = []
    start = 0
    for order, parts in layouts:
        for p in range(half):
            block = plan.relative(order, core * half + p) ^ mine
            for rows, target, columns in parts:
                stage[start : start + rows, :] = blocks[start : start + rows, :].astype(F32)
                spot = pl.ds(pl.multiple_of(block * rows, 16), rows)
                copy = pltpu.make_async_copy(
                    stage.at[pl.ds(start, rows), :],
                    targets[target].at[spot, columns],
                    sent.at[len(copies)],
                )
                copy.start()
                copies.append(copy)
                start += rows
    for copy in copies:
        copy.wait()


def finish(plan, name, layouts, near, far, shapes):
    count = len(shapes)
    copies = plan.blocks // 2 * sum(len(parts) for _, parts in layouts)
    outs = [(shape, F32) for shape in shapes]
    scratch = [pltpu.VMEM(near.shape, F32), pltpu.SemaphoreType.DMA((copies,))]
    everywhere = tuple(range(count))
    targets = call(
        functools.partial(finish_kernel, plan, layouts, 0, count),
        name + "_near", outs, scratch, bytes_accessed=6 * near.size, out_anywhere=everywhere,
    )(near)
    return call(
        functools.partial(finish_kernel, plan, layouts, 1, count),
        name + "_far", outs, scratch, bytes_accessed=6 * near.size,
        anywhere=tuple(range(1, count + 1)), out_anywhere=everywhere,
        aliases={1 + number: number for number in everywhere},
    )(far, *targets)


def add(left, right):
    return (left.astype(F32) + right.astype(F32)).astype(BF16)


def gather_row(plan, array, order):
    held = array[None]
    for number, bit in enumerate(order):
        arrived = plan.swap(held, ("seq", bit))
        if number == len(order) - 1:
            return held, arrived
        held = jnp.concatenate([held, arrived], axis=0)


class Order:
    def __init__(self):
        self.last = ()

    def turn(self, array):
        return after(array, *self.last) if self.last else array

    def done(self, *arrays):
        self.last = arrays


class RowScatter:
    def __init__(self, plan, order, array, bits):
        self.plan, self.order, self.held, self.bits = plan, order, array, list(bits)

    def step(self):
        half = self.held.shape[0] // 2
        arrived = self.plan.swap(self.held[half:], ("seq", self.bits.pop()))
        self.held = add(self.held[:half], self.order.turn(arrived))
        self.order.done(self.held)


def after(value, *earlier):
    return lax.optimization_barrier((value, *earlier))[0]


class Reduction:
    def __init__(self, plan, order, send, keep, split, first_a, first_b, extra=0):
        self.plan, self.order, self.split, self.extra = plan, order, split, extra
        self.send, self.keep = send, keep
        self.bits = list(zip(first_a, first_b))

    def swap(self, array, bit):
        return self.order.turn(self.plan.swap(array, bit))

    def halve(self, array, bit, extra):
        half = (array.shape[0] - extra) // 2
        arrived = self.swap(array[half:], bit)
        total = add(array[:half], arrived[:half])
        if extra:
            total = jnp.concatenate([total, add(array[2 * half :], arrived[half:])], axis=0)
        self.order.done(total)
        return total

    def core(self):
        total = add(self.keep, self.swap(self.send, self.plan.core))
        self.part_a, self.part_b = total[: self.split], total[self.split :]
        self.order.done(self.part_a, self.part_b)

    def scatter_a(self, number):
        self.part_a = self.halve(self.part_a, self.bits[number][0], 0)

    def scatter_b(self, number):
        self.part_b = self.halve(self.part_b, self.bits[number][1], self.extra)

    def scatter_tail(self, number):
        part_a, part_b = self.part_a, self.part_b
        half_a, half_b = part_a.shape[0] // 2, (part_b.shape[0] - self.extra) // 2
        sent = jnp.concatenate([part_a[half_a:], part_b[half_b:]], axis=0)
        arrived = self.swap(sent, self.plan.tail[number])
        self.part_a = add(part_a[:half_a], arrived[:half_a])
        kept = jnp.concatenate([part_b[:half_b], part_b[2 * half_b :]], axis=0)
        self.part_b = add(kept, arrived[half_a:])
        self.order.done(self.part_a, self.part_b)

    def rest(self):
        rows = self.part_a.shape[0]
        for bit in self.plan.rest:
            arrived = self.plan.swap(jnp.concatenate([self.part_a, self.part_b], axis=0), bit)
            self.part_a = add(self.part_a, arrived[:rows])
            self.part_b = add(self.part_b, arrived[rows:])
        kept = self.part_b.shape[0] - self.extra
        self.part_b, extra = self.part_b[:kept], self.part_b[kept:]
        return extra

    def gather_tail(self, number):
        rows = self.part_a.shape[0]
        sent = jnp.concatenate([self.part_a, self.part_b], axis=0)
        arrived = self.swap(sent, self.plan.tail[number])
        self.part_a = jnp.concatenate([self.part_a, arrived[:rows]], axis=0)
        self.part_b = jnp.concatenate([self.part_b, arrived[rows:]], axis=0)
        self.order.done(self.part_a, self.part_b)

    def gather_a(self, number):
        far = self.swap(self.part_a, self.bits[number][0])
        self.part_a = jnp.concatenate([self.part_a, far], axis=0)
        self.order.done(self.part_a)

    def gather_b(self, number):
        far = self.swap(self.part_b, self.bits[number][1])
        self.part_b = jnp.concatenate([self.part_b, far], axis=0)
        self.order.done(self.part_b)

    def last(self):
        near = jnp.concatenate([self.part_a, self.part_b], axis=0)
        return near, self.plan.swap(near, self.plan.core)


def body(
    plan, tokens, segments, cotangent, gain_attn, w_query, w_key, w_value, conv_key, conv_value,
    w_out, gain_ffn, w_up, w_down,
):
    batch, _, length, width = tokens.shape
    slots = length // 3
    square = (width, width)
    flat = ((batch, length, width), BF16)
    flat32 = ((batch, length, width), F32)
    square_here = pltpu.VMEM(square, BF16)
    conv_here = pltpu.VMEM(conv_key.shape, BF16)
    x, normed, queries, key_rows, value_rows, packed_key, packed_value, segment_column = call(
        project_kernel,
        "project",
        [flat32] + [flat] * 4
        + [
            ((batch, slots + EXTRA_ROWS, width), BF16), ((batch, slots, width), BF16),
            ((batch, length, 1), F32),
        ],
        scratch=[square_here] * 3 + [conv_here] * 2
        + [
            pltpu.VMEM(tokens.shape, BF16), pltpu.VMEM(gain_attn.shape, BF16),
            pltpu.VMEM(segments.shape, jnp.int32), pltpu.SemaphoreType.DMA((8,)),
        ],
        flops=2 * batch * length * width * width * 5,
        bytes_accessed=2 * width * width * 9,
        anywhere=tuple(range(8)),
    )(tokens, gain_attn, segments, w_query, w_key, w_value, conv_key, conv_value)

    total_slots = slots * plan.n_seq
    short = total_slots <= SHORT_ROW
    one, one32 = ((length, width), BF16), ((length, width), F32)
    wide = ((length, w_up.shape[1]), BF16)
    packed_shape = ((plan.n_seq, slots, width), BF16)
    layers = []
    for b in range(batch):
        keys = gather_row(plan, packed_key[b], plan.key_order)
        values = gather_row(plan, packed_value[b], plan.value_order)
        layers.append(
            call(
                functools.partial(layer_kernel, plan, short, b),
                "layer",
                [one, one32, one, wide, wide, one, one, one]
                + [one, one32, one32, packed_shape, packed_shape, ((1, width), F32)],
                scratch=[
                    pltpu.VMEM((total_slots, width), BF16),
                    pltpu.VMEM((total_slots, width), BF16),
                    pltpu.VMEM((plan.n_seq, EXTRA_ROWS, LANES), BF16),
                    pltpu.VMEM((length, total_slots), F32),
                    pltpu.VMEM((GROUPS, 2 * length, LANES), F32),
                    pltpu.VMEM((GROUPS if short else 1, 2 * length, total_slots), F32),
                    pltpu.VMEM((length, width), F32),
                    pltpu.VMEM((length, width), F32),
                    pltpu.VMEM((length, width), BF16),
                ],
                flops=2 * length * width * width * 24,
                bytes_accessed=2 * width * width * 20,
                vmem=VMEM_SMALL if short else VMEM_LARGE,
            )(
                x, cotangent, queries, key_rows, value_rows, segment_column, gain_ffn,
                *keys, *values, w_out, w_up, w_down,
            )
        )
    (
        layer_out, d_hidden, normed_ffn, activated, d_expanded, cotangent_rows, attended, d_branch,
        d_query, d_key_own, d_value_own, d_packed_key, d_packed_value, gain_ffn_grad,
    ) = zip(*layers)
    order = Order()
    rows = [
        RowScatter(plan, order, part, bits)
        for b in range(batch)
        for part, bits in ((d_packed_key[b], plan.key_order), (d_packed_value[b], plan.value_order))
    ]
    steps = len(plan.key_order)
    for row in rows[:2]:
        row.step()

    core = [plan.core]
    order_a, order_b = core + plan.first + plan.tail, core + plan.second + plan.tail
    half = plan.blocks // 2
    thin = width // plan.blocks
    down_block = w_down.shape[0] // plan.blocks
    chunks = w_up.shape[1] // width
    rows_a, rows_b = down_block + thin, (chunks + 1) * thin
    buffer = ((half * (rows_a + rows_b), width), BF16)
    ffn_send, ffn_keep = call(
        functools.partial(ffn_grad_kernel, plan, order_a, order_b, batch),
        "ffn_grads",
        [buffer, buffer],
        scratch=[
            pltpu.VMEM((w_down.shape[0], width), BF16),
            pltpu.VMEM((chunks, width, width), BF16),
            square_here,
            square_here,
        ],
        flops=2 * batch * length * width * width * 10,
        bytes_accessed=2 * width * width * 18,
    )(order.turn(activated[0]), *activated[1:], *cotangent_rows, *normed_ffn, *d_expanded, *attended, *d_branch, *d_query, normed)
    ffn = Reduction(plan, order, ffn_send, ffn_keep, half * rows_a, plan.first, plan.second)
    stages, tails = range(len(plan.first)), range(len(plan.tail))
    for row in rows[2:]:
        row.step()
    ffn.core()
    for number in range(1, steps):
        for row in rows:
            row.step()
    own_key_grad, own_value_grad = (
        [row.held[0] for row in rows[kind::2]] for kind in range(2)
    )
    conv_block = conv_key.shape[0] // plan.blocks
    tail_rows = conv_block + thin
    tail_buffer = ((plan.blocks * tail_rows + EXTRA_ROWS, width), BF16)
    tail_send, tail_keep, grad_tokens = call(
        functools.partial(tail_kernel, plan, order_b, order_a, batch),
        "tail",
        [tail_buffer, tail_buffer, (tokens.shape, BF16)],
        scratch=[conv_here, conv_here, square_here, square_here],
        flops=2 * batch * length * width * width * 10,
        bytes_accessed=2 * width * width * 18,
    )(
        x, normed, key_rows, value_rows, segment_column, gain_attn,
        *own_key_grad, *own_value_grad, order.turn(d_query[0]), *d_query[1:], *d_key_own, *d_value_own, *d_hidden,
        *gain_ffn_grad, w_query, w_key, w_value, conv_key, conv_value,
    )
    tail = Reduction(
        plan, order, tail_send, tail_keep, half * tail_rows, plan.second, plan.first, EXTRA_ROWS
    )
    for number in stages[:1]:
        ffn.scatter_a(number)
        ffn.scatter_b(number)
    tail.core()
    for number in stages[1:]:
        ffn.scatter_a(number)
        ffn.scatter_b(number)
    for number in tails[:1]:
        ffn.scatter_tail(number)
    for number in stages[:1]:
        tail.scatter_a(number)
        tail.scatter_b(number)
    for number in tails[1:]:
        ffn.scatter_tail(number)
    for number in stages[1:]:
        tail.scatter_a(number)
        tail.scatter_b(number)
    ffn.rest()
    for number in tails:
        ffn.gather_tail(tails[-1 - number])
        tail.scatter_tail(number)
    gains = tail.rest().astype(F32)
    for number in stages[1:]:
        ffn.gather_a(number)
        ffn.gather_b(number)
    for number in tails:
        tail.gather_tail(tails[-1 - number])
    for number in stages[:1]:
        ffn.gather_a(number)
        ffn.gather_b(number)
    ffn_near, ffn_far = ffn.last()
    for number in stages[1:]:
        tail.gather_a(number)
        tail.gather_b(number)
    for number in stages[:1]:
        tail.gather_a(number)
        tail.gather_b(number)
    tail_near, tail_far = tail.last()
    everything = slice(None)
    ups = [(thin, 2, slice(c * width, (c + 1) * width)) for c in range(chunks)]
    grad_down, grad_out, grad_up, grad_query = finish(
        plan, "ffn_finish",
        [
            (order_a, [(down_block, 0, everything), (thin, 1, everything)]),
            (order_b, ups + [(thin, 3, everything)]),
        ],
        ffn_near, ffn_far, [w_down.shape, square, w_up.shape, square],
    )
    grad_conv_key, grad_key, grad_conv_value, grad_value = finish(
        plan, "tail_finish",
        [
            (order_b, [(conv_block, 0, everything), (thin, 1, everything)]),
            (order_a, [(conv_block, 2, everything), (thin, 3, everything)]),
        ],
        tail_near, tail_far, [conv_key.shape, square, conv_value.shape, square],
    )
    return (
        jnp.stack(layer_out)[:, None], grad_tokens, gains[0], grad_query, grad_key, grad_value,
        grad_conv_key, grad_conv_value, grad_out, gains[1], grad_up, grad_down,
    )


def solution(mesh):
    packed = P(None, "rows", "seq", None)
    in_specs = (packed, P(None, "rows", "seq"), packed) + (P(),) * 10
    out_specs = (packed, packed) + (P(),) * 10
    return jax.shard_map(
        functools.partial(body, Plan(mesh)),
        mesh=mesh, in_specs=in_specs, out_specs=out_specs, check_vma=False,
    )
```

```python
import functools

import jax
import jax.numpy as jnp
from jax import lax
from jax.experimental import pallas as pl
from jax.experimental.pallas import tpu as pltpu
from jax.sharding import PartitionSpec as P

HEADS = 8
HEAD_DIM = 64
LANES = 128
GROUPS = HEADS * HEAD_DIM // LANES
EPSILON = 1e-05
MASKED_OUT = -1e30
SCALE = HEAD_DIM ** (-0.5)
GELU_SCALE = 0.7978845608028654
GELU_CUBIC = 0.044715
SCATTER_BITS = 5
EXTRA_ROWS = 16
VMEM_SMALL = 28 * 1024 * 1024
VMEM_LARGE = 60 * 1024 * 1024
SHORT_ROW = 768
BYTES_MICROSECOND = 3_690_000

EVENTS = (
    "Wb", "Wa", "A1", "A0", "K", "V", "K", "A1", "V", "A0", "K", "TK", "V", "TV", "A1", "B0",
    "A0", "B1", "A1", "A0", "A1", "A0", "B0", "B1", "A1", "A0", "B0", "A1", "B1", "A0", "B0",
    "B1", "A1", "B0", "A0", "B1", "B0", "B1", "B0", "B1", "A1", "A0", "B0", "B1", "A0n", "A0f",
    "A1n", "A1f", "B0", "B0n", "B1", "B0f", "B1n", "B1f",
)

BF16 = jnp.bfloat16
F32 = jnp.float32


def dot(left, right):
    return jnp.dot(left, right, preferred_element_type=F32)


def dot_nt(left, right):
    return lax.dot_general(left, right, (((1,), (1,)), ((), ())), preferred_element_type=F32)


def dot_tn(left, right):
    return lax.dot_general(left, right, (((0,), (0,)), ((), ())), preferred_element_type=F32)


def normalize(values):
    average = jnp.mean(values, axis=-1, keepdims=True)
    centred = values - average
    variance = jnp.mean(centred * centred, axis=-1, keepdims=True)
    inverse_dev = lax.rsqrt(variance + EPSILON)
    return centred * inverse_dev, inverse_dev


def normalize_back(grad_normed, unit, inverse_dev, gain):
    grad_unit = grad_normed * gain
    first_mean = jnp.mean(grad_unit, axis=-1, keepdims=True)
    second_mean = jnp.mean(grad_unit * unit, axis=-1, keepdims=True)
    return inverse_dev * (grad_unit - first_mean - unit * second_mean)


class Plan:
    def __init__(self, mesh):
        self.n_rows = mesh.shape["rows"]
        self.n_seq = mesh.shape["seq"]
        rows = [("rows", 1 << i) for i in range(self.n_rows.bit_length() - 1)]
        seq = [("seq", 1 << i) for i in range(self.n_seq.bit_length() - 1)]
        kept = max(0, min(len(seq), SCATTER_BITS - len(rows)))
        self.seq_block = 1 << kept
        self.blocks = self.n_rows * self.seq_block
        core, others = rows[:1], rows[1:]
        low, high = seq[:1], seq[1:kept] if kept else []
        low = low[:kept]
        self.core = core[0]
        self.first = others + low
        self.second = low + others
        self.tail = high
        self.rest = seq[kept:]
        bits = [1 << i for i in range(len(seq))]
        self.key_order = bits[::-1]
        self.value_order = bits[:1] + bits[:0:-1]

    def mask(self, bit):
        axis, value = bit
        return value * self.seq_block if axis == "rows" else value

    def relative(self, order, position):
        result = 0
        for number, bit in enumerate(order):
            if position >> (len(order) - 1 - number) & 1:
                result |= self.mask(bit)
        return result

    def seq_relative(self, order, position):
        result = 0
        for number, bit in enumerate(order):
            if position >> number & 1:
                result |= bit
        return result

    def swap(self, array, bit):
        axis, value = bit
        size = self.n_rows if axis == "rows" else self.n_seq
        return lax.ppermute(array, axis, [(i, i ^ value) for i in range(size)])


def order_matrix(length, transposed):
    slots = length // 3
    rows = lax.broadcasted_iota(jnp.int32, (length, length), 1 if transposed else 0)
    columns = lax.broadcasted_iota(jnp.int32, (length, length), 0 if transposed else 1)
    tap = (rows >= slots).astype(jnp.int32) + (rows >= 2 * slots).astype(jnp.int32)
    return (columns == 3 * (rows - tap * slots) + tap).astype(BF16)


def window_masks(segment_column, slots):
    last = segment_column[2 * slots :]
    return [(segment_column[i * slots : (i + 1) * slots] == last).astype(F32) for i in range(3)]


def fetch_all(pairs, arrived):
    copies = [
        pltpu.make_async_copy(source, target, arrived.at[number])
        for number, (source, target) in enumerate(pairs)
    ]
    for copy in copies:
        copy.start()

    def ready(number):
        copies[number].wait()
        return pairs[number][1]

    return ready


class Order:
    def __init__(self):
        self.last = ()

    def call(
        self, kernel, name, outs, scratch=(), anywhere=(), out_anywhere=(), aliases=None,
        vmem=VMEM_SMALL, microseconds=0.3, token=0,
    ):
        def spec(number, places):
            return pl.BlockSpec(memory_space=pl.ANY if number in places else pltpu.VMEM)

        def run(*operands):
            count, last = len(operands), self.last

            def without_last(*refs):
                kernel(*refs[:count], *refs[count + len(last) :])

            operands = [
                pltpu.with_memory_space_constraint(operand, pltpu.HBM)
                if number in anywhere and not aliases
                else operand
                for number, operand in enumerate(operands)
            ]
            results = pl.pallas_call(
                without_last,
                name=name,
                out_shape=[
                    pltpu.HBM(shape, dtype)
                    if number in out_anywhere
                    else jax.ShapeDtypeStruct(shape, dtype)
                    for number, (shape, dtype) in enumerate(outs)
                ],
                in_specs=[spec(number, anywhere) for number in range(count)]
                + [pl.BlockSpec(memory_space=pl.ANY)] * len(last),
                out_specs=[spec(number, out_anywhere) for number in range(len(outs))],
                scratch_shapes=list(scratch),
                input_output_aliases=aliases or {},
                compiler_params=pltpu.CompilerParams(vmem_limit_bytes=vmem),
                cost_estimate=pl.CostEstimate(
                    flops=int(microseconds * 1_150_000_000), bytes_accessed=int(microseconds * BYTES_MICROSECOND), transcendentals=0
                ),
            )(*operands, *last)
            self.last = (results[token],)
            return results

        return run

    def combine(self, name, inputs, outs, microseconds=0.3):
        width = inputs[0].shape[1]

        def kernel(*refs):
            sources, targets = refs[: len(inputs)], refs[len(inputs) :]
            for target, pieces in zip(targets, outs):
                offset = 0
                for number, start, rows, *other in pieces:
                    part = sources[number][start : start + rows, :]
                    if other:
                        added = sources[other[0]][other[1] : other[1] + rows, :]
                        part = (part.astype(F32) + added.astype(F32)).astype(BF16)
                    target[offset : offset + rows, :] = part
                    offset += rows

        shapes = [((sum(piece[2] for piece in pieces), width), BF16) for pieces in outs]
        return self.call(kernel, name, shapes, microseconds=microseconds)(*inputs)


def own_places(plan):
    seq = lax.axis_index("seq")
    return seq, lax.axis_index("rows") * plan.seq_block + lax.rem(seq, plan.seq_block)


def read_segments(order, segments, batch):
    length = order.shape[0]
    rows = [segments[b].astype(F32) for b in range(batch)]
    rows = jnp.concatenate(rows + [jnp.zeros((EXTRA_ROWS - batch, length), F32)], axis=0)
    columns = dot_nt(order, rows.astype(BF16))
    return rows, [columns[:, b : b + 1] for b in range(batch)]


def project_kernel(
    tokens_far, gain_far, segments_far, w_query, w_key, w_value, conv_key, conv_value,
    x_out, normed_out, query_out, key_out, value_out, segment_out, packed_key, packed_value,
    query_here, key_here, value_here, conv_key_here, conv_value_here, tokens, gain, segments,
    arrived,
):
    ready = fetch_all(
        [
            (tokens_far, tokens), (segments_far, segments), (gain_far, gain), (w_key, key_here), (conv_key, conv_key_here), (w_value, value_here),
            (conv_value, conv_value_here), (w_query, query_here),
        ],
        arrived,
    )
    batch, _, length, width = tokens.shape
    slots = length // 3
    order = order_matrix(length, False)
    for number in range(3):
        ready(number)
    rows = [dot(order, tokens[b, 0]) for b in range(batch)]
    segment_rows, segment_columns = read_segments(order, segments, batch)
    x = jnp.concatenate(rows, axis=0)
    x_out[...] = x
    for b in range(batch):
        segment_out[b] = segment_columns[b]
    last = lax.broadcasted_iota(jnp.int32, (length, width), 0)
    slot = lax.broadcasted_iota(jnp.int32, (length, width), 1)
    extra = dot(segment_rows.astype(BF16), (last == 3 * slot + 2).astype(BF16)).astype(BF16)
    unit, _ = normalize(x)
    normed = (unit * gain[...].astype(F32).reshape(1, width)).astype(BF16)

    normed_out[...] = normed
    for number, flat_out, packed_out in ((3, key_out, packed_key), (5, value_out, packed_value)):
        flat = dot(normed, ready(number)[...]).astype(BF16)
        flat_out[...] = flat
        taps = [[], [], []]
        for b in range(batch):
            masks = window_masks(segment_columns[b], slots)
            for i in range(3):
                start = b * length + i * slots
                part = flat[start : start + slots].astype(F32) * masks[i]
                taps[i].append(part.astype(BF16))
        conv = ready(number + 1)
        total = None
        for i in range(3):
            term = dot(jnp.concatenate(taps[i], axis=0), conv[i * width : (i + 1) * width, :])
            total = term if total is None else total + term
        packed_out[0 : batch * slots, :] = total.astype(BF16)
    packed_key[batch * slots :, :] = extra
    query_out[...] = dot(normed, ready(7)[...]).astype(BF16)


def layer_kernel(
    plan, short,
    x_in, cotangent, query_in, key_in, value_in, segment_column, gain_ffn,
    keys_near, keys_far, values_near, values_far, w_out, w_up, w_down,
    layer_out, d_hidden_out, normed_ffn_out, activated_out, d_expanded_out, cotangent_out,
    attended_out, d_branch_out, d_query_out, d_key_own, d_value_own,
    d_key_keep, d_key_send, d_value_keep, d_value_send, gain_grad,
    all_keys, all_values, all_extra, bias, statistics, prob_keep, expanded_sum, d_normed_sum,
    d_attended, *copied,
):
    batch, _, length, width = cotangent.shape
    slots = length // 3
    n_seq = plan.n_seq
    half = n_seq // 2
    total_slots = slots * n_seq
    own_place = lax.axis_index("seq")
    key_position = {plan.seq_relative(plan.key_order, p): p for p in range(n_seq)}
    packed_rows = batch * slots
    payload = packed_rows + EXTRA_ROWS
    copies = []

    def put(source, start, rows, target, lanes=slice(None)):
        if short:
            target[...] = source[start : start + rows, lanes]
            return
        copies.append(
            pltpu.make_async_copy(
                source.at[pl.ds(start, rows), lanes], target, copied[0].at[len(copies)]
            )
        )
        copies[-1].start()

    for p in range(n_seq):
        keys, values = (keys_near, values_near) if p < half else (keys_far, values_far)
        place = p % half
        q = key_position[plan.seq_relative(plan.value_order, p)]
        put(
            keys, place * payload + packed_rows, EXTRA_ROWS, all_extra.at[p], slice(0, LANES)
        )
        for b in range(batch):
            put(
                keys, place * payload + b * slots, slots,
                all_keys.at[b, pl.ds(p * slots, slots), :],
            )
            put(
                values, place * packed_rows + b * slots, slots,
                all_values.at[b, pl.ds(q * slots, slots), :],
            )
    for copy in copies:
        copy.wait()

    segment_rows = jnp.zeros((EXTRA_ROWS, total_slots), F32)
    slot_lane = lax.broadcasted_iota(jnp.int32, (1, total_slots), 1)
    slot_end = jnp.zeros((1, total_slots), jnp.int32)
    select_row = lax.broadcasted_iota(jnp.int32, (LANES, total_slots), 0)
    select_lane = lax.broadcasted_iota(jnp.int32, (LANES, total_slots), 1)
    for p in range(n_seq):
        selected = (select_lane == select_row + p * slots) & (select_row < slots)
        segment_rows += dot(all_extra[p], selected.astype(BF16))
        owner = plan.seq_relative(plan.key_order, p) ^ own_place
        here = (slot_lane >= p * slots) & (slot_lane < (p + 1) * slots)
        slot_end = jnp.where(here, length * owner - length * p + 3 * slot_lane + 2, slot_end)
    row = lax.broadcasted_iota(jnp.int32, (length, 1), 0)
    tap = (row >= slots).astype(jnp.int32) + (row >= 2 * slots).astype(jnp.int32)
    query_place = length * own_place + 3 * (row - tap * slots) + tap
    causal = slot_end <= query_place
    for b in range(batch):
        matching = segment_rows[b : b + 1, :] == segment_column[b]
        bias[b] = jnp.where(causal & matching, 0.0, MASKED_OUT)

    low_lane = lax.broadcasted_iota(jnp.int32, (length, LANES), 1) < HEAD_DIM

    def stacked(part):
        zero = jnp.zeros_like(part)
        return jnp.concatenate(
            [jnp.where(low_lane, part, zero), jnp.where(low_lane, zero, part)], axis=0
        )

    def twice(part):
        return jnp.concatenate([part, part], axis=0)

    def merged(part):
        return jnp.where(low_lane, part[:length], part[length:])

    def lanes_of(g):
        return pl.ds(pl.multiple_of(g * LANES, LANES), LANES)

    def place_of(number):
        b, g = number // GROUPS, number % GROUPS
        if short:
            return b, slice(b * length, (b + 1) * length), slice(g * LANES, (g + 1) * LANES)
        return b, pl.ds(pl.multiple_of(b * length, 16), length), lanes_of(g)

    def each(step):
        if short:
            for number in range(batch * GROUPS):
                step(number)
        else:
            lax.fori_loop(0, batch * GROUPS, lambda number, carry: (step(number), carry)[1], 0)

    def scaled_queries(rows, lanes):
        part = query_in[rows, lanes].astype(F32) * SCALE
        return stacked(part).astype(BF16)

    def attend(number):
        b, rows, lanes = place_of(number)
        queries = scaled_queries(rows, lanes)
        own_key = twice(key_in[rows, lanes].astype(F32))
        scores = dot_nt(queries, all_keys[b, :, lanes]) + twice(bias[b])
        own_score = jnp.sum(queries.astype(F32) * own_key, axis=-1, keepdims=True)
        top = jnp.maximum(own_score, jnp.max(scores, axis=-1, keepdims=True))
        raised = jnp.exp(scores - top)
        own_raised = jnp.exp(own_score - top)
        inverse = 1.0 / (own_raised + jnp.sum(raised, axis=-1, keepdims=True))
        prob = raised * inverse
        own_prob = own_raised * inverse
        if short:
            prob_keep[number] = prob
        statistics[number, :, 0:1] = own_prob
        statistics[number, :, 1:2] = top - jnp.log(inverse)
        result = dot(prob.astype(BF16), all_values[b, :, lanes])
        own_value = twice(value_in[rows, lanes].astype(F32))
        result += own_prob.astype(BF16).astype(F32) * own_value
        attended_out[rows, lanes] = merged(result).astype(BF16)

    each(attend)

    x = x_in[...]
    hidden = x + dot(attended_out[...], w_out[...])
    unit, inverse_dev = normalize(hidden)
    gain = gain_ffn[...].astype(F32).reshape(1, width)
    normed_ffn_out[...] = (unit * gain).astype(BF16)
    order = order_matrix(length, False)
    for b in range(batch):
        cotangent_out[b * length : (b + 1) * length, :] = dot(order, cotangent[b, 0]).astype(BF16)
    expanded_sum[...] = hidden
    d_normed_sum[...] = jnp.zeros_like(d_normed_sum)
    chunk = width
    total_width = w_up.shape[1]

    def feed(number, carry):
        columns = pl.ds(pl.multiple_of(number * chunk, chunk), chunk)
        expanded = dot(normed_ffn_out[...], w_up[:, columns])
        square = expanded * expanded
        curve = jnp.tanh(GELU_SCALE * expanded * (1.0 + GELU_CUBIC * square))
        activated = (0.5 * expanded * (1.0 + curve)).astype(BF16)
        activated_out[:, columns] = activated
        slope = 0.5 * (1.0 + curve) + 0.5 * expanded * (1.0 - curve * curve) * (
            GELU_SCALE * (1.0 + 3.0 * GELU_CUBIC * square)
        )
        expanded_sum[...] += dot(activated, w_down[columns, :])
        d_activated = dot_nt(cotangent_out[...], w_down[columns, :])
        d_expanded = (d_activated * slope).astype(BF16)
        d_expanded_out[:, columns] = d_expanded
        d_normed_sum[...] += dot_nt(d_expanded, w_up[:, columns])
        return carry

    lax.fori_loop(0, total_width // chunk, feed, 0, unroll=True)

    unorder = order_matrix(length, True)
    for b in range(batch):
        part = expanded_sum[b * length : (b + 1) * length, :].astype(BF16)
        layer_out[b, 0] = dot(unorder, part).astype(BF16)
    d_normed = d_normed_sum[...]
    gain_grad[...] = jnp.sum(d_normed * unit, axis=0, keepdims=True)
    d_hidden = cotangent_out[...].astype(F32) + normalize_back(d_normed, unit, inverse_dev, gain)
    d_hidden_out[...] = d_hidden
    d_branch = d_hidden.astype(BF16)
    d_branch_out[...] = d_branch
    d_attended[...] = dot_nt(d_branch, w_out[...]).astype(BF16)

    value_spot = [key_position[plan.seq_relative(plan.value_order, p)] for p in range(n_seq)]

    def attend_back(number):
        b, rows, lanes = place_of(number)
        queries = scaled_queries(rows, lanes)
        own_prob = statistics[number, :, 0:1]
        if short:
            prob = prob_keep[number]
        else:
            scores = dot_nt(queries, all_keys[b, :, lanes]) + twice(bias[b])
            prob = jnp.exp(scores - statistics[number, :, 1:2])
        grads = stacked(d_attended[rows, lanes])
        own_value = twice(value_in[rows, lanes].astype(F32))
        own_key = twice(key_in[rows, lanes].astype(F32))
        prob_grad = dot_nt(grads, all_values[b, :, lanes])
        own_prob_grad = jnp.sum(grads.astype(F32) * own_value, axis=-1, keepdims=True)
        delta = own_prob * own_prob_grad + jnp.sum(prob * prob_grad, axis=-1, keepdims=True)
        d_score = (prob * (prob_grad - delta)).astype(BF16)
        d_own = (own_prob * (own_prob_grad - delta)).astype(BF16).astype(F32)
        own_low = own_prob.astype(BF16).astype(F32)
        d_query = merged(dot(d_score, all_keys[b, :, lanes]) + d_own * own_key) * SCALE
        d_query_out[rows, lanes] = d_query.astype(BF16)
        d_key_own[rows, lanes] = merged(d_own * queries.astype(F32))
        d_value_own[rows, lanes] = merged(own_low * grads.astype(F32))
        key_sums = dot_tn(d_score, queries).astype(BF16)
        value_sums = dot_tn(prob.astype(BF16), grads).astype(BF16)
        for p in range(n_seq):
            spot = pl.ds(p % half * packed_rows + b * slots, slots)
            key_target, value_target = (
                (d_key_keep, d_value_keep) if p < half else (d_key_send, d_value_send)
            )
            key_target[spot, lanes] = key_sums[p * slots : (p + 1) * slots]
            q = value_spot[p]
            value_target[spot, lanes] = value_sums[q * slots : (q + 1) * slots]

    each(attend_back)


def spread(plan, place, order, parts, send, keep):
    half = plan.blocks // 2
    for target, core in ((send, 1), (keep, 0)):
        start = 0
        for p in range(half):
            block = plan.relative(order, core * half + p) ^ place
            for source, rows in parts:
                target[start : start + rows, :] = source[
                    pl.ds(pl.multiple_of(block * rows, 16), rows), :
                ]
                start += rows


def down_grad_kernel(
    plan, order, activated, cotangent, attended, d_branch, send, keep, down_rows, out_rows
):
    width = cotangent.shape[1]
    wide = activated.shape[1]
    for c in range(wide // width):
        columns = slice(c * width, (c + 1) * width)
        down_rows[columns, :] = dot_tn(activated[:, columns], cotangent[...]).astype(BF16)
    out_rows[...] = dot_tn(attended[...], d_branch[...]).astype(BF16)
    _, mine = own_places(plan)
    parts = ((down_rows, wide // plan.blocks), (out_rows, width // plan.blocks))
    spread(plan, mine, order, parts, send, keep)


def up_grad_kernel(
    plan, order, normed_ffn, d_expanded, normed, d_query, send, keep, up_rows, query_rows
):
    width = normed_ffn.shape[1]
    chunks = d_expanded.shape[1] // width
    for c in range(chunks):
        columns = slice(c * width, (c + 1) * width)
        up_rows[c] = dot_tn(normed_ffn[...], d_expanded[:, columns]).astype(BF16)
    query_rows[...] = dot_tn(normed[...], d_query[...]).astype(BF16)
    _, mine = own_places(plan)
    thin = width // plan.blocks
    parts = tuple((up_rows.at[c], thin) for c in range(chunks)) + ((query_rows, thin),)
    spread(plan, mine, order, parts, send, keep)


def conv_grads(
    plan, order, segment_column, d_packed, flat, own, conv, normed, conv_rows, flat_rows, send, keep
):
    batch, length, _ = segment_column.shape
    width = conv.shape[1]
    slots = length // 3
    masks = [window_masks(segment_column[b], slots) for b in range(batch)]
    back = d_packed[...]
    pieces = [[None] * 3 for _ in range(batch)]
    for i in range(3):
        taps = []
        from_tap = dot_nt(back, conv[i * width : (i + 1) * width, :])
        for b in range(batch):
            start = b * length + i * slots
            part = flat[start : start + slots, :].astype(F32) * masks[b][i]
            taps.append(part.astype(BF16))
            pieces[b][i] = from_tap[b * slots : (b + 1) * slots] * masks[b][i]
        window = jnp.concatenate(taps, axis=0)
        conv_rows[i * width : (i + 1) * width, :] = dot_tn(window, back).astype(BF16)
    whole = jnp.concatenate([piece for row in pieces for piece in row], axis=0)
    d_flat = (whole + own[...]).astype(BF16)
    flat_rows[...] = dot_tn(normed[...], d_flat).astype(BF16)
    _, mine = own_places(plan)
    parts = ((conv_rows, 3 * width // plan.blocks), (flat_rows, width // plan.blocks))
    spread(plan, mine, order, parts, send, keep)
    return d_flat


def key_grad_kernel(
    plan, order, segment_column, d_packed, flat, own, conv, normed,
    send, keep, d_flat_out, conv_rows, flat_rows,
):
    d_flat_out[...] = conv_grads(
        plan, order, segment_column, d_packed, flat, own, conv, normed, conv_rows, flat_rows,
        send, keep,
    )


def value_grad_kernel(
    plan, order, segment_column, d_packed, flat, own, conv, normed,
    x_in, gain, d_query, d_keys, d_hidden, gain_ffn_grad, w_query, w_key, w_value,
    send, keep, grad_tokens, conv_rows, flat_rows,
):
    batch, _, length, width = grad_tokens.shape
    d_values = conv_grads(
        plan, order, segment_column, d_packed, flat, own, conv, normed, conv_rows, flat_rows,
        send, keep,
    )
    d_normed = (
        dot_nt(d_query[...], w_query[...])
        + dot_nt(d_keys[...], w_key[...])
        + dot_nt(d_values, w_value[...])
    )
    unit, inverse_dev = normalize(x_in[...])
    gain_grad = jnp.sum(d_normed * unit, axis=0, keepdims=True)
    d_input = normalize_back(d_normed, unit, inverse_dev, gain[...].astype(F32).reshape(1, width))
    result = (d_hidden[...] + d_input).astype(BF16)
    unorder = order_matrix(length, True)
    for b in range(batch):
        part = result[b * length : (b + 1) * length, :]
        grad_tokens[b, 0] = dot(unorder, part).astype(BF16)
    row = lax.broadcasted_iota(jnp.int32, (EXTRA_ROWS, width), 0)
    gains = jnp.where(row == 0, gain_grad, jnp.where(row == 1, gain_ffn_grad[...], 0.0))
    send[send.shape[0] - EXTRA_ROWS :, :] = gains.astype(BF16)
    keep[keep.shape[0] - EXTRA_ROWS :, :] = gains.astype(BF16)


def finish_kernel(plan, layout, parts, core, count, *refs):
    blocks, refs = refs[0], refs[1 + core * count :]
    targets, (token, stage, sent) = refs[:count], refs[count:]
    token[...] = jnp.zeros_like(token)
    _, mine = own_places(plan)
    half = plan.blocks // 2
    copies = []
    start = 0
    for p in range(half):
        block = plan.relative(layout, core * half + p) ^ mine
        for rows, target, columns in parts:
            stage[start : start + rows, :] = blocks[start : start + rows, :].astype(F32)
            spot = pl.ds(pl.multiple_of(block * rows, 16), rows)
            copy = pltpu.make_async_copy(
                stage.at[pl.ds(start, rows), :],
                targets[target].at[spot, columns],
                sent.at[len(copies)],
            )
            copy.start()
            copies.append(copy)
            start += rows
    for copy in copies:
        copy.wait()


class RowGather:
    def __init__(self, plan, order, array, bits):
        self.plan, self.order, self.held, self.bits = plan, order, array, list(bits)

    def step(self):
        arrived = self.plan.swap(self.held, ("seq", self.bits.pop(0)))
        if not self.bits:
            return [self.held, arrived]
        rows = self.held.shape[0]
        self.held, = self.order.combine(
            "gather_row", [self.held, arrived], [[(0, 0, rows), (1, 0, rows)]]
        )


class RowScatter:
    def __init__(self, plan, order, keep, send, bits):
        self.plan, self.order, self.keep, self.send = plan, order, keep, send
        self.bits = list(bits)

    def step(self):
        if not self.bits:
            return
        arrived = self.plan.swap(self.send, ("seq", self.bits.pop()))
        rows = self.keep.shape[0]
        half = rows // 2
        outs = [(0, rows)] if not self.bits else [(0, half), (half, half)]
        self.keep, *send = self.order.combine(
            "scatter_row", [self.keep, arrived], [[(0, start, size, 1, start)] for start, size in outs]
        )
        self.send = send[0] if send else None


class Part:
    def __init__(self, plan, order, bits, send, keep, shapes, parts, extra=0):
        self.plan, self.order, self.bits, self.extra = plan, order, bits, extra
        self.send, self.keep = send, keep
        self.shapes, self.parts = shapes, parts
        self.done = 0

    def step(self):
        if self.done < len(self.bits):
            self.scatter(self.bits[self.done])
        else:
            self.gather(self.bits[2 * len(self.bits) - 1 - self.done])
        self.done += 1

    def scatter(self, bit):
        arrived = self.plan.swap(self.send, bit)
        extra = self.extra
        rows = self.keep.shape[0] - extra
        last = [(0, rows, extra, 1, rows)]
        if self.done < len(self.bits) - 1:
            half = rows // 2
            outs = [[(0, start, half, 1, start)] + (last if extra else []) for start in (0, half)]
            self.keep, self.send = self.order.combine("scatter", [self.keep, arrived], outs)
            return
        outs = [[(0, 0, rows, 1, 0)]] + ([last] if extra else [])
        self.held, *self.sums = self.order.combine("scatter", [self.keep, arrived], outs)
        for bit in self.plan.rest:
            arrays = [self.held] + self.sums
            arrived = [self.plan.swap(array, bit) for array in arrays]
            self.held, *self.sums = self.order.combine(
                "scatter_rest", arrays + arrived,
                [
                    [(i, 0, array.shape[0], i + len(arrays), 0)]
                    for i, array in enumerate(arrays)
                ],
            )

    def gather(self, bit):
        arrived = self.plan.swap(self.held, bit)
        if bit == self.plan.core:
            self.far = arrived
            return
        rows = self.held.shape[0]
        self.held, = self.order.combine(
            "gather", [self.held, arrived], [[(0, 0, rows), (1, 0, rows)]]
        )

    def finish(self, core, *targets):
        if core:
            self.gather(self.plan.core)
        blocks = self.far if core else self.held
        count = len(self.shapes)
        everywhere = tuple(range(count))
        copies = self.plan.blocks // 2 * len(self.parts)
        return self.order.call(
            functools.partial(finish_kernel, self.plan, self.bits, self.parts, core, count),
            "finish",
            [(shape, F32) for shape in self.shapes] + [((8, LANES), F32)],
            [pltpu.VMEM(blocks.shape, F32), pltpu.SemaphoreType.DMA((copies,))],
            anywhere=tuple(range(1, count + 1)) if core else (),
            out_anywhere=everywhere,
            aliases={1 + number: number for number in everywhere} if core else None,
            token=count,
        )(blocks, *targets)[:count]


def body(
    plan, tokens, segments, cotangent, gain_attn, w_query, w_key, w_value, conv_key, conv_value,
    w_out, gain_ffn, w_up, w_down,
):
    batch, _, length, width = tokens.shape
    slots = length // 3
    square = (width, width)
    positions = batch * length
    flat, flat32 = ((positions, width), BF16), ((positions, width), F32)
    square_here = pltpu.VMEM(square, BF16)
    conv_here = pltpu.VMEM(conv_key.shape, BF16)
    order = Order()
    x, normed, queries, key_rows, value_rows, segment_column, packed_key, packed_value = order.call(
        project_kernel,
        "project",
        [flat32] + [flat] * 4 + [((batch, length, 1), F32)]
        + [((batch * slots + EXTRA_ROWS, width), BF16), ((batch * slots, width), BF16)],
        scratch=[square_here] * 3 + [conv_here] * 2
        + [
            pltpu.VMEM(tokens.shape, BF16), pltpu.VMEM(gain_attn.shape, BF16),
            pltpu.VMEM(segments.shape, jnp.int32), pltpu.SemaphoreType.DMA((8,)),
        ],
        anywhere=tuple(range(8)),
        token=5,
    )(tokens, gain_attn, segments, w_query, w_key, w_value, conv_key, conv_value)

    steps = len(plan.key_order)
    keys = RowGather(plan, order, packed_key, plan.key_order)
    values = RowGather(plan, order, packed_value, plan.value_order)
    for number in range(steps - 1):
        for gather in (values, keys) if number == 0 else (keys, values):
            gather.step()

    total_slots = slots * plan.n_seq
    short = total_slots <= SHORT_ROW
    wide = ((positions, w_up.shape[1]), BF16)
    half_packed = ((batch * total_slots // 2, width), BF16)
    copied = [] if short else [pltpu.SemaphoreType.DMA((plan.n_seq * (1 + 2 * batch),))]
    (
        layer_out, d_hidden, normed_ffn, activated, d_expanded, cotangent_rows, attended, d_branch,
        d_query, d_key_own, d_value_own, *d_packed, gain_ffn_grad,
    ) = order.call(
        functools.partial(layer_kernel, plan, short),
        "layer",
        [(tokens.shape, BF16), flat32, flat, wide, wide, flat, flat, flat]
        + [flat, flat32, flat32] + [half_packed] * 4 + [((1, width), F32)],
        scratch=[
            pltpu.VMEM((batch, total_slots, width), BF16),
            pltpu.VMEM((batch, total_slots, width), BF16),
            pltpu.VMEM((plan.n_seq, EXTRA_ROWS, LANES), BF16),
            pltpu.VMEM((batch, length, total_slots), F32),
            pltpu.VMEM((batch * GROUPS, 2 * length, LANES), F32),
            pltpu.VMEM((batch * GROUPS if short else 1, 2 * length, total_slots), F32),
            pltpu.VMEM((positions, width), F32),
            pltpu.VMEM((positions, width), F32),
            pltpu.VMEM((positions, width), BF16),
        ]
        + copied,
        anywhere=() if short else (7, 8, 9, 10),
        vmem=VMEM_SMALL if short else VMEM_LARGE,
        token=-1,
    )(
        x, cotangent, queries, key_rows, value_rows, segment_column, gain_ffn,
        *keys.step(), *values.step(), w_out, w_up, w_down,
    )
    rows = [
        RowScatter(plan, order, d_packed[0], d_packed[1], plan.key_order),
        RowScatter(plan, order, d_packed[2], d_packed[3], plan.value_order),
    ]

    core = [plan.core]
    x_first, y_first = core + plan.first + plan.tail, core + plan.second + plan.tail
    bits = {"A0": y_first, "A1": x_first, "B0": y_first, "B1": x_first}
    half = plan.blocks // 2
    thin, down_block, conv_block = (
        rows // plan.blocks for rows in (width, w_down.shape[0], conv_key.shape[0])
    )
    chunks = w_up.shape[1] // width
    everything = slice(None)
    ups = [(thin, 0, slice(c * width, (c + 1) * width)) for c in range(chunks)]
    layouts = {
        "A0": ([w_down.shape, square], [(down_block, 0, everything), (thin, 1, everything)]),
        "A1": ([w_up.shape, square], ups + [(thin, 1, everything)]),
        "B0": ([conv_key.shape, square], [(conv_block, 0, everything), (thin, 1, everything)]),
        "B1": ([conv_value.shape, square], [(conv_block, 0, everything), (thin, 1, everything)]),
    }
    chains, results = {"K": rows[0], "V": rows[1]}, {}

    def make(name, kernel, outs, scratch, operands, extra=0):
        shapes, parts = layouts[name]
        total = half * sum(part[0] for part in parts) + extra
        send, keep, *others = order.call(
            functools.partial(kernel, plan, bits[name]),
            kernel.__name__,
            [((total, width), BF16)] * 2 + outs,
            scratch=scratch,
        )(*operands)
        chains[name] = Part(plan, order, bits[name], send, keep, shapes, parts, extra)
        return others

    wide_here = pltpu.VMEM(w_down.shape, BF16)
    for event in EVENTS:
        if event == "Wa":
            make(
                "A0", down_grad_kernel, [], [wide_here, square_here],
                (activated, cotangent_rows, attended, d_branch),
            )
        elif event == "Wb":
            make(
                "A1", up_grad_kernel, [],
                [pltpu.VMEM((chunks, width, width), BF16), square_here],
                (normed_ffn, d_expanded, normed, d_query),
            )
        elif event == "TK":
            while rows[0].bits:
                rows[0].step()
            d_keys, = make(
                "B0", key_grad_kernel, [flat], [conv_here, square_here],
                (segment_column, rows[0].keep, key_rows, d_key_own, conv_key, normed),
            )
        elif event == "TV":
            while rows[1].bits:
                rows[1].step()
            grad_tokens, = make(
                "B1", value_grad_kernel, [(tokens.shape, BF16)], [conv_here, square_here],
                (
                    segment_column, rows[1].keep, value_rows, d_value_own, conv_value, normed,
                    x, gain_attn, d_query, d_keys, d_hidden, gain_ffn_grad,
                    w_query, w_key, w_value,
                ),
                EXTRA_ROWS,
            )
        elif event[2:] == "n":
            results[event[:2]] = chains[event[:2]].finish(0)
        elif event[2:] == "f":
            results[event[:2]] = chains[event[:2]].finish(1, *results[event[:2]])
        else:
            chains[event].step()
    grad_down, grad_out = results["A0"]
    grad_up, grad_query = results["A1"]
    grad_conv_key, grad_key = results["B0"]
    grad_conv_value, grad_value = results["B1"]
    gains = chains["B1"].sums[0].astype(F32)
    return (
        layer_out, grad_tokens, gains[0], grad_query, grad_key, grad_value,
        grad_conv_key, grad_conv_value, grad_out, gains[1], grad_up, grad_down,
    )


def solution(mesh):
    packed = P(None, "rows", "seq", None)
    in_specs = (packed, P(None, "rows", "seq"), packed) + (P(),) * 10
    out_specs = (packed, packed) + (P(),) * 10
    return jax.shard_map(
        functools.partial(body, Plan(mesh)),
        mesh=mesh, in_specs=in_specs, out_specs=out_specs, check_vma=False,
    )
```

```python
import functools

import jax
import jax.numpy as jnp
from jax import lax
from jax.experimental import pallas as pl
from jax.experimental.pallas import tpu as pltpu
from jax.sharding import PartitionSpec as P

HEADS = 8
HEAD_DIM = 64
LANES = 128
GROUPS = HEADS * HEAD_DIM // LANES
EPSILON = 1e-05
MASKED_OUT = -1e30
SCALE = HEAD_DIM ** (-0.5)
GELU_SCALE = 0.7978845608028654
GELU_CUBIC = 0.044715
SCATTER_BITS = 5
EXTRA_ROWS = 16
VMEM_SMALL = 28 * 1024 * 1024
VMEM_LARGE = 62 * 1024 * 1024
SHORT_ROW = 768
BYTES_MICROSECOND = 3_690_000
EACH = 5

EVENTS = (
    "A1", "A0", "K", "V", "A1", "A0", "V", "K", "A1", "K", "TK", "V", "TV", "A0", "A1", "B0",
    "B1", "A1", "A0", "B0", "B1", "A0", "A1", "B0", "A0", "A1", "B1", "A0", "B0", "B1", "A1",
    "B0", "B1", "A0", "B0", "B1", "A1", "B0", "B1", "A0", "B0", "B1", "A0n", "A1n", "A1f", "A0f",
    "B0", "B0n", "B1", "B0f", "B1n", "B1f",
)

BF16 = jnp.bfloat16
F32 = jnp.float32


def dot(left, right):
    return jnp.dot(left, right, preferred_element_type=F32)


def dot_nt(left, right):
    return lax.dot_general(left, right, (((1,), (1,)), ((), ())), preferred_element_type=F32)


def dot_tn(left, right):
    return lax.dot_general(left, right, (((0,), (0,)), ((), ())), preferred_element_type=F32)


def normalize(values):
    average = jnp.mean(values, axis=-1, keepdims=True)
    centred = values - average
    variance = jnp.mean(centred * centred, axis=-1, keepdims=True)
    inverse_dev = lax.rsqrt(variance + EPSILON)
    return centred * inverse_dev, inverse_dev


def normalize_back(grad_normed, unit, inverse_dev, gain):
    grad_unit = grad_normed * gain
    first_mean = jnp.mean(grad_unit, axis=-1, keepdims=True)
    second_mean = jnp.mean(grad_unit * unit, axis=-1, keepdims=True)
    return inverse_dev * (grad_unit - first_mean - unit * second_mean)


class Plan:
    def __init__(self, mesh):
        self.n_rows = mesh.shape["rows"]
        self.n_seq = mesh.shape["seq"]
        rows = [("rows", 1 << i) for i in range(self.n_rows.bit_length() - 1)]
        seq = [("seq", 1 << i) for i in range(self.n_seq.bit_length() - 1)]
        kept = max(0, min(len(seq), SCATTER_BITS - len(rows)))
        self.seq_block = 1 << kept
        self.blocks = self.n_rows * self.seq_block
        core, others = rows[:1], rows[1:]
        low, high = seq[:1], seq[1:kept] if kept else []
        low = low[:kept]
        self.core = core[0]
        self.first = others + low
        self.second = low + others
        self.tail = high
        self.rest = seq[kept:]
        bits = [1 << i for i in range(len(seq))]
        self.key_order = bits[::-1]
        self.value_order = bits[:1] + bits[:0:-1]

    def mask(self, bit):
        axis, value = bit
        return value * self.seq_block if axis == "rows" else value

    def relative(self, order, position):
        result = 0
        for number, bit in enumerate(order):
            if position >> (len(order) - 1 - number) & 1:
                result |= self.mask(bit)
        return result

    def seq_relative(self, order, position):
        result = 0
        for number, bit in enumerate(order):
            if position >> number & 1:
                result |= bit
        return result

    def swap(self, array, bit, name):
        axis, value = bit
        size = self.n_rows if axis == "rows" else self.n_seq
        with jax.named_scope(f"swap_{name}"):
            return lax.ppermute(array, axis, [(i, i ^ value) for i in range(size)])


def order_matrix(length, transposed):
    slots = length // 3
    rows = lax.broadcasted_iota(jnp.int32, (length, length), 1 if transposed else 0)
    columns = lax.broadcasted_iota(jnp.int32, (length, length), 0 if transposed else 1)
    tap = (rows >= slots).astype(jnp.int32) + (rows >= 2 * slots).astype(jnp.int32)
    return (columns == 3 * (rows - tap * slots) + tap).astype(BF16)


def window_masks(segment_column, slots):
    last = segment_column[2 * slots :]
    return [(segment_column[i * slots : (i + 1) * slots] == last).astype(F32) for i in range(3)]


def fetch_all(pairs, arrived):
    copies = [
        pltpu.make_async_copy(source, target, arrived.at[number])
        for number, (source, target) in enumerate(pairs)
    ]
    for copy in copies:
        copy.start()

    def ready(number):
        copies[number].wait()
        return pairs[number][1]

    return ready


class Order:
    def __init__(self):
        self.last = ()

    def call(
        self, kernel, name, outs, scratch=(), anywhere=(), out_anywhere=(), aliases=None,
        vmem=VMEM_SMALL, microseconds=EACH, token=0,
    ):
        def spec(number, places):
            return pl.BlockSpec(memory_space=pl.ANY if number in places else pltpu.VMEM)

        def run(*operands):
            count, last = len(operands), self.last

            def without_last(*refs):
                kernel(*refs[:count], *refs[count + len(last) :])

            operands = [
                pltpu.with_memory_space_constraint(operand, pltpu.HBM)
                if number in anywhere and not aliases
                else operand
                for number, operand in enumerate(operands)
            ]
            results = pl.pallas_call(
                without_last,
                name=name,
                out_shape=[
                    pltpu.HBM(shape, dtype)
                    if number in out_anywhere
                    else jax.ShapeDtypeStruct(shape, dtype)
                    for number, (shape, dtype) in enumerate(outs)
                ],
                in_specs=[spec(number, anywhere) for number in range(count)]
                + [pl.BlockSpec(memory_space=pl.ANY)] * len(last),
                out_specs=[spec(number, out_anywhere) for number in range(len(outs))],
                scratch_shapes=list(scratch),
                input_output_aliases=aliases or {},
                compiler_params=pltpu.CompilerParams(vmem_limit_bytes=vmem),
                cost_estimate=pl.CostEstimate(
                    flops=1 + int(microseconds * 1_150_000_000), bytes_accessed=1 + int(microseconds * BYTES_MICROSECOND), transcendentals=0
                ),
            )(*operands, *last)
            self.last = (results[token],)
            return results

        return run

    def combine(self, name, inputs, outs, microseconds=EACH):
        width = inputs[0].shape[1]

        def kernel(*refs):
            sources, targets = refs[: len(inputs)], refs[len(inputs) :]
            for target, pieces in zip(targets, outs):
                offset = 0
                for number, start, rows, *other in pieces:
                    part = sources[number][start : start + rows, :]
                    if other:
                        added = sources[other[0]][other[1] : other[1] + rows, :]
                        part = (part.astype(F32) + added.astype(F32)).astype(BF16)
                    target[offset : offset + rows, :] = part
                    offset += rows

        shapes = [((sum(piece[2] for piece in pieces), width), BF16) for pieces in outs]
        return self.call(kernel, name, shapes, microseconds=microseconds)(*inputs)


def own_places(plan):
    seq = lax.axis_index("seq")
    return seq, lax.axis_index("rows") * plan.seq_block + lax.rem(seq, plan.seq_block)


def read_segments(order, segments, batch):
    length = order.shape[0]
    rows = [segments[b].astype(F32) for b in range(batch)]
    rows = jnp.concatenate(rows + [jnp.zeros((EXTRA_ROWS - batch, length), F32)], axis=0)
    columns = dot_nt(order, rows.astype(BF16))
    return rows, [columns[:, b : b + 1] for b in range(batch)]


def project_kernel(
    tokens_far, gain_far, segments_far, w_query, w_key, w_value, conv_key, conv_value,
    x_out, normed_out, query_out, key_out, value_out, segment_out, packed_key, packed_value,
    query_here, key_here, value_here, conv_key_here, conv_value_here, tokens, gain, segments,
    arrived,
):
    ready = fetch_all(
        [
            (tokens_far, tokens), (segments_far, segments), (gain_far, gain), (w_key, key_here), (conv_key, conv_key_here), (w_value, value_here),
            (conv_value, conv_value_here), (w_query, query_here),
        ],
        arrived,
    )
    batch, _, length, width = tokens.shape
    slots = length // 3
    order = order_matrix(length, False)
    for number in range(3):
        ready(number)
    rows = [dot(order, tokens[b, 0]) for b in range(batch)]
    segment_rows, segment_columns = read_segments(order, segments, batch)
    x = jnp.concatenate(rows, axis=0)
    x_out[...] = x
    for b in range(batch):
        segment_out[b] = segment_columns[b]
    last = lax.broadcasted_iota(jnp.int32, (length, width), 0)
    slot = lax.broadcasted_iota(jnp.int32, (length, width), 1)
    extra = dot(segment_rows.astype(BF16), (last == 3 * slot + 2).astype(BF16)).astype(BF16)
    unit, _ = normalize(x)
    normed = (unit * gain[...].astype(F32).reshape(1, width)).astype(BF16)

    normed_out[...] = normed
    for number, flat_out, packed_out in ((3, key_out, packed_key), (5, value_out, packed_value)):
        flat = dot(normed, ready(number)[...]).astype(BF16)
        flat_out[...] = flat
        taps = [[], [], []]
        for b in range(batch):
            masks = window_masks(segment_columns[b], slots)
            for i in range(3):
                start = b * length + i * slots
                part = flat[start : start + slots].astype(F32) * masks[i]
                taps[i].append(part.astype(BF16))
        conv = ready(number + 1)
        total = None
        for i in range(3):
            term = dot(jnp.concatenate(taps[i], axis=0), conv[i * width : (i + 1) * width, :])
            total = term if total is None else total + term
        packed_out[0 : batch * slots, :] = total.astype(BF16)
    packed_key[batch * slots :, :] = extra
    query_out[...] = dot(normed, ready(7)[...]).astype(BF16)


def layer_kernel(
    plan, short, down_order, up_order,
    x_in, normed_in, cotangent, query_in, key_in, value_in, segment_column, gain_ffn,
    keys_near, keys_far, values_near, values_far, w_out, w_up, w_down,
    layer_out, d_hidden_out, d_query_out, d_key_own, d_value_own,
    d_key_keep, d_key_send, d_value_keep, d_value_send,
    down_send, down_keep, up_send, up_keep, gain_grad,
    all_keys, all_values, all_extra, bias, statistics, prob_keep, expanded_sum, d_normed_sum,
    d_attended, normed_ffn_out, activated_out, d_expanded_out, cotangent_out, attended_out,
    d_branch_out, down_rows, up_rows, out_rows, query_rows, *copied,
):
    batch, _, length, width = cotangent.shape
    slots = length // 3
    n_seq = plan.n_seq
    half = n_seq // 2
    total_slots = slots * n_seq
    own_place = lax.axis_index("seq")
    key_position = {plan.seq_relative(plan.key_order, p): p for p in range(n_seq)}
    packed_rows = batch * slots
    payload = packed_rows + EXTRA_ROWS
    copies = []

    def put(source, start, rows, target, lanes=slice(None)):
        if short:
            target[...] = source[start : start + rows, lanes]
            return
        copies.append(
            pltpu.make_async_copy(
                source.at[pl.ds(start, rows), lanes], target, copied[0].at[len(copies)]
            )
        )
        copies[-1].start()

    for p in range(n_seq):
        keys, values = (keys_near, values_near) if p < half else (keys_far, values_far)
        place = p % half
        q = key_position[plan.seq_relative(plan.value_order, p)]
        put(
            keys, place * payload + packed_rows, EXTRA_ROWS, all_extra.at[p], slice(0, LANES)
        )
        for b in range(batch):
            put(
                keys, place * payload + b * slots, slots,
                all_keys.at[b, pl.ds(p * slots, slots), :],
            )
            put(
                values, place * packed_rows + b * slots, slots,
                all_values.at[b, pl.ds(q * slots, slots), :],
            )
    for copy in copies:
        copy.wait()

    segment_rows = jnp.zeros((EXTRA_ROWS, total_slots), F32)
    slot_lane = lax.broadcasted_iota(jnp.int32, (1, total_slots), 1)
    slot_end = jnp.zeros((1, total_slots), jnp.int32)
    select_row = lax.broadcasted_iota(jnp.int32, (LANES, total_slots), 0)
    select_lane = lax.broadcasted_iota(jnp.int32, (LANES, total_slots), 1)
    for p in range(n_seq):
        selected = (select_lane == select_row + p * slots) & (select_row < slots)
        segment_rows += dot(all_extra[p], selected.astype(BF16))
        owner = plan.seq_relative(plan.key_order, p) ^ own_place
        here = (slot_lane >= p * slots) & (slot_lane < (p + 1) * slots)
        slot_end = jnp.where(here, length * owner - length * p + 3 * slot_lane + 2, slot_end)
    row = lax.broadcasted_iota(jnp.int32, (length, 1), 0)
    tap = (row >= slots).astype(jnp.int32) + (row >= 2 * slots).astype(jnp.int32)
    query_place = length * own_place + 3 * (row - tap * slots) + tap
    causal = slot_end <= query_place
    for b in range(batch):
        matching = segment_rows[b : b + 1, :] == segment_column[b]
        bias[b] = jnp.where(causal & matching, 0.0, MASKED_OUT)

    low_lane = lax.broadcasted_iota(jnp.int32, (length, LANES), 1) < HEAD_DIM

    def stacked(part):
        zero = jnp.zeros_like(part)
        return jnp.concatenate(
            [jnp.where(low_lane, part, zero), jnp.where(low_lane, zero, part)], axis=0
        )

    def twice(part):
        return jnp.concatenate([part, part], axis=0)

    def merged(part):
        return jnp.where(low_lane, part[:length], part[length:])

    def lanes_of(g):
        return pl.ds(pl.multiple_of(g * LANES, LANES), LANES)

    def place_of(number):
        b, g = number // GROUPS, number % GROUPS
        if short:
            return b, slice(b * length, (b + 1) * length), slice(g * LANES, (g + 1) * LANES)
        return b, pl.ds(pl.multiple_of(b * length, 16), length), lanes_of(g)

    def each(step):
        if short:
            for number in range(batch * GROUPS):
                step(number)
        else:
            lax.fori_loop(0, batch * GROUPS, lambda number, carry: (step(number), carry)[1], 0)

    def scaled_queries(rows, lanes):
        part = query_in[rows, lanes].astype(F32) * SCALE
        return stacked(part).astype(BF16)

    def attend(number):
        b, rows, lanes = place_of(number)
        queries = scaled_queries(rows, lanes)
        own_key = twice(key_in[rows, lanes].astype(F32))
        scores = dot_nt(queries, all_keys[b, :, lanes]) + twice(bias[b])
        own_score = jnp.sum(queries.astype(F32) * own_key, axis=-1, keepdims=True)
        top = jnp.maximum(own_score, jnp.max(scores, axis=-1, keepdims=True))
        raised = jnp.exp(scores - top)
        own_raised = jnp.exp(own_score - top)
        inverse = 1.0 / (own_raised + jnp.sum(raised, axis=-1, keepdims=True))
        prob = raised * inverse
        own_prob = own_raised * inverse
        if short:
            prob_keep[number] = prob
        statistics[number, :, 0:1] = own_prob
        statistics[number, :, 1:2] = top - jnp.log(inverse)
        result = dot(prob.astype(BF16), all_values[b, :, lanes])
        own_value = twice(value_in[rows, lanes].astype(F32))
        result += own_prob.astype(BF16).astype(F32) * own_value
        attended_out[rows, lanes] = merged(result).astype(BF16)

    each(attend)

    x = x_in[...]
    hidden = x + dot(attended_out[...], w_out[...])
    unit, inverse_dev = normalize(hidden)
    gain = gain_ffn[...].astype(F32).reshape(1, width)
    normed_ffn_out[...] = (unit * gain).astype(BF16)
    order = order_matrix(length, False)
    for b in range(batch):
        cotangent_out[b * length : (b + 1) * length, :] = dot(order, cotangent[b, 0]).astype(BF16)
    expanded_sum[...] = hidden
    d_normed_sum[...] = jnp.zeros_like(d_normed_sum)
    chunk = width
    total_width = w_up.shape[1]

    def feed(number, carry):
        columns = pl.ds(pl.multiple_of(number * chunk, chunk), chunk)
        expanded = dot(normed_ffn_out[...], w_up[:, columns])
        square = expanded * expanded
        curve = jnp.tanh(GELU_SCALE * expanded * (1.0 + GELU_CUBIC * square))
        activated = (0.5 * expanded * (1.0 + curve)).astype(BF16)
        activated_out[:, columns] = activated
        slope = 0.5 * (1.0 + curve) + 0.5 * expanded * (1.0 - curve * curve) * (
            GELU_SCALE * (1.0 + 3.0 * GELU_CUBIC * square)
        )
        expanded_sum[...] += dot(activated, w_down[columns, :])
        d_activated = dot_nt(cotangent_out[...], w_down[columns, :])
        d_expanded = (d_activated * slope).astype(BF16)
        d_expanded_out[:, columns] = d_expanded
        d_normed_sum[...] += dot_nt(d_expanded, w_up[:, columns])
        return carry

    lax.fori_loop(0, total_width // chunk, feed, 0, unroll=short)

    unorder = order_matrix(length, True)
    for b in range(batch):
        part = expanded_sum[b * length : (b + 1) * length, :].astype(BF16)
        layer_out[b, 0] = dot(unorder, part).astype(BF16)
    d_normed = d_normed_sum[...]
    gain_grad[...] = jnp.sum(d_normed * unit, axis=0, keepdims=True)
    d_hidden = cotangent_out[...].astype(F32) + normalize_back(d_normed, unit, inverse_dev, gain)
    d_hidden_out[...] = d_hidden
    d_branch = d_hidden.astype(BF16)
    d_branch_out[...] = d_branch
    d_attended[...] = dot_nt(d_branch, w_out[...]).astype(BF16)

    value_spot = [key_position[plan.seq_relative(plan.value_order, p)] for p in range(n_seq)]

    def attend_back(number):
        b, rows, lanes = place_of(number)
        queries = scaled_queries(rows, lanes)
        own_prob = statistics[number, :, 0:1]
        if short:
            prob = prob_keep[number]
        else:
            scores = dot_nt(queries, all_keys[b, :, lanes]) + twice(bias[b])
            prob = jnp.exp(scores - statistics[number, :, 1:2])
        grads = stacked(d_attended[rows, lanes])
        own_value = twice(value_in[rows, lanes].astype(F32))
        own_key = twice(key_in[rows, lanes].astype(F32))
        prob_grad = dot_nt(grads, all_values[b, :, lanes])
        own_prob_grad = jnp.sum(grads.astype(F32) * own_value, axis=-1, keepdims=True)
        delta = own_prob * own_prob_grad + jnp.sum(prob * prob_grad, axis=-1, keepdims=True)
        d_score = (prob * (prob_grad - delta)).astype(BF16)
        d_own = (own_prob * (own_prob_grad - delta)).astype(BF16).astype(F32)
        own_low = own_prob.astype(BF16).astype(F32)
        d_query = merged(dot(d_score, all_keys[b, :, lanes]) + d_own * own_key) * SCALE
        d_query_out[rows, lanes] = d_query.astype(BF16)
        d_key_own[rows, lanes] = merged(d_own * queries.astype(F32))
        d_value_own[rows, lanes] = merged(own_low * grads.astype(F32))
        key_sums = dot_tn(d_score, queries).astype(BF16)
        value_sums = dot_tn(prob.astype(BF16), grads).astype(BF16)
        for p in range(n_seq):
            spot = pl.ds(p % half * packed_rows + b * slots, slots)
            key_target, value_target = (
                (d_key_keep, d_value_keep) if p < half else (d_key_send, d_value_send)
            )
            key_target[spot, lanes] = key_sums[p * slots : (p + 1) * slots]
            q = value_spot[p]
            value_target[spot, lanes] = value_sums[q * slots : (q + 1) * slots]

    each(attend_back)

    for c in range(total_width // chunk):
        columns = slice(c * chunk, (c + 1) * chunk)
        down_rows[columns, :] = dot_tn(activated_out[:, columns], cotangent_out[...]).astype(BF16)
        up_rows[c] = dot_tn(normed_ffn_out[...], d_expanded_out[:, columns]).astype(BF16)
    out_rows[...] = dot_tn(attended_out[...], d_branch_out[...]).astype(BF16)
    query_rows[...] = dot_tn(normed_in[...], d_query_out[...]).astype(BF16)
    _, mine = own_places(plan)
    thin = width // plan.blocks
    parts = ((down_rows, total_width // plan.blocks), (out_rows, thin))
    spread(plan, mine, down_order, parts, down_send, down_keep)
    parts = tuple((up_rows.at[c], thin) for c in range(total_width // chunk))
    spread(plan, mine, up_order, parts + ((query_rows, thin),), up_send, up_keep)


def spread(plan, place, order, parts, send, keep):
    half = plan.blocks // 2
    for target, core in ((send, 1), (keep, 0)):
        start = 0
        for p in range(half):
            block = plan.relative(order, core * half + p) ^ place
            for source, rows in parts:
                target[start : start + rows, :] = source[
                    pl.ds(pl.multiple_of(block * rows, 16), rows), :
                ]
                start += rows


def conv_grads(
    plan, order, segment_column, d_packed, flat, own, conv, normed, conv_rows, flat_rows, send, keep
):
    batch, length, _ = segment_column.shape
    width = conv.shape[1]
    slots = length // 3
    masks = [window_masks(segment_column[b], slots) for b in range(batch)]
    back = d_packed[...]
    pieces = [[None] * 3 for _ in range(batch)]
    for i in range(3):
        taps = []
        from_tap = dot_nt(back, conv[i * width : (i + 1) * width, :])
        for b in range(batch):
            start = b * length + i * slots
            part = flat[start : start + slots, :].astype(F32) * masks[b][i]
            taps.append(part.astype(BF16))
            pieces[b][i] = from_tap[b * slots : (b + 1) * slots] * masks[b][i]
        window = jnp.concatenate(taps, axis=0)
        conv_rows[i * width : (i + 1) * width, :] = dot_tn(window, back).astype(BF16)
    whole = jnp.concatenate([piece for row in pieces for piece in row], axis=0)
    d_flat = (whole + own[...]).astype(BF16)
    flat_rows[...] = dot_tn(normed[...], d_flat).astype(BF16)
    _, mine = own_places(plan)
    parts = ((conv_rows, 3 * width // plan.blocks), (flat_rows, width // plan.blocks))
    spread(plan, mine, order, parts, send, keep)
    return d_flat


def key_grad_kernel(
    plan, order, segment_column, d_packed, flat, own, conv, normed,
    send, keep, d_flat_out, conv_rows, flat_rows,
):
    d_flat_out[...] = conv_grads(
        plan, order, segment_column, d_packed, flat, own, conv, normed, conv_rows, flat_rows,
        send, keep,
    )


def value_grad_kernel(
    plan, order, segment_column, d_packed, flat, own, conv, normed,
    x_in, gain, d_query, d_keys, d_hidden, gain_ffn_grad, w_query, w_key, w_value,
    send, keep, grad_tokens, conv_rows, flat_rows,
):
    batch, _, length, width = grad_tokens.shape
    d_values = conv_grads(
        plan, order, segment_column, d_packed, flat, own, conv, normed, conv_rows, flat_rows,
        send, keep,
    )
    d_normed = (
        dot_nt(d_query[...], w_query[...])
        + dot_nt(d_keys[...], w_key[...])
        + dot_nt(d_values, w_value[...])
    )
    unit, inverse_dev = normalize(x_in[...])
    gain_grad = jnp.sum(d_normed * unit, axis=0, keepdims=True)
    d_input = normalize_back(d_normed, unit, inverse_dev, gain[...].astype(F32).reshape(1, width))
    result = (d_hidden[...] + d_input).astype(BF16)
    unorder = order_matrix(length, True)
    for b in range(batch):
        part = result[b * length : (b + 1) * length, :]
        grad_tokens[b, 0] = dot(unorder, part).astype(BF16)
    row = lax.broadcasted_iota(jnp.int32, (EXTRA_ROWS, width), 0)
    gains = jnp.where(row == 0, gain_grad, jnp.where(row == 1, gain_ffn_grad[...], 0.0))
    send[send.shape[0] - EXTRA_ROWS :, :] = gains.astype(BF16)
    keep[keep.shape[0] - EXTRA_ROWS :, :] = gains.astype(BF16)


def finish_kernel(plan, layout, parts, core, count, *refs):
    blocks, refs = refs[0], refs[1 + core * count :]
    targets, (token, stage, sent) = refs[:count], refs[count:]
    token[...] = jnp.zeros_like(token)
    _, mine = own_places(plan)
    half = plan.blocks // 2
    copies = []
    start = 0
    for p in range(half):
        block = plan.relative(layout, core * half + p) ^ mine
        for rows, target, columns in parts:
            stage[start : start + rows, :] = blocks[start : start + rows, :].astype(F32)
            spot = pl.ds(pl.multiple_of(block * rows, 16), rows)
            copy = pltpu.make_async_copy(
                stage.at[pl.ds(start, rows), :],
                targets[target].at[spot, columns],
                sent.at[len(copies)],
            )
            copy.start()
            copies.append(copy)
            start += rows
    for copy in copies:
        copy.wait()


class RowGather:
    def __init__(self, name, plan, order, array, bits):
        self.name, self.plan, self.order = name, plan, order
        self.held, self.bits = array, list(bits)

    def step(self):
        arrived = self.plan.swap(self.held, ("seq", self.bits.pop(0)), self.name)
        if not self.bits:
            return [self.held, arrived]
        rows = self.held.shape[0]
        self.held, = self.order.combine(
            "gather_row", [self.held, arrived], [[(0, 0, rows), (1, 0, rows)]]
        )


class RowScatter:
    def __init__(self, name, plan, order, keep, send, bits):
        self.name, self.plan, self.order, self.keep, self.send = name, plan, order, keep, send
        self.bits = list(bits)

    def step(self, microseconds=EACH):
        if not self.bits:
            return
        arrived = self.plan.swap(self.send, ("seq", self.bits.pop()), self.name)
        rows = self.keep.shape[0]
        half = rows // 2
        outs = [(0, rows)] if not self.bits else [(0, half), (half, half)]
        self.keep, *send = self.order.combine(
            "scatter_row", [self.keep, arrived],
            [[(0, start, size, 1, start)] for start, size in outs], microseconds,
        )
        self.send = send[0] if send else None


class Part:
    def __init__(self, name, plan, order, bits, send, keep, shapes, parts, extra=0):
        self.name, self.plan, self.order, self.bits, self.extra = name, plan, order, bits, extra
        self.send, self.keep = send, keep
        self.shapes, self.parts = shapes, parts
        self.done = 0

    def step(self, microseconds):
        if self.done < len(self.bits):
            self.scatter(self.bits[self.done], microseconds)
        else:
            self.gather(self.bits[2 * len(self.bits) - 1 - self.done], microseconds)
        self.done += 1

    def scatter(self, bit, microseconds):
        arrived = self.plan.swap(self.send, bit, self.name)
        extra = self.extra
        rows = self.keep.shape[0] - extra
        last = [(0, rows, extra, 1, rows)]
        if self.done < len(self.bits) - 1:
            half = rows // 2
            outs = [[(0, start, half, 1, start)] + (last if extra else []) for start in (0, half)]
            self.keep, self.send = self.order.combine(
                "scatter", [self.keep, arrived], outs, microseconds
            )
            return
        outs = [[(0, 0, rows, 1, 0)]] + ([last] if extra else [])
        self.held, *self.sums = self.order.combine(
            "scatter", [self.keep, arrived], outs, microseconds
        )
        for bit in self.plan.rest:
            arrays = [self.held] + self.sums
            arrived = [self.plan.swap(array, bit, self.name) for array in arrays]
            self.held, *self.sums = self.order.combine(
                "scatter_rest", arrays + arrived,
                [
                    [(i, 0, array.shape[0], i + len(arrays), 0)]
                    for i, array in enumerate(arrays)
                ],
            )

    def gather(self, bit, microseconds=EACH):
        arrived = self.plan.swap(self.held, bit, self.name)
        if bit == self.plan.core:
            self.far = arrived
            return
        rows = self.held.shape[0]
        self.held, = self.order.combine(
            "gather", [self.held, arrived], [[(0, 0, rows), (1, 0, rows)]], microseconds
        )

    def finish(self, core, *targets):
        if core:
            self.gather(self.plan.core)
        blocks = self.far if core else self.held
        count = len(self.shapes)
        everywhere = tuple(range(count))
        copies = self.plan.blocks // 2 * len(self.parts)
        return self.order.call(
            functools.partial(finish_kernel, self.plan, self.bits, self.parts, core, count),
            "finish",
            [(shape, F32) for shape in self.shapes] + [((8, LANES), F32)],
            [pltpu.VMEM(blocks.shape, F32), pltpu.SemaphoreType.DMA((copies,))],
            anywhere=tuple(range(1, count + 1)) if core else (),
            out_anywhere=everywhere,
            aliases={1 + number: number for number in everywhere} if core else None,
            token=count,
        )(blocks, *targets)[:count]


def body(
    plan, tokens, segments, cotangent, gain_attn, w_query, w_key, w_value, conv_key, conv_value,
    w_out, gain_ffn, w_up, w_down,
):
    batch, _, length, width = tokens.shape
    slots = length // 3
    square = (width, width)
    positions = batch * length
    flat, flat32 = ((positions, width), BF16), ((positions, width), F32)
    square_here = pltpu.VMEM(square, BF16)
    conv_here = pltpu.VMEM(conv_key.shape, BF16)
    order = Order()
    x, normed, queries, key_rows, value_rows, segment_column, packed_key, packed_value = order.call(
        project_kernel,
        "project",
        [flat32] + [flat] * 4 + [((batch, length, 1), F32)]
        + [((batch * slots + EXTRA_ROWS, width), BF16), ((batch * slots, width), BF16)],
        scratch=[square_here] * 3 + [conv_here] * 2
        + [
            pltpu.VMEM(tokens.shape, BF16), pltpu.VMEM(gain_attn.shape, BF16),
            pltpu.VMEM(segments.shape, jnp.int32), pltpu.SemaphoreType.DMA((8,)),
        ],
        anywhere=tuple(range(8)),
        token=5,
    )(tokens, gain_attn, segments, w_query, w_key, w_value, conv_key, conv_value)

    steps = len(plan.key_order)
    keys = RowGather("gather_keys", plan, order, packed_key, plan.key_order)
    values = RowGather("gather_values", plan, order, packed_value, plan.value_order)
    for number in range(steps - 1):
        keys.step()
        values.step()

    core = [plan.core]
    x_first, y_first = core + plan.first + plan.tail, core + plan.second + plan.tail
    bits = {"A0": y_first, "A1": x_first, "B0": y_first, "B1": x_first}
    half = plan.blocks // 2
    thin, down_block, conv_block = (
        rows // plan.blocks for rows in (width, w_down.shape[0], conv_key.shape[0])
    )
    chunks = w_up.shape[1] // width
    everything = slice(None)
    ups = [(thin, 0, slice(c * width, (c + 1) * width)) for c in range(chunks)]
    layouts = {
        "A0": ([w_down.shape, square], [(down_block, 0, everything), (thin, 1, everything)]),
        "A1": ([w_up.shape, square], ups + [(thin, 1, everything)]),
        "B0": ([conv_key.shape, square], [(conv_block, 0, everything), (thin, 1, everything)]),
        "B1": ([conv_value.shape, square], [(conv_block, 0, everything), (thin, 1, everything)]),
    }

    def half_rows(name):
        return half * sum(part[0] for part in layouts[name][1])

    total_slots = slots * plan.n_seq
    short = total_slots <= SHORT_ROW
    half_packed = ((batch * total_slots // 2, width), BF16)
    halves = [((half_rows(name), width), BF16) for name in ("A0", "A0", "A1", "A1")]
    flat_here = pltpu.VMEM((positions, width), BF16)
    wide_here = pltpu.VMEM((positions, w_up.shape[1]), BF16)
    copied = [] if short else [pltpu.SemaphoreType.DMA((plan.n_seq * (1 + 2 * batch),))]
    layer_out, d_hidden, d_query, d_key_own, d_value_own, *outs, gain_ffn_grad = order.call(
        functools.partial(layer_kernel, plan, short, bits["A0"], bits["A1"]),
        "layer",
        [(tokens.shape, BF16), flat32, flat, flat32, flat32] + [half_packed] * 4 + halves
        + [((1, width), F32)],
        scratch=[
            pltpu.VMEM((batch, total_slots, width), BF16),
            pltpu.VMEM((batch, total_slots, width), BF16),
            pltpu.VMEM((plan.n_seq, EXTRA_ROWS, LANES), BF16),
            pltpu.VMEM((batch, length, total_slots), F32),
            pltpu.VMEM((batch * GROUPS, 2 * length, LANES), F32),
            pltpu.VMEM((batch * GROUPS, 2 * length, total_slots) if short else (1, 8, LANES), F32),
            pltpu.VMEM((positions, width), F32),
            pltpu.VMEM((positions, width), F32),
            flat_here, flat_here, wide_here, wide_here, flat_here, flat_here, flat_here,
            pltpu.VMEM(w_down.shape, BF16),
            pltpu.VMEM((chunks, width, width), BF16),
            square_here, square_here,
        ]
        + copied,
        anywhere=() if short else (8, 9, 10, 11),
        vmem=VMEM_SMALL if short else VMEM_LARGE,
        token=-1,
    )(
        x, normed, cotangent, queries, key_rows, value_rows, segment_column, gain_ffn,
        *keys.step(), *values.step(), w_out, w_up, w_down,
    )
    rows = [
        RowScatter("K", plan, order, outs[0], outs[1], plan.key_order),
        RowScatter("V", plan, order, outs[2], outs[3], plan.value_order),
    ]
    chains, results = {"K": rows[0], "V": rows[1]}, {}
    for name, (send, keep) in (("A0", outs[4:6]), ("A1", outs[6:8])):
        chains[name] = Part(name, plan, order, bits[name], send, keep, *layouts[name])

    def make(name, kernel, outs, scratch, operands, extra=0):
        total = half_rows(name) + extra
        send, keep, *others = order.call(
            functools.partial(kernel, plan, bits[name]),
            kernel.__name__,
            [((total, width), BF16)] * 2 + outs,
            scratch=scratch,
        )(*operands)
        chains[name] = Part(name, plan, order, bits[name], send, keep, *layouts[name], extra)
        return others

    for event in EVENTS:
        if event == "TK":
            while rows[0].bits:
                rows[0].step()
            d_keys, = make(
                "B0", key_grad_kernel, [flat], [conv_here, square_here],
                (segment_column, rows[0].keep, key_rows, d_key_own, conv_key, normed),
            )
        elif event == "TV":
            while rows[1].bits:
                rows[1].step()
            grad_tokens, = make(
                "B1", value_grad_kernel, [(tokens.shape, BF16)], [conv_here, square_here],
                (
                    segment_column, rows[1].keep, value_rows, d_value_own, conv_value, normed,
                    x, gain_attn, d_query, d_keys, d_hidden, gain_ffn_grad,
                    w_query, w_key, w_value,
                ),
                EXTRA_ROWS,
            )
        elif event[2:] == "n":
            results[event[:2]] = chains[event[:2]].finish(0)
        elif event[2:] == "f":
            results[event[:2]] = chains[event[:2]].finish(1, *results[event[:2]])
        else:
            name, _, cost = event.partition(":")
            chains[name].step(float(cost or EACH))
    grad_down, grad_out = results["A0"]
    grad_up, grad_query = results["A1"]
    grad_conv_key, grad_key = results["B0"]
    grad_conv_value, grad_value = results["B1"]
    gains = chains["B1"].sums[0].astype(F32)
    return (
        layer_out, grad_tokens, gains[0], grad_query, grad_key, grad_value,
        grad_conv_key, grad_conv_value, grad_out, gains[1], grad_up, grad_down,
    )


def solution(mesh):
    packed = P(None, "rows", "seq", None)
    in_specs = (packed, P(None, "rows", "seq"), packed) + (P(),) * 10
    out_specs = (packed, packed) + (P(),) * 10
    return jax.shard_map(
        functools.partial(body, Plan(mesh)),
        mesh=mesh, in_specs=in_specs, out_specs=out_specs, check_vma=False,
    )
```

```python
import functools

import jax
import jax.numpy as jnp
from jax import lax
from jax.experimental import pallas as pl
from jax.experimental.pallas import tpu as pltpu
from jax.sharding import PartitionSpec as P

HEADS = 8
HEAD_DIM = 64
LANES = 128
GROUPS = HEADS * HEAD_DIM // LANES
EPSILON = 1e-05
MASKED_OUT = -1e30
SCALE = HEAD_DIM ** (-0.5)
GELU_SCALE = 0.7978845608028654
GELU_CUBIC = 0.044715
SCATTER_BITS = 5
EXTRA_ROWS = 16
VMEM_SMALL = 28 * 1024 * 1024
VMEM_LARGE = 62 * 1024 * 1024
SHORT_ROW = 768
BYTES_MICROSECOND = 3_690_000
EACH = 5

EVENTS = (
    "A0", "A1", "K", "V", "A1", "A0", "V", "K", "A1", "K", "V", "TK", "TV", "T3", "A0", "A1",
    "B2", "B1", "B0", "A0", "A1", "B1", "B2", "B0", "A0", "A1", "B1", "B2", "A0", "A1", "B0",
    "B2", "B1", "A0", "A1", "B0", "B2", "B1", "A0", "B0", "B2", "B1", "B0", "A1", "B2", "B1",
    "B0", "A0", "B2", "B0", "B1", "B2", "Af", "B0", "B1", "Bn", "Bf",
)

BF16 = jnp.bfloat16
F32 = jnp.float32


def dot(left, right):
    return jnp.dot(left, right, preferred_element_type=F32)


def dot_nt(left, right):
    return lax.dot_general(left, right, (((1,), (1,)), ((), ())), preferred_element_type=F32)


def dot_tn(left, right):
    return lax.dot_general(left, right, (((0,), (0,)), ((), ())), preferred_element_type=F32)


def normalize(values):
    average = jnp.mean(values, axis=-1, keepdims=True)
    centred = values - average
    variance = jnp.mean(centred * centred, axis=-1, keepdims=True)
    inverse_dev = lax.rsqrt(variance + EPSILON)
    return centred * inverse_dev, inverse_dev


def normalize_back(grad_normed, unit, inverse_dev, gain):
    grad_unit = grad_normed * gain
    first_mean = jnp.mean(grad_unit, axis=-1, keepdims=True)
    second_mean = jnp.mean(grad_unit * unit, axis=-1, keepdims=True)
    return inverse_dev * (grad_unit - first_mean - unit * second_mean)


class Plan:
    def __init__(self, mesh):
        self.n_rows = mesh.shape["rows"]
        self.n_seq = mesh.shape["seq"]
        rows = [("rows", 1 << i) for i in range(self.n_rows.bit_length() - 1)]
        seq = [("seq", 1 << i) for i in range(self.n_seq.bit_length() - 1)]
        kept = max(0, min(len(seq), SCATTER_BITS - len(rows)))
        self.seq_block = 1 << kept
        self.blocks = self.n_rows * self.seq_block
        core, others = rows[:1], rows[1:]
        low, high = seq[:1], seq[1:kept] if kept else []
        low = low[:kept]
        self.core = core[0]
        self.first = others + low
        self.second = low + others
        self.tail = high
        self.rest = seq[kept:]
        bits = [1 << i for i in range(len(seq))]
        self.key_order = bits[::-1]
        self.value_order = bits[:1] + bits[:0:-1]

    def mask(self, bit):
        axis, value = bit
        return value * self.seq_block if axis == "rows" else value

    def relative(self, order, position):
        result = 0
        for number, bit in enumerate(order):
            if position >> (len(order) - 1 - number) & 1:
                result |= self.mask(bit)
        return result

    def seq_relative(self, order, position):
        result = 0
        for number, bit in enumerate(order):
            if position >> number & 1:
                result |= bit
        return result

    def swap(self, array, bit, name):
        axis, value = bit
        size = self.n_rows if axis == "rows" else self.n_seq
        with jax.named_scope(f"swap_{name}"):
            return lax.ppermute(array, axis, [(i, i ^ value) for i in range(size)])


def order_matrix(length, transposed):
    slots = length // 3
    rows = lax.broadcasted_iota(jnp.int32, (length, length), 1 if transposed else 0)
    columns = lax.broadcasted_iota(jnp.int32, (length, length), 0 if transposed else 1)
    tap = (rows >= slots).astype(jnp.int32) + (rows >= 2 * slots).astype(jnp.int32)
    return (columns == 3 * (rows - tap * slots) + tap).astype(BF16)


def window_masks(segment_column, slots):
    last = segment_column[2 * slots :]
    return [(segment_column[i * slots : (i + 1) * slots] == last).astype(F32) for i in range(3)]


def fetch_all(pairs, arrived):
    copies = [
        pltpu.make_async_copy(source, target, arrived.at[number])
        for number, (source, target) in enumerate(pairs)
    ]
    for copy in copies:
        copy.start()

    def ready(number):
        copies[number].wait()
        return pairs[number][1]

    return ready


class Order:
    def __init__(self):
        self.last = ()

    def call(
        self, kernel, name, outs, scratch=(), anywhere=(), out_anywhere=(), aliases=None,
        vmem=VMEM_SMALL, microseconds=EACH, token=0,
    ):
        def spec(number, places):
            return pl.BlockSpec(memory_space=pl.ANY if number in places else pltpu.VMEM)

        def run(*operands):
            count, last = len(operands), self.last

            def without_last(*refs):
                kernel(*refs[:count], *refs[count + len(last) :])

            operands = [
                pltpu.with_memory_space_constraint(operand, pltpu.HBM)
                if number in anywhere and not aliases
                else operand
                for number, operand in enumerate(operands)
            ]
            results = pl.pallas_call(
                without_last,
                name=name,
                out_shape=[
                    pltpu.HBM(shape, dtype)
                    if number in out_anywhere
                    else jax.ShapeDtypeStruct(shape, dtype)
                    for number, (shape, dtype) in enumerate(outs)
                ],
                in_specs=[spec(number, anywhere) for number in range(count)]
                + [pl.BlockSpec(memory_space=pl.ANY)] * len(last),
                out_specs=[spec(number, out_anywhere) for number in range(len(outs))],
                scratch_shapes=list(scratch),
                input_output_aliases=aliases or {},
                compiler_params=pltpu.CompilerParams(vmem_limit_bytes=vmem),
                cost_estimate=pl.CostEstimate(
                    flops=1 + int(microseconds * 1_150_000_000), bytes_accessed=1 + int(microseconds * BYTES_MICROSECOND), transcendentals=0
                ),
            )(*operands, *last)
            self.last = (results[token],)
            return results

        return run

    def combine(self, name, inputs, outs, microseconds=EACH):
        width = inputs[0].shape[1]

        def kernel(*refs):
            sources, targets = refs[: len(inputs)], refs[len(inputs) :]
            for target, pieces in zip(targets, outs):
                offset = 0
                for number, start, rows, *other in pieces:
                    part = sources[number][start : start + rows, :]
                    if other:
                        added = sources[other[0]][other[1] : other[1] + rows, :]
                        part = (part.astype(F32) + added.astype(F32)).astype(BF16)
                    target[offset : offset + rows, :] = part
                    offset += rows

        shapes = [((sum(piece[2] for piece in pieces), width), BF16) for pieces in outs]
        return self.call(kernel, name, shapes, microseconds=microseconds)(*inputs)


def own_places(plan):
    seq = lax.axis_index("seq")
    return seq, lax.axis_index("rows") * plan.seq_block + lax.rem(seq, plan.seq_block)


def read_segments(order, segments, batch):
    length = order.shape[0]
    rows = [segments[b].astype(F32) for b in range(batch)]
    rows = jnp.concatenate(rows + [jnp.zeros((EXTRA_ROWS - batch, length), F32)], axis=0)
    columns = dot_nt(order, rows.astype(BF16))
    return rows, [columns[:, b : b + 1] for b in range(batch)]


def project_kernel(
    tokens_far, gain_far, segments_far, w_query, w_key, w_value, conv_key, conv_value,
    x_out, normed_out, query_out, key_out, value_out, segment_out, packed_key, packed_value,
    conv_key_here, conv_value_here, query_here, key_here, value_here, tokens, gain, segments,
    arrived,
):
    ready = fetch_all(
        [
            (tokens_far, tokens), (segments_far, segments), (gain_far, gain), (w_key, key_here), (conv_key, conv_key_here), (w_value, value_here),
            (conv_value, conv_value_here), (w_query, query_here),
        ],
        arrived,
    )
    batch, _, length, width = tokens.shape
    slots = length // 3
    order = order_matrix(length, False)
    for number in range(3):
        ready(number)
    rows = [dot(order, tokens[b, 0]) for b in range(batch)]
    segment_rows, segment_columns = read_segments(order, segments, batch)
    x = jnp.concatenate(rows, axis=0)
    x_out[...] = x
    for b in range(batch):
        segment_out[b] = segment_columns[b]
    last = lax.broadcasted_iota(jnp.int32, (length, width), 0)
    slot = lax.broadcasted_iota(jnp.int32, (length, width), 1)
    extra = dot(segment_rows.astype(BF16), (last == 3 * slot + 2).astype(BF16)).astype(BF16)
    unit, _ = normalize(x)
    normed = (unit * gain[...].astype(F32).reshape(1, width)).astype(BF16)

    normed_out[...] = normed
    for number, flat_out, packed_out in ((3, key_out, packed_key), (5, value_out, packed_value)):
        flat = dot(normed, ready(number)[...]).astype(BF16)
        flat_out[...] = flat
        taps = [[], [], []]
        for b in range(batch):
            masks = window_masks(segment_columns[b], slots)
            for i in range(3):
                start = b * length + i * slots
                part = flat[start : start + slots].astype(F32) * masks[i]
                taps[i].append(part.astype(BF16))
        conv = ready(number + 1)
        total = None
        for i in range(3):
            term = dot(jnp.concatenate(taps[i], axis=0), conv[i * width : (i + 1) * width, :])
            total = term if total is None else total + term
        packed_out[0 : batch * slots, :] = total.astype(BF16)
    packed_key[batch * slots :, :] = extra
    query_out[...] = dot(normed, ready(7)[...]).astype(BF16)


def layer_kernel(
    plan, short, down_order, up_order,
    x_in, normed_in, cotangent, query_in, key_in, value_in, segment_column, gain_ffn,
    keys_near, keys_far, values_near, values_far, w_out, w_up, w_down,
    layer_out, d_hidden_out, d_query_out, d_key_own, d_value_own,
    d_key_keep, d_key_send, d_value_keep, d_value_send,
    down_send, down_keep, up_send, up_keep, gain_grad,
    all_keys, all_values, all_extra, bias, statistics, prob_keep, expanded_sum, d_normed_sum,
    d_attended, normed_ffn_out, activated_out, d_expanded_out, cotangent_out, attended_out,
    d_branch_out, down_rows, up_rows, out_rows, query_rows, *copied,
):
    batch, _, length, width = cotangent.shape
    slots = length // 3
    n_seq = plan.n_seq
    half = n_seq // 2
    total_slots = slots * n_seq
    own_place = lax.axis_index("seq")
    key_position = {plan.seq_relative(plan.key_order, p): p for p in range(n_seq)}
    packed_rows = batch * slots
    payload = packed_rows + EXTRA_ROWS
    copies = []

    def put(source, start, rows, target, lanes=slice(None)):
        if short:
            target[...] = source[start : start + rows, lanes]
            return
        copies.append(
            pltpu.make_async_copy(
                source.at[pl.ds(start, rows), lanes], target, copied[0].at[len(copies)]
            )
        )
        copies[-1].start()

    for p in range(n_seq):
        keys, values = (keys_near, values_near) if p < half else (keys_far, values_far)
        place = p % half
        q = key_position[plan.seq_relative(plan.value_order, p)]
        put(
            keys, place * payload + packed_rows, EXTRA_ROWS, all_extra.at[p], slice(0, LANES)
        )
        for b in range(batch):
            put(
                keys, place * payload + b * slots, slots,
                all_keys.at[b, pl.ds(p * slots, slots), :],
            )
            put(
                values, place * packed_rows + b * slots, slots,
                all_values.at[b, pl.ds(q * slots, slots), :],
            )
    for copy in copies:
        copy.wait()

    segment_rows = jnp.zeros((EXTRA_ROWS, total_slots), F32)
    slot_lane = lax.broadcasted_iota(jnp.int32, (1, total_slots), 1)
    slot_end = jnp.zeros((1, total_slots), jnp.int32)
    select_row = lax.broadcasted_iota(jnp.int32, (LANES, total_slots), 0)
    select_lane = lax.broadcasted_iota(jnp.int32, (LANES, total_slots), 1)
    for p in range(n_seq):
        selected = (select_lane == select_row + p * slots) & (select_row < slots)
        segment_rows += dot(all_extra[p], selected.astype(BF16))
        owner = plan.seq_relative(plan.key_order, p) ^ own_place
        here = (slot_lane >= p * slots) & (slot_lane < (p + 1) * slots)
        slot_end = jnp.where(here, length * owner - length * p + 3 * slot_lane + 2, slot_end)
    row = lax.broadcasted_iota(jnp.int32, (length, 1), 0)
    tap = (row >= slots).astype(jnp.int32) + (row >= 2 * slots).astype(jnp.int32)
    query_place = length * own_place + 3 * (row - tap * slots) + tap
    causal = slot_end <= query_place
    for b in range(batch):
        matching = segment_rows[b : b + 1, :] == segment_column[b]
        bias[b] = jnp.where(causal & matching, 0.0, MASKED_OUT)

    low_lane = lax.broadcasted_iota(jnp.int32, (length, LANES), 1) < HEAD_DIM

    def stacked(part):
        zero = jnp.zeros_like(part)
        return jnp.concatenate(
            [jnp.where(low_lane, part, zero), jnp.where(low_lane, zero, part)], axis=0
        )

    def twice(part):
        return jnp.concatenate([part, part], axis=0)

    def merged(part):
        return jnp.where(low_lane, part[:length], part[length:])

    def lanes_of(g):
        return pl.ds(pl.multiple_of(g * LANES, LANES), LANES)

    def place_of(number):
        b, g = number // GROUPS, number % GROUPS
        if short:
            return b, slice(b * length, (b + 1) * length), slice(g * LANES, (g + 1) * LANES)
        return b, pl.ds(pl.multiple_of(b * length, 16), length), lanes_of(g)

    def each(step):
        if short:
            for number in range(batch * GROUPS):
                step(number)
        else:
            lax.fori_loop(0, batch * GROUPS, lambda number, carry: (step(number), carry)[1], 0)

    def scaled_queries(rows, lanes):
        part = query_in[rows, lanes].astype(F32) * SCALE
        return stacked(part).astype(BF16)

    def attend(number):
        b, rows, lanes = place_of(number)
        queries = scaled_queries(rows, lanes)
        own_key = twice(key_in[rows, lanes].astype(F32))
        scores = dot_nt(queries, all_keys[b, :, lanes]) + twice(bias[b])
        own_score = jnp.sum(queries.astype(F32) * own_key, axis=-1, keepdims=True)
        top = jnp.maximum(own_score, jnp.max(scores, axis=-1, keepdims=True))
        raised = jnp.exp(scores - top)
        own_raised = jnp.exp(own_score - top)
        inverse = 1.0 / (own_raised + jnp.sum(raised, axis=-1, keepdims=True))
        prob = raised * inverse
        own_prob = own_raised * inverse
        if short:
            prob_keep[number] = prob
        statistics[number, :, 0:1] = own_prob
        statistics[number, :, 1:2] = top - jnp.log(inverse)
        result = dot(prob.astype(BF16), all_values[b, :, lanes])
        own_value = twice(value_in[rows, lanes].astype(F32))
        result += own_prob.astype(BF16).astype(F32) * own_value
        attended_out[rows, lanes] = merged(result).astype(BF16)

    each(attend)

    x = x_in[...]
    hidden = x + dot(attended_out[...], w_out[...])
    unit, inverse_dev = normalize(hidden)
    gain = gain_ffn[...].astype(F32).reshape(1, width)
    normed_ffn_out[...] = (unit * gain).astype(BF16)
    order = order_matrix(length, False)
    for b in range(batch):
        cotangent_out[b * length : (b + 1) * length, :] = dot(order, cotangent[b, 0]).astype(BF16)
    expanded_sum[...] = hidden
    d_normed_sum[...] = jnp.zeros_like(d_normed_sum)
    chunk = width
    total_width = w_up.shape[1]

    def feed(number, carry):
        columns = pl.ds(pl.multiple_of(number * chunk, chunk), chunk)
        expanded = dot(normed_ffn_out[...], w_up[:, columns])
        square = expanded * expanded
        curve = jnp.tanh(GELU_SCALE * expanded * (1.0 + GELU_CUBIC * square))
        activated = (0.5 * expanded * (1.0 + curve)).astype(BF16)
        activated_out[:, columns] = activated
        slope = 0.5 * (1.0 + curve) + 0.5 * expanded * (1.0 - curve * curve) * (
            GELU_SCALE * (1.0 + 3.0 * GELU_CUBIC * square)
        )
        expanded_sum[...] += dot(activated, w_down[columns, :])
        d_activated = dot_nt(cotangent_out[...], w_down[columns, :])
        d_expanded = (d_activated * slope).astype(BF16)
        d_expanded_out[:, columns] = d_expanded
        d_normed_sum[...] += dot_nt(d_expanded, w_up[:, columns])
        return carry

    lax.fori_loop(0, total_width // chunk, feed, 0, unroll=short)

    unorder = order_matrix(length, True)
    for b in range(batch):
        part = expanded_sum[b * length : (b + 1) * length, :].astype(BF16)
        layer_out[b, 0] = dot(unorder, part).astype(BF16)
    d_normed = d_normed_sum[...]
    gain_grad[...] = jnp.sum(d_normed * unit, axis=0, keepdims=True)
    d_hidden = cotangent_out[...].astype(F32) + normalize_back(d_normed, unit, inverse_dev, gain)
    d_hidden_out[...] = d_hidden
    d_branch = d_hidden.astype(BF16)
    d_branch_out[...] = d_branch
    d_attended[...] = dot_nt(d_branch, w_out[...]).astype(BF16)

    value_spot = [key_position[plan.seq_relative(plan.value_order, p)] for p in range(n_seq)]

    def attend_back(number):
        b, rows, lanes = place_of(number)
        queries = scaled_queries(rows, lanes)
        own_prob = statistics[number, :, 0:1]
        if short:
            prob = prob_keep[number]
        else:
            scores = dot_nt(queries, all_keys[b, :, lanes]) + twice(bias[b])
            prob = jnp.exp(scores - statistics[number, :, 1:2])
        grads = stacked(d_attended[rows, lanes])
        own_value = twice(value_in[rows, lanes].astype(F32))
        own_key = twice(key_in[rows, lanes].astype(F32))
        prob_grad = dot_nt(grads, all_values[b, :, lanes])
        own_prob_grad = jnp.sum(grads.astype(F32) * own_value, axis=-1, keepdims=True)
        delta = own_prob * own_prob_grad + jnp.sum(prob * prob_grad, axis=-1, keepdims=True)
        d_score = (prob * (prob_grad - delta)).astype(BF16)
        d_own = (own_prob * (own_prob_grad - delta)).astype(BF16).astype(F32)
        own_low = own_prob.astype(BF16).astype(F32)
        d_query = merged(dot(d_score, all_keys[b, :, lanes]) + d_own * own_key) * SCALE
        d_query_out[rows, lanes] = d_query.astype(BF16)
        d_key_own[rows, lanes] = merged(d_own * queries.astype(F32))
        d_value_own[rows, lanes] = merged(own_low * grads.astype(F32))
        key_sums = dot_tn(d_score, queries).astype(BF16)
        value_sums = dot_tn(prob.astype(BF16), grads).astype(BF16)
        for p in range(n_seq):
            spot = pl.ds(p % half * packed_rows + b * slots, slots)
            key_target, value_target = (
                (d_key_keep, d_value_keep) if p < half else (d_key_send, d_value_send)
            )
            key_target[spot, lanes] = key_sums[p * slots : (p + 1) * slots]
            q = value_spot[p]
            value_target[spot, lanes] = value_sums[q * slots : (q + 1) * slots]

    def weight_piece(number):
        c = number // 2
        columns = slice(c * chunk, (c + 1) * chunk)
        if c == total_width // chunk:
            out_rows[...] = dot_tn(attended_out[...], d_branch_out[...]).astype(BF16)
        elif number % 2 == 0:
            product = dot_tn(activated_out[:, columns], cotangent_out[...])
            down_rows[columns, :] = product.astype(BF16)
        else:
            up_rows[c] = dot_tn(normed_ffn_out[...], d_expanded_out[:, columns]).astype(BF16)

    pieces = list(range(2 * (total_width // chunk) + 1))

    def attend_back_and_weigh(number):
        attend_back(number)
        if short and pieces:
            weight_piece(pieces.pop(0))

    each(attend_back_and_weigh)
    while pieces:
        weight_piece(pieces.pop(0))
    query_rows[...] = dot_tn(normed_in[...], d_query_out[...]).astype(BF16)
    _, mine = own_places(plan)
    thin = width // plan.blocks
    parts = ((down_rows, total_width // plan.blocks), (out_rows, thin))
    spread(plan, mine, down_order, parts, down_send, down_keep)
    parts = tuple((up_rows.at[c], thin) for c in range(total_width // chunk))
    spread(plan, mine, up_order, parts + ((query_rows, thin),), up_send, up_keep)


def spread(plan, place, order, parts, send, keep):
    half = plan.blocks // 2
    for target, core in ((send, 1), (keep, 0)):
        start = 0
        for p in range(half):
            block = plan.relative(order, core * half + p) ^ place
            for source, rows in parts:
                target[start : start + rows, :] = source[
                    pl.ds(pl.multiple_of(block * rows, 16), rows), :
                ]
                start += rows


def conv_grad_kernel(
    plan, order, segment_column, d_packed, flat, own, conv, send, keep, d_flat_out, conv_rows
):
    batch, length, _ = segment_column.shape
    width = conv.shape[1]
    slots = length // 3
    masks = [window_masks(segment_column[b], slots) for b in range(batch)]
    back = d_packed[...]
    for i in range(3):
        taps = []
        for b in range(batch):
            start = b * length + i * slots
            part = flat[start : start + slots, :].astype(F32) * masks[b][i]
            taps.append(part.astype(BF16))
        window = jnp.concatenate(taps, axis=0)
        conv_rows[i * width : (i + 1) * width, :] = dot_tn(window, back).astype(BF16)
    _, mine = own_places(plan)
    spread(plan, mine, order, ((conv_rows, 3 * width // plan.blocks),), send, keep)
    for i in range(3):
        from_tap = dot_nt(back, conv[i * width : (i + 1) * width, :])
        for b in range(batch):
            start = b * length + i * slots
            part = from_tap[b * slots : (b + 1) * slots] * masks[b][i]
            d_flat_out[start : start + slots, :] = (part + own[start : start + slots, :]).astype(BF16)


def tail_kernel(
    plan, order, normed, x_in, gain, d_query, d_keys, d_values, d_hidden, gain_ffn_grad,
    w_query, w_key, w_value,
    send, keep, grad_tokens, key_rows, value_rows,
):
    batch, _, length, width = grad_tokens.shape
    key_rows[...] = dot_tn(normed[...], d_keys[...]).astype(BF16)
    value_rows[...] = dot_tn(normed[...], d_values[...]).astype(BF16)
    _, mine = own_places(plan)
    thin = width // plan.blocks
    spread(plan, mine, order, ((key_rows, thin), (value_rows, thin)), send, keep)
    d_normed = (
        dot_nt(d_query[...], w_query[...])
        + dot_nt(d_keys[...], w_key[...])
        + dot_nt(d_values[...], w_value[...])
    )
    unit, inverse_dev = normalize(x_in[...])
    gain_grad = jnp.sum(d_normed * unit, axis=0, keepdims=True)
    d_input = normalize_back(d_normed, unit, inverse_dev, gain[...].astype(F32).reshape(1, width))
    result = (d_hidden[...] + d_input).astype(BF16)
    unorder = order_matrix(length, True)
    for b in range(batch):
        part = result[b * length : (b + 1) * length, :]
        grad_tokens[b, 0] = dot(unorder, part).astype(BF16)
    row = lax.broadcasted_iota(jnp.int32, (EXTRA_ROWS, width), 0)
    gains = jnp.where(row == 0, gain_grad, jnp.where(row == 1, gain_ffn_grad[...], 0.0))
    send[send.shape[0] - EXTRA_ROWS :, :] = gains.astype(BF16)
    keep[keep.shape[0] - EXTRA_ROWS :, :] = gains.astype(BF16)


def finish_kernel(plan, items, count, aliased, *refs):
    blocks, refs = refs[: len(items)], refs[len(items) + (count if aliased else 0) :]
    targets, (token, sent, *stages) = refs[:count], refs[count:]
    token[...] = jnp.zeros_like(token)
    _, mine = own_places(plan)
    half = plan.blocks // 2
    copies = []
    for source, stage, (layout, parts, core) in zip(blocks, stages, items):
        start = 0
        for p in range(half):
            block = plan.relative(layout, core * half + p) ^ mine
            for rows, target, columns in parts:
                stage[start : start + rows, :] = source[start : start + rows, :].astype(F32)
                spot = pl.ds(pl.multiple_of(block * rows, 16), rows)
                copy = pltpu.make_async_copy(
                    stage.at[pl.ds(start, rows), :],
                    targets[target].at[spot, columns],
                    sent.at[len(copies)],
                )
                copy.start()
                copies.append(copy)
                start += rows
    for copy in copies:
        copy.wait()


def finish(plan, order, name, chosen, cores, targets=()):
    items, blocks, shapes = [], [], []
    for part in chosen:
        for core in cores:
            parts = [(rows, len(shapes) + target, columns) for rows, target, columns in part.parts]
            items.append((part.bits, parts, core))
            blocks.append(part.far if core else part.held)
        shapes += part.shapes
    count = len(shapes)
    everywhere = tuple(range(count))
    copies = sum(plan.blocks // 2 * len(parts) for _, parts, _ in items)
    return order.call(
        functools.partial(finish_kernel, plan, items, count, bool(targets)),
        name,
        [(shape, F32) for shape in shapes] + [((8, LANES), F32)],
        [pltpu.SemaphoreType.DMA((copies,))] + [pltpu.VMEM(array.shape, F32) for array in blocks],
        anywhere=tuple(range(len(items), len(items) + count)) if targets else (),
        out_anywhere=everywhere,
        aliases={len(items) + number: number for number in everywhere} if targets else None,
        token=count,
    )(*blocks, *targets)[:count]


class RowGather:
    def __init__(self, name, plan, order, array, bits):
        self.name, self.plan, self.order = name, plan, order
        self.held, self.bits = array, list(bits)

    def step(self):
        arrived = self.plan.swap(self.held, ("seq", self.bits.pop(0)), self.name)
        if not self.bits:
            return [self.held, arrived]
        rows = self.held.shape[0]
        self.held, = self.order.combine(
            "gather_row", [self.held, arrived], [[(0, 0, rows), (1, 0, rows)]]
        )


class RowScatter:
    def __init__(self, name, plan, order, keep, send, bits):
        self.name, self.plan, self.order, self.keep, self.send = name, plan, order, keep, send
        self.bits = list(bits)

    def step(self, microseconds=EACH):
        if not self.bits:
            return
        arrived = self.plan.swap(self.send, ("seq", self.bits.pop()), self.name)
        rows = self.keep.shape[0]
        half = rows // 2
        outs = [(0, rows)] if not self.bits else [(0, half), (half, half)]
        self.keep, *send = self.order.combine(
            "scatter_row", [self.keep, arrived],
            [[(0, start, size, 1, start)] for start, size in outs], microseconds,
        )
        self.send = send[0] if send else None


class Part:
    def __init__(self, name, plan, order, bits, send, keep, shapes, parts, extra=0):
        self.name, self.plan, self.order, self.bits, self.extra = name, plan, order, bits, extra
        self.send, self.keep = send, keep
        self.shapes, self.parts = shapes, parts
        self.done = 0

    def step(self, microseconds):
        if self.done < len(self.bits):
            self.scatter(self.bits[self.done], microseconds)
        else:
            self.gather(self.bits[2 * len(self.bits) - 1 - self.done], microseconds)
        self.done += 1

    def scatter(self, bit, microseconds):
        arrived = self.plan.swap(self.send, bit, self.name)
        extra = self.extra
        rows = self.keep.shape[0] - extra
        last = [(0, rows, extra, 1, rows)]
        if self.done < len(self.bits) - 1:
            half = rows // 2
            outs = [[(0, start, half, 1, start)] + (last if extra else []) for start in (0, half)]
            self.keep, self.send = self.order.combine(
                "scatter", [self.keep, arrived], outs, microseconds
            )
            return
        outs = [[(0, 0, rows, 1, 0)]] + ([last] if extra else [])
        self.held, *self.sums = self.order.combine(
            "scatter", [self.keep, arrived], outs, microseconds
        )
        for bit in self.plan.rest:
            arrays = [self.held] + self.sums
            arrived = [self.plan.swap(array, bit, self.name) for array in arrays]
            self.held, *self.sums = self.order.combine(
                "scatter_rest", arrays + arrived,
                [
                    [(i, 0, array.shape[0], i + len(arrays), 0)]
                    for i, array in enumerate(arrays)
                ],
            )

    def gather(self, bit, microseconds=EACH):
        arrived = self.plan.swap(self.held, bit, self.name)
        rows = self.held.shape[0]
        self.held, = self.order.combine(
            "gather", [self.held, arrived], [[(0, 0, rows), (1, 0, rows)]], microseconds
        )
        if self.done == 2 * len(self.bits) - 2:
            self.far = self.plan.swap(self.held, self.plan.core, self.name)


def body(
    plan, tokens, segments, cotangent, gain_attn, w_query, w_key, w_value, conv_key, conv_value,
    w_out, gain_ffn, w_up, w_down,
):
    batch, _, length, width = tokens.shape
    slots = length // 3
    square = (width, width)
    positions = batch * length
    flat, flat32 = ((positions, width), BF16), ((positions, width), F32)
    square_here = pltpu.VMEM(square, BF16)
    conv_here = pltpu.VMEM(conv_key.shape, BF16)
    order = Order()
    later = [conv_key, conv_value, w_query, w_key, w_value]
    short = slots * plan.n_seq <= SHORT_ROW
    (
        x, normed, queries, key_rows, value_rows, segment_column, packed_key, packed_value, *here,
    ) = order.call(
        project_kernel,
        "project",
        [flat32] + [flat] * 4 + [((batch, length, 1), F32)]
        + [((batch * slots + EXTRA_ROWS, width), BF16), ((batch * slots, width), BF16)]
        + ([(array.shape, BF16) for array in later] if short else []),
        scratch=([] if short else [conv_here] * 2 + [square_here] * 3)
        + [
            pltpu.VMEM(tokens.shape, BF16), pltpu.VMEM(gain_attn.shape, BF16),
            pltpu.VMEM(segments.shape, jnp.int32), pltpu.SemaphoreType.DMA((8,)),
        ],
        anywhere=tuple(range(8)),
        token=5,
    )(tokens, gain_attn, segments, w_query, w_key, w_value, conv_key, conv_value)

    later = here or later
    steps = len(plan.key_order)
    keys = RowGather("gather_keys", plan, order, packed_key, plan.key_order)
    values = RowGather("gather_values", plan, order, packed_value, plan.value_order)
    for number in range(steps - 1):
        keys.step()
        values.step()

    core = [plan.core]
    x_first, y_first = core + plan.first + plan.tail, core + plan.second + plan.tail
    z_first = core + plan.tail[:1] + plan.first + plan.tail[1:]
    bits = {"A0": y_first, "A1": x_first, "B0": y_first, "B1": x_first, "B2": z_first}
    half = plan.blocks // 2
    thin, down_block, conv_block = (
        rows // plan.blocks for rows in (width, w_down.shape[0], conv_key.shape[0])
    )
    chunks = w_up.shape[1] // width
    everything = slice(None)
    ups = [(thin, 0, slice(c * width, (c + 1) * width)) for c in range(chunks)]
    layouts = {
        "A0": ([w_down.shape, square], [(down_block, 0, everything), (thin, 1, everything)]),
        "A1": ([w_up.shape, square], ups + [(thin, 1, everything)]),
        "B0": ([conv_key.shape], [(conv_block, 0, everything)]),
        "B1": ([conv_value.shape], [(conv_block, 0, everything)]),
        "B2": ([square, square], [(thin, 0, everything), (thin, 1, everything)]),
    }

    def half_rows(name):
        return half * sum(part[0] for part in layouts[name][1])

    total_slots = slots * plan.n_seq
    half_packed = ((batch * total_slots // 2, width), BF16)
    halves = [((half_rows(name), width), BF16) for name in ("A0", "A0", "A1", "A1")]
    flat_here = pltpu.VMEM((positions, width), BF16)
    wide_here = pltpu.VMEM((positions, w_up.shape[1]), BF16)
    copied = [] if short else [pltpu.SemaphoreType.DMA((plan.n_seq * (1 + 2 * batch),))]
    layer_out, d_hidden, d_query, d_key_own, d_value_own, *outs, gain_ffn_grad = order.call(
        functools.partial(layer_kernel, plan, short, bits["A0"], bits["A1"]),
        "layer",
        [(tokens.shape, BF16), flat32, flat, flat32, flat32] + [half_packed] * 4 + halves
        + [((1, width), F32)],
        scratch=[
            pltpu.VMEM((batch, total_slots, width), BF16),
            pltpu.VMEM((batch, total_slots, width), BF16),
            pltpu.VMEM((plan.n_seq, EXTRA_ROWS, LANES), BF16),
            pltpu.VMEM((batch, length, total_slots), F32),
            pltpu.VMEM((batch * GROUPS, 2 * length, LANES), F32),
            pltpu.VMEM((batch * GROUPS, 2 * length, total_slots) if short else (1, 8, LANES), F32),
            pltpu.VMEM((positions, width), F32),
            pltpu.VMEM((positions, width), F32),
            flat_here, flat_here, wide_here, wide_here, flat_here, flat_here, flat_here,
            pltpu.VMEM(w_down.shape, BF16),
            pltpu.VMEM((chunks, width, width), BF16),
            square_here, square_here,
        ]
        + copied,
        anywhere=() if short else (8, 9, 10, 11),
        vmem=VMEM_SMALL if short else VMEM_LARGE,
        token=-1,
    )(
        x, normed, cotangent, queries, key_rows, value_rows, segment_column, gain_ffn,
        *keys.step(), *values.step(), w_out, w_up, w_down,
    )
    rows = [
        RowScatter("K", plan, order, outs[0], outs[1], plan.key_order),
        RowScatter("V", plan, order, outs[2], outs[3], plan.value_order),
    ]
    chains, d_flats = {"K": rows[0], "V": rows[1]}, {}
    for name, (send, keep) in (("A0", outs[4:6]), ("A1", outs[6:8])):
        chains[name] = Part(name, plan, order, bits[name], send, keep, *layouts[name])

    def make(name, kernel, outs, scratch, operands, extra=0):
        total = half_rows(name) + extra
        send, keep, *others = order.call(
            functools.partial(kernel, plan, bits[name]),
            kernel.__name__,
            [((total, width), BF16)] * 2 + outs,
            scratch=scratch,
        )(*operands)
        chains[name] = Part(name, plan, order, bits[name], send, keep, *layouts[name], extra)
        return others

    for event in EVENTS:
        if event in ("TK", "TV"):
            number = 0 if event == "TK" else 1
            row = rows[number]
            while row.bits:
                row.step()
            d_flat, = make(
                f"B{number}", conv_grad_kernel, [flat], [conv_here],
                (
                    segment_column, row.keep, (key_rows, value_rows)[number],
                    (d_key_own, d_value_own)[number], later[number],
                ),
            )
            d_flats[event] = d_flat
        elif event == "T3":
            grad_tokens, = make(
                "B2", tail_kernel, [(tokens.shape, BF16)], [square_here, square_here],
                (
                    normed, x, gain_attn, d_query, d_flats["TK"], d_flats["TV"], d_hidden,
                    gain_ffn_grad, *later[2:],
                ),
                EXTRA_ROWS,
            )
        elif event == "Af":
            grads = finish(plan, order, "finish", [chains["A0"], chains["A1"]], (0, 1))
            grad_down, grad_out, grad_up, grad_query = grads
        elif event in ("Bn", "Bf"):
            chosen = [chains[name] for name in ("B0", "B1", "B2")]
            previous = () if event == "Bn" else results
            results = finish(plan, order, "finish", chosen, (int(event == "Bf"),), previous)
        else:
            name, _, cost = event.partition(":")
            chains[name].step(float(cost or EACH))
    grad_conv_key, grad_conv_value, grad_key, grad_value = results
    gains = chains["B2"].sums[0].astype(F32)
    return (
        layer_out, grad_tokens, gains[0], grad_query, grad_key, grad_value,
        grad_conv_key, grad_conv_value, grad_out, gains[1], grad_up, grad_down,
    )


def solution(mesh):
    packed = P(None, "rows", "seq", None)
    in_specs = (packed, P(None, "rows", "seq"), packed) + (P(),) * 10
    out_specs = (packed, packed) + (P(),) * 10
    return jax.shard_map(
        functools.partial(body, Plan(mesh)),
        mesh=mesh, in_specs=in_specs, out_specs=out_specs, check_vma=False,
    )
```

```python
import functools

import jax
import jax.numpy as jnp
from jax import lax
from jax.experimental import pallas as pl
from jax.experimental.pallas import tpu as pltpu
from jax.sharding import PartitionSpec as P

HEADS = 8
HEAD_DIM = 64
LANES = 128
GROUPS = HEADS * HEAD_DIM // LANES
EPSILON = 1e-05
MASKED_OUT = -1e30
SCALE = HEAD_DIM ** (-0.5)
GELU_SCALE = 0.7978845608028654
GELU_CUBIC = 0.044715
SCATTER_BITS = 5
EXTRA_ROWS = 16
VMEM_SMALL = 28 * 1024 * 1024
VMEM_LARGE = 62 * 1024 * 1024
SHORT_ROW = 768
BYTES_MICROSECOND = 3_690_000
EACH = 5

EVENTS = (
    "A0", "A1", "K", "V", "V:0", "K:0", "A1:0", "A0", "K", "V", "TK", "TV", "T3", "B0", "B1",
    "A0", "A1", "B2", "A0", "A1", "B1", "B0", "B2", "A1", "A0", "A1", "B1", "B2", "A0", "A1",
    "B0", "B2", "B1", "A0", "A1", "B0", "B2", "B1", "A0", "B0", "B2", "B1", "B0", "A1", "B2",
    "B1", "B0", "A0", "B2", "B0", "B1", "B2", "Af", "B0", "B1", "Bn", "Bf",
)

BF16 = jnp.bfloat16
F32 = jnp.float32


def dot(left, right):
    return jnp.dot(left, right, preferred_element_type=F32)


def dot_nt(left, right):
    return lax.dot_general(left, right, (((1,), (1,)), ((), ())), preferred_element_type=F32)


def dot_tn(left, right):
    return lax.dot_general(left, right, (((0,), (0,)), ((), ())), preferred_element_type=F32)


def normalize(values):
    average = jnp.mean(values, axis=-1, keepdims=True)
    centred = values - average
    variance = jnp.mean(centred * centred, axis=-1, keepdims=True)
    inverse_dev = lax.rsqrt(variance + EPSILON)
    return centred * inverse_dev, inverse_dev


def normalize_back(grad_normed, unit, inverse_dev, gain):
    grad_unit = grad_normed * gain
    first_mean = jnp.mean(grad_unit, axis=-1, keepdims=True)
    second_mean = jnp.mean(grad_unit * unit, axis=-1, keepdims=True)
    return inverse_dev * (grad_unit - first_mean - unit * second_mean)


class Plan:
    def __init__(self, mesh):
        self.n_rows = mesh.shape["rows"]
        self.n_seq = mesh.shape["seq"]
        rows = [("rows", 1 << i) for i in range(self.n_rows.bit_length() - 1)]
        seq = [("seq", 1 << i) for i in range(self.n_seq.bit_length() - 1)]
        kept = max(0, min(len(seq), SCATTER_BITS - len(rows)))
        self.seq_block = 1 << kept
        self.blocks = self.n_rows * self.seq_block
        core, others = rows[:1], rows[1:]
        low, high = seq[:1], seq[1:kept] if kept else []
        low = low[:kept]
        self.core = core[0]
        self.first = others + low
        self.second = low + others
        self.tail = high
        self.rest = seq[kept:]
        bits = [1 << i for i in range(len(seq))]
        self.key_order = bits[::-1]
        self.value_order = bits[:1] + bits[:0:-1]

    def mask(self, bit):
        axis, value = bit
        return value * self.seq_block if axis == "rows" else value

    def relative(self, order, position):
        result = 0
        for number, bit in enumerate(order):
            if position >> (len(order) - 1 - number) & 1:
                result |= self.mask(bit)
        return result

    def seq_relative(self, order, position):
        result = 0
        for number, bit in enumerate(order):
            if position >> number & 1:
                result |= bit
        return result

    def swap(self, array, bit, name):
        axis, value = bit
        size = self.n_rows if axis == "rows" else self.n_seq
        with jax.named_scope(f"swap_{name}"):
            return lax.ppermute(array, axis, [(i, i ^ value) for i in range(size)])


def order_matrix(length, transposed):
    slots = length // 3
    rows = lax.broadcasted_iota(jnp.int32, (length, length), 1 if transposed else 0)
    columns = lax.broadcasted_iota(jnp.int32, (length, length), 0 if transposed else 1)
    tap = (rows >= slots).astype(jnp.int32) + (rows >= 2 * slots).astype(jnp.int32)
    return (columns == 3 * (rows - tap * slots) + tap).astype(BF16)


def window_masks(segment_column, slots):
    last = segment_column[2 * slots :]
    return [(segment_column[i * slots : (i + 1) * slots] == last).astype(F32) for i in range(3)]


def fetch_all(pairs, arrived):
    copies = [
        pltpu.make_async_copy(source, target, arrived.at[number])
        for number, (source, target) in enumerate(pairs)
    ]
    for copy in copies:
        copy.start()

    def ready(number):
        copies[number].wait()
        return pairs[number][1]

    return ready


class Order:
    def __init__(self):
        self.last = ()

    def call(
        self, kernel, name, outs, scratch=(), anywhere=(), out_anywhere=(), aliases=None,
        vmem=VMEM_SMALL, microseconds=EACH, token=0,
    ):
        def spec(number, places):
            return pl.BlockSpec(memory_space=pl.ANY if number in places else pltpu.VMEM)

        def run(*operands):
            count, last = len(operands), self.last

            def without_last(*refs):
                kernel(*refs[:count], *refs[count + len(last) :])

            operands = [
                pltpu.with_memory_space_constraint(operand, pltpu.HBM)
                if number in anywhere and not aliases
                else operand
                for number, operand in enumerate(operands)
            ]
            results = pl.pallas_call(
                without_last,
                name=name,
                out_shape=[
                    pltpu.HBM(shape, dtype)
                    if number in out_anywhere
                    else jax.ShapeDtypeStruct(shape, dtype)
                    for number, (shape, dtype) in enumerate(outs)
                ],
                in_specs=[spec(number, anywhere) for number in range(count)]
                + [pl.BlockSpec(memory_space=pl.ANY)] * len(last),
                out_specs=[spec(number, out_anywhere) for number in range(len(outs))],
                scratch_shapes=list(scratch),
                input_output_aliases=aliases or {},
                compiler_params=pltpu.CompilerParams(vmem_limit_bytes=vmem),
                cost_estimate=pl.CostEstimate(
                    flops=1 + int(microseconds * 1_150_000_000), bytes_accessed=1 + int(microseconds * BYTES_MICROSECOND), transcendentals=0
                ),
            )(*operands, *last)
            self.last = (results[token],)
            return results

        return run

    def combine(self, name, inputs, outs, microseconds=EACH):
        width = inputs[0].shape[1]

        def kernel(*refs):
            sources, targets = refs[: len(inputs)], refs[len(inputs) :]
            for target, pieces in zip(targets, outs):
                offset = 0
                for number, start, rows, *other in pieces:
                    part = sources[number][start : start + rows, :]
                    if other:
                        added = sources[other[0]][other[1] : other[1] + rows, :]
                        part = (part.astype(F32) + added.astype(F32)).astype(BF16)
                    target[offset : offset + rows, :] = part
                    offset += rows

        shapes = [((sum(piece[2] for piece in pieces), width), BF16) for pieces in outs]
        return self.call(kernel, name, shapes, microseconds=microseconds)(*inputs)


def own_places(plan):
    seq = lax.axis_index("seq")
    return seq, lax.axis_index("rows") * plan.seq_block + lax.rem(seq, plan.seq_block)


def read_segments(order, segments, batch):
    length = order.shape[0]
    rows = [segments[b].astype(F32) for b in range(batch)]
    rows = jnp.concatenate(rows + [jnp.zeros((EXTRA_ROWS - batch, length), F32)], axis=0)
    columns = dot_nt(order, rows.astype(BF16))
    return rows, [columns[:, b : b + 1] for b in range(batch)]


def project_kernel(
    tokens_far, gain_far, segments_far, w_query, w_key, w_value, conv_key, conv_value,
    x_out, normed_out, query_out, key_out, value_out, segment_out, packed_key, packed_value,
    conv_key_here, conv_value_here, query_here, key_here, value_here, tokens, gain, segments,
    arrived,
):
    ready = fetch_all(
        [
            (tokens_far, tokens), (segments_far, segments), (gain_far, gain), (w_key, key_here), (conv_key, conv_key_here), (w_value, value_here),
            (conv_value, conv_value_here), (w_query, query_here),
        ],
        arrived,
    )
    batch, _, length, width = tokens.shape
    slots = length // 3
    order = order_matrix(length, False)
    for number in range(3):
        ready(number)
    rows = [dot(order, tokens[b, 0]) for b in range(batch)]
    segment_rows, segment_columns = read_segments(order, segments, batch)
    x = jnp.concatenate(rows, axis=0)
    x_out[...] = x
    for b in range(batch):
        segment_out[b] = segment_columns[b]
    last = lax.broadcasted_iota(jnp.int32, (length, width), 0)
    slot = lax.broadcasted_iota(jnp.int32, (length, width), 1)
    extra = dot(segment_rows.astype(BF16), (last == 3 * slot + 2).astype(BF16)).astype(BF16)
    unit, _ = normalize(x)
    normed = (unit * gain[...].astype(F32).reshape(1, width)).astype(BF16)

    normed_out[...] = normed
    for number, flat_out, packed_out in ((3, key_out, packed_key), (5, value_out, packed_value)):
        flat = dot(normed, ready(number)[...]).astype(BF16)
        flat_out[...] = flat
        taps = [[], [], []]
        for b in range(batch):
            masks = window_masks(segment_columns[b], slots)
            for i in range(3):
                start = b * length + i * slots
                part = flat[start : start + slots].astype(F32) * masks[i]
                taps[i].append(part.astype(BF16))
        conv = ready(number + 1)
        total = None
        for i in range(3):
            term = dot(jnp.concatenate(taps[i], axis=0), conv[i * width : (i + 1) * width, :])
            total = term if total is None else total + term
        packed_out[0 : batch * slots, :] = total.astype(BF16)
    packed_key[batch * slots :, :] = extra
    query_out[...] = dot(normed, ready(7)[...]).astype(BF16)


def layer_kernel(
    plan, short, down_order, up_order,
    x_in, normed_in, cotangent, query_in, key_in, value_in, segment_column, gain_ffn,
    keys_near, keys_far, values_near, values_far, w_out, w_up, w_down,
    layer_out, d_hidden_out, d_query_out, d_key_own, d_value_own,
    d_key_keep, d_key_send, d_value_keep, d_value_send,
    down_send, down_keep, up_send, up_keep, gain_grad,
    all_keys, all_values, all_extra, bias, statistics, prob_keep, expanded_sum, d_normed_sum,
    d_attended, normed_ffn_out, activated_out, d_expanded_out, cotangent_out, attended_out,
    d_branch_out, down_rows, up_rows, out_rows, query_rows, *copied,
):
    batch, _, length, width = cotangent.shape
    slots = length // 3
    n_seq = plan.n_seq
    half = n_seq // 2
    total_slots = slots * n_seq
    own_place = lax.axis_index("seq")
    key_position = {plan.seq_relative(plan.key_order, p): p for p in range(n_seq)}
    packed_rows = batch * slots
    payload = packed_rows + EXTRA_ROWS
    copies = []

    def put(source, start, rows, target, lanes=slice(None)):
        if short:
            target[...] = source[start : start + rows, lanes]
            return
        copies.append(
            pltpu.make_async_copy(
                source.at[pl.ds(start, rows), lanes], target, copied[0].at[len(copies)]
            )
        )
        copies[-1].start()

    for p in range(n_seq):
        keys, values = (keys_near, values_near) if p < half else (keys_far, values_far)
        place = p % half
        q = key_position[plan.seq_relative(plan.value_order, p)]
        put(
            keys, place * payload + packed_rows, EXTRA_ROWS, all_extra.at[p], slice(0, LANES)
        )
        for b in range(batch):
            put(
                keys, place * payload + b * slots, slots,
                all_keys.at[b, pl.ds(p * slots, slots), :],
            )
            put(
                values, place * packed_rows + b * slots, slots,
                all_values.at[b, pl.ds(q * slots, slots), :],
            )
    for copy in copies:
        copy.wait()

    segment_rows = jnp.zeros((EXTRA_ROWS, total_slots), F32)
    slot_lane = lax.broadcasted_iota(jnp.int32, (1, total_slots), 1)
    slot_end = jnp.zeros((1, total_slots), jnp.int32)
    select_row = lax.broadcasted_iota(jnp.int32, (LANES, total_slots), 0)
    select_lane = lax.broadcasted_iota(jnp.int32, (LANES, total_slots), 1)
    for p in range(n_seq):
        selected = (select_lane == select_row + p * slots) & (select_row < slots)
        segment_rows += dot(all_extra[p], selected.astype(BF16))
        owner = plan.seq_relative(plan.key_order, p) ^ own_place
        here = (slot_lane >= p * slots) & (slot_lane < (p + 1) * slots)
        slot_end = jnp.where(here, length * owner - length * p + 3 * slot_lane + 2, slot_end)
    row = lax.broadcasted_iota(jnp.int32, (length, 1), 0)
    tap = (row >= slots).astype(jnp.int32) + (row >= 2 * slots).astype(jnp.int32)
    query_place = length * own_place + 3 * (row - tap * slots) + tap
    causal = slot_end <= query_place
    for b in range(batch):
        matching = segment_rows[b : b + 1, :] == segment_column[b]
        bias[b] = jnp.where(causal & matching, 0.0, MASKED_OUT)

    low_lane = lax.broadcasted_iota(jnp.int32, (length, LANES), 1) < HEAD_DIM

    def stacked(part):
        zero = jnp.zeros_like(part)
        return jnp.concatenate(
            [jnp.where(low_lane, part, zero), jnp.where(low_lane, zero, part)], axis=0
        )

    def twice(part):
        return jnp.concatenate([part, part], axis=0)

    def merged(part):
        return jnp.where(low_lane, part[:length], part[length:])

    def lanes_of(g):
        return pl.ds(pl.multiple_of(g * LANES, LANES), LANES)

    def place_of(number):
        b, g = number // GROUPS, number % GROUPS
        if short:
            return b, slice(b * length, (b + 1) * length), slice(g * LANES, (g + 1) * LANES)
        return b, pl.ds(pl.multiple_of(b * length, 16), length), lanes_of(g)

    def each(step):
        if short:
            for number in range(batch * GROUPS):
                step(number)
        else:
            lax.fori_loop(0, batch * GROUPS, lambda number, carry: (step(number), carry)[1], 0)

    def scaled_queries(rows, lanes):
        part = query_in[rows, lanes].astype(F32) * SCALE
        return stacked(part).astype(BF16)

    def attend(number):
        b, rows, lanes = place_of(number)
        queries = scaled_queries(rows, lanes)
        own_key = twice(key_in[rows, lanes].astype(F32))
        scores = dot_nt(queries, all_keys[b, :, lanes]) + twice(bias[b])
        own_score = jnp.sum(queries.astype(F32) * own_key, axis=-1, keepdims=True)
        top = jnp.maximum(own_score, jnp.max(scores, axis=-1, keepdims=True))
        raised = jnp.exp(scores - top)
        own_raised = jnp.exp(own_score - top)
        inverse = 1.0 / (own_raised + jnp.sum(raised, axis=-1, keepdims=True))
        prob = raised * inverse
        own_prob = own_raised * inverse
        if short:
            prob_keep[number] = prob
        statistics[number, :, 0:1] = own_prob
        statistics[number, :, 1:2] = top - jnp.log(inverse)
        result = dot(prob.astype(BF16), all_values[b, :, lanes])
        own_value = twice(value_in[rows, lanes].astype(F32))
        result += own_prob.astype(BF16).astype(F32) * own_value
        attended_out[rows, lanes] = merged(result).astype(BF16)

    each(attend)

    x = x_in[...]
    hidden = x + dot(attended_out[...], w_out[...])
    unit, inverse_dev = normalize(hidden)
    gain = gain_ffn[...].astype(F32).reshape(1, width)
    normed_ffn_out[...] = (unit * gain).astype(BF16)
    order = order_matrix(length, False)
    for b in range(batch):
        cotangent_out[b * length : (b + 1) * length, :] = dot(order, cotangent[b, 0]).astype(BF16)
    expanded_sum[...] = hidden
    d_normed_sum[...] = jnp.zeros_like(d_normed_sum)
    chunk = width
    total_width = w_up.shape[1]

    def feed(number, carry):
        columns = pl.ds(pl.multiple_of(number * chunk, chunk), chunk)
        expanded = dot(normed_ffn_out[...], w_up[:, columns])
        square = expanded * expanded
        curve = jnp.tanh(GELU_SCALE * expanded * (1.0 + GELU_CUBIC * square))
        activated = (0.5 * expanded * (1.0 + curve)).astype(BF16)
        activated_out[:, columns] = activated
        slope = 0.5 * (1.0 + curve) + 0.5 * expanded * (1.0 - curve * curve) * (
            GELU_SCALE * (1.0 + 3.0 * GELU_CUBIC * square)
        )
        expanded_sum[...] += dot(activated, w_down[columns, :])
        d_activated = dot_nt(cotangent_out[...], w_down[columns, :])
        d_expanded = (d_activated * slope).astype(BF16)
        d_expanded_out[:, columns] = d_expanded
        d_normed_sum[...] += dot_nt(d_expanded, w_up[:, columns])
        return carry

    lax.fori_loop(0, total_width // chunk, feed, 0, unroll=short)

    unorder = order_matrix(length, True)
    for b in range(batch):
        part = expanded_sum[b * length : (b + 1) * length, :].astype(BF16)
        layer_out[b, 0] = dot(unorder, part).astype(BF16)
    d_normed = d_normed_sum[...]
    gain_grad[...] = jnp.sum(d_normed * unit, axis=0, keepdims=True)
    d_hidden = cotangent_out[...].astype(F32) + normalize_back(d_normed, unit, inverse_dev, gain)
    d_hidden_out[...] = d_hidden
    d_branch = d_hidden.astype(BF16)
    d_branch_out[...] = d_branch
    d_attended[...] = dot_nt(d_branch, w_out[...]).astype(BF16)

    value_spot = [key_position[plan.seq_relative(plan.value_order, p)] for p in range(n_seq)]

    def attend_back(number):
        b, rows, lanes = place_of(number)
        queries = scaled_queries(rows, lanes)
        own_prob = statistics[number, :, 0:1]
        if short:
            prob = prob_keep[number]
        else:
            scores = dot_nt(queries, all_keys[b, :, lanes]) + twice(bias[b])
            prob = jnp.exp(scores - statistics[number, :, 1:2])
        grads = stacked(d_attended[rows, lanes])
        own_value = twice(value_in[rows, lanes].astype(F32))
        own_key = twice(key_in[rows, lanes].astype(F32))
        prob_grad = dot_nt(grads, all_values[b, :, lanes])
        own_prob_grad = jnp.sum(grads.astype(F32) * own_value, axis=-1, keepdims=True)
        delta = own_prob * own_prob_grad + jnp.sum(prob * prob_grad, axis=-1, keepdims=True)
        d_score = (prob * (prob_grad - delta)).astype(BF16)
        d_own = (own_prob * (own_prob_grad - delta)).astype(BF16).astype(F32)
        own_low = own_prob.astype(BF16).astype(F32)
        d_query = merged(dot(d_score, all_keys[b, :, lanes]) + d_own * own_key) * SCALE
        d_query_out[rows, lanes] = d_query.astype(BF16)
        d_key_own[rows, lanes] = merged(d_own * queries.astype(F32))
        d_value_own[rows, lanes] = merged(own_low * grads.astype(F32))
        key_sums = dot_tn(d_score, queries).astype(BF16)
        value_sums = dot_tn(prob.astype(BF16), grads).astype(BF16)
        for p in range(n_seq):
            spot = pl.ds(p % half * packed_rows + b * slots, slots)
            key_target, value_target = (
                (d_key_keep, d_value_keep) if p < half else (d_key_send, d_value_send)
            )
            key_target[spot, lanes] = key_sums[p * slots : (p + 1) * slots]
            q = value_spot[p]
            value_target[spot, lanes] = value_sums[q * slots : (q + 1) * slots]

    def weight_piece(number):
        c = number // 2
        columns = slice(c * chunk, (c + 1) * chunk)
        if c == total_width // chunk:
            out_rows[...] = dot_tn(attended_out[...], d_branch_out[...]).astype(BF16)
        elif number % 2 == 0:
            product = dot_tn(activated_out[:, columns], cotangent_out[...])
            down_rows[columns, :] = product.astype(BF16)
        else:
            up_rows[c] = dot_tn(normed_ffn_out[...], d_expanded_out[:, columns]).astype(BF16)

    pieces = list(range(2 * (total_width // chunk) + 1))

    def attend_back_and_weigh(number):
        attend_back(number)
        if short and pieces:
            weight_piece(pieces.pop(0))

    each(attend_back_and_weigh)
    while pieces:
        weight_piece(pieces.pop(0))
    query_rows[...] = dot_tn(normed_in[...], d_query_out[...]).astype(BF16)
    _, mine = own_places(plan)
    thin = width // plan.blocks
    parts = ((down_rows, total_width // plan.blocks), (out_rows, thin))
    spread(plan, mine, down_order, parts, down_send, down_keep)
    parts = tuple((up_rows.at[c], thin) for c in range(total_width // chunk))
    spread(plan, mine, up_order, parts + ((query_rows, thin),), up_send, up_keep)


def spread(plan, place, order, parts, send, keep):
    half = plan.blocks // 2
    for target, core in ((send, 1), (keep, 0)):
        start = 0
        for p in range(half):
            block = plan.relative(order, core * half + p) ^ place
            for source, rows in parts:
                target[start : start + rows, :] = source[
                    pl.ds(pl.multiple_of(block * rows, 16), rows), :
                ]
                start += rows


def conv_grad_kernel(
    plan, order, segment_column, d_packed, flat, own, conv, send, keep, d_flat_out, conv_rows
):
    batch, length, _ = segment_column.shape
    width = conv.shape[1]
    slots = length // 3
    masks = [window_masks(segment_column[b], slots) for b in range(batch)]
    back = d_packed[...]
    for i in range(3):
        taps = []
        for b in range(batch):
            start = b * length + i * slots
            part = flat[start : start + slots, :].astype(F32) * masks[b][i]
            taps.append(part.astype(BF16))
        window = jnp.concatenate(taps, axis=0)
        conv_rows[i * width : (i + 1) * width, :] = dot_tn(window, back).astype(BF16)
    _, mine = own_places(plan)
    spread(plan, mine, order, ((conv_rows, 3 * width // plan.blocks),), send, keep)
    for i in range(3):
        from_tap = dot_nt(back, conv[i * width : (i + 1) * width, :])
        for b in range(batch):
            start = b * length + i * slots
            part = from_tap[b * slots : (b + 1) * slots] * masks[b][i]
            d_flat_out[start : start + slots, :] = (part + own[start : start + slots, :]).astype(BF16)


def tail_kernel(
    plan, order, normed, x_in, gain, d_query, d_keys, d_values, d_hidden, gain_ffn_grad,
    w_query, w_key, w_value,
    send, keep, grad_tokens, key_rows, value_rows,
):
    batch, _, length, width = grad_tokens.shape
    key_rows[...] = dot_tn(normed[...], d_keys[...]).astype(BF16)
    value_rows[...] = dot_tn(normed[...], d_values[...]).astype(BF16)
    _, mine = own_places(plan)
    thin = width // plan.blocks
    spread(plan, mine, order, ((key_rows, thin), (value_rows, thin)), send, keep)
    d_normed = (
        dot_nt(d_query[...], w_query[...])
        + dot_nt(d_keys[...], w_key[...])
        + dot_nt(d_values[...], w_value[...])
    )
    unit, inverse_dev = normalize(x_in[...])
    gain_grad = jnp.sum(d_normed * unit, axis=0, keepdims=True)
    d_input = normalize_back(d_normed, unit, inverse_dev, gain[...].astype(F32).reshape(1, width))
    result = (d_hidden[...] + d_input).astype(BF16)
    unorder = order_matrix(length, True)
    for b in range(batch):
        part = result[b * length : (b + 1) * length, :]
        grad_tokens[b, 0] = dot(unorder, part).astype(BF16)
    row = lax.broadcasted_iota(jnp.int32, (EXTRA_ROWS, width), 0)
    gains = jnp.where(row == 0, gain_grad, jnp.where(row == 1, gain_ffn_grad[...], 0.0))
    send[send.shape[0] - EXTRA_ROWS :, :] = gains.astype(BF16)
    keep[keep.shape[0] - EXTRA_ROWS :, :] = gains.astype(BF16)


def finish_kernel(plan, items, count, aliased, n_gains, *refs):
    blocks, refs = refs[: len(items)], refs[len(items) :]
    gains, refs = refs[: min(n_gains, 1)], refs[min(n_gains, 1) + (count if aliased else 0) :]
    targets, token, refs = refs[:count], refs[count], refs[count + 1 :]
    gain_targets, (sent, *stages) = refs[:n_gains], refs[n_gains:]
    token[...] = jnp.zeros_like(token)
    for row, target in enumerate(gain_targets):
        target[...] = gains[0][...].astype(F32)[row : row + 1, :].reshape(-1)
    _, mine = own_places(plan)
    half = plan.blocks // 2
    copies = []
    for source, stage, (layout, parts, core) in zip(blocks, stages, items):
        start = 0
        for p in range(half):
            block = plan.relative(layout, core * half + p) ^ mine
            for rows, target, columns in parts:
                stage[start : start + rows, :] = source[start : start + rows, :].astype(F32)
                spot = pl.ds(pl.multiple_of(block * rows, 16), rows)
                copy = pltpu.make_async_copy(
                    stage.at[pl.ds(start, rows), :],
                    targets[target].at[spot, columns],
                    sent.at[len(copies)],
                )
                copy.start()
                copies.append(copy)
                start += rows
    for copy in copies:
        copy.wait()


def finish(plan, order, name, chosen, cores, targets=(), gains=()):
    items, blocks, shapes = [], [], []
    for part in chosen:
        for core in cores:
            parts = [(rows, len(shapes) + target, columns) for rows, target, columns in part.parts]
            items.append((part.bits, parts, core))
            blocks.append(part.far if core else part.held)
        shapes += part.shapes
    count = len(shapes)
    everywhere = tuple(range(count))
    copies = sum(plan.blocks // 2 * len(parts) for _, parts, _ in items)
    n_gains = 2 * len(gains)
    results = order.call(
        functools.partial(finish_kernel, plan, items, count, bool(targets), n_gains),
        name,
        [(shape, F32) for shape in shapes] + [((8, LANES), F32)]
        + [((array.shape[1],), F32) for array in gains] * 2,
        [pltpu.SemaphoreType.DMA((copies,))] + [pltpu.VMEM(array.shape, F32) for array in blocks],
        anywhere=tuple(range(len(items), len(items) + count)) if targets else (),
        out_anywhere=everywhere,
        aliases={len(items) + number: number for number in everywhere} if targets else None,
        token=count,
    )(*blocks, *gains, *targets)
    return results[:count], results[count + 1 :]


class RowGather:
    def __init__(self, name, plan, order, array, bits):
        self.name, self.plan, self.order = name, plan, order
        self.held, self.bits = array, list(bits)

    def step(self):
        arrived = self.plan.swap(self.held, ("seq", self.bits.pop(0)), self.name)
        if not self.bits:
            return [self.held, arrived]
        rows = self.held.shape[0]
        self.held, = self.order.combine(
            "gather_row", [self.held, arrived], [[(0, 0, rows), (1, 0, rows)]]
        )


class RowScatter:
    def __init__(self, name, plan, order, keep, send, bits):
        self.name, self.plan, self.order, self.keep, self.send = name, plan, order, keep, send
        self.bits = list(bits)

    def step(self, microseconds=EACH):
        if not self.bits:
            return
        arrived = self.plan.swap(self.send, ("seq", self.bits.pop()), self.name)
        rows = self.keep.shape[0]
        half = rows // 2
        outs = [(0, rows)] if not self.bits else [(0, half), (half, half)]
        self.keep, *send = self.order.combine(
            "scatter_row", [self.keep, arrived],
            [[(0, start, size, 1, start)] for start, size in outs], microseconds,
        )
        self.send = send[0] if send else None


class Part:
    def __init__(self, name, plan, order, bits, send, keep, shapes, parts, extra=0):
        self.name, self.plan, self.order, self.bits, self.extra = name, plan, order, bits, extra
        self.send, self.keep = send, keep
        self.shapes, self.parts = shapes, parts
        self.done = 0

    def step(self, microseconds):
        if self.done < len(self.bits):
            self.scatter(self.bits[self.done], microseconds)
        else:
            self.gather(self.bits[2 * len(self.bits) - 1 - self.done], microseconds)
        self.done += 1

    def scatter(self, bit, microseconds):
        arrived = self.plan.swap(self.send, bit, self.name)
        extra = self.extra
        rows = self.keep.shape[0] - extra
        last = [(0, rows, extra, 1, rows)]
        if self.done < len(self.bits) - 1:
            half = rows // 2
            outs = [[(0, start, half, 1, start)] + (last if extra else []) for start in (0, half)]
            self.keep, self.send = self.order.combine(
                "scatter", [self.keep, arrived], outs, microseconds
            )
            return
        outs = [[(0, 0, rows, 1, 0)]] + ([last] if extra else [])
        self.held, *self.sums = self.order.combine(
            "scatter", [self.keep, arrived], outs, microseconds
        )
        for bit in self.plan.rest:
            arrays = [self.held] + self.sums
            arrived = [self.plan.swap(array, bit, self.name) for array in arrays]
            self.held, *self.sums = self.order.combine(
                "scatter_rest", arrays + arrived,
                [
                    [(i, 0, array.shape[0], i + len(arrays), 0)]
                    for i, array in enumerate(arrays)
                ],
            )

    def gather(self, bit, microseconds=EACH):
        arrived = self.plan.swap(self.held, bit, self.name)
        rows = self.held.shape[0]
        self.held, = self.order.combine(
            "gather", [self.held, arrived], [[(0, 0, rows), (1, 0, rows)]], microseconds
        )
        if self.done == 2 * len(self.bits) - 2:
            self.far = self.plan.swap(self.held, self.plan.core, self.name)


def body(
    plan, tokens, segments, cotangent, gain_attn, w_query, w_key, w_value, conv_key, conv_value,
    w_out, gain_ffn, w_up, w_down,
):
    batch, _, length, width = tokens.shape
    slots = length // 3
    square = (width, width)
    positions = batch * length
    flat, flat32 = ((positions, width), BF16), ((positions, width), F32)
    square_here = pltpu.VMEM(square, BF16)
    conv_here = pltpu.VMEM(conv_key.shape, BF16)
    order = Order()
    later = [conv_key, conv_value, w_query, w_key, w_value]
    short = slots * plan.n_seq <= SHORT_ROW
    (
        x, normed, queries, key_rows, value_rows, segment_column, packed_key, packed_value, *here,
    ) = order.call(
        project_kernel,
        "project",
        [flat32] + [flat] * 4 + [((batch, length, 1), F32)]
        + [((batch * slots + EXTRA_ROWS, width), BF16), ((batch * slots, width), BF16)]
        + ([(array.shape, BF16) for array in later] if short else []),
        scratch=([] if short else [conv_here] * 2 + [square_here] * 3)
        + [
            pltpu.VMEM(tokens.shape, BF16), pltpu.VMEM(gain_attn.shape, BF16),
            pltpu.VMEM(segments.shape, jnp.int32), pltpu.SemaphoreType.DMA((8,)),
        ],
        anywhere=tuple(range(8)),
        token=5,
    )(tokens, gain_attn, segments, w_query, w_key, w_value, conv_key, conv_value)

    later = here or later
    steps = len(plan.key_order)
    keys = RowGather("gather_keys", plan, order, packed_key, plan.key_order)
    values = RowGather("gather_values", plan, order, packed_value, plan.value_order)
    for number in range(steps - 1):
        keys.step()
        values.step()

    core = [plan.core]
    x_first, y_first = core + plan.first + plan.tail, core + plan.second + plan.tail
    z_first = core + plan.tail[:1] + plan.first + plan.tail[1:]
    bits = {"A0": y_first, "A1": x_first, "B0": y_first, "B1": x_first, "B2": z_first}
    half = plan.blocks // 2
    thin, down_block, conv_block = (
        rows // plan.blocks for rows in (width, w_down.shape[0], conv_key.shape[0])
    )
    chunks = w_up.shape[1] // width
    everything = slice(None)
    ups = [(thin, 0, slice(c * width, (c + 1) * width)) for c in range(chunks)]
    layouts = {
        "A0": ([w_down.shape, square], [(down_block, 0, everything), (thin, 1, everything)]),
        "A1": ([w_up.shape, square], ups + [(thin, 1, everything)]),
        "B0": ([conv_key.shape], [(conv_block, 0, everything)]),
        "B1": ([conv_value.shape], [(conv_block, 0, everything)]),
        "B2": ([square, square], [(thin, 0, everything), (thin, 1, everything)]),
    }

    def half_rows(name):
        return half * sum(part[0] for part in layouts[name][1])

    total_slots = slots * plan.n_seq
    half_packed = ((batch * total_slots // 2, width), BF16)
    halves = [((half_rows(name), width), BF16) for name in ("A0", "A0", "A1", "A1")]
    flat_here = pltpu.VMEM((positions, width), BF16)
    wide_here = pltpu.VMEM((positions, w_up.shape[1]), BF16)
    copied = [] if short else [pltpu.SemaphoreType.DMA((plan.n_seq * (1 + 2 * batch),))]
    layer_out, d_hidden, d_query, d_key_own, d_value_own, *outs, gain_ffn_grad = order.call(
        functools.partial(layer_kernel, plan, short, bits["A0"], bits["A1"]),
        "layer",
        [(tokens.shape, BF16), flat32, flat, flat32, flat32] + [half_packed] * 4 + halves
        + [((1, width), F32)],
        scratch=[
            pltpu.VMEM((batch, total_slots, width), BF16),
            pltpu.VMEM((batch, total_slots, width), BF16),
            pltpu.VMEM((plan.n_seq, EXTRA_ROWS, LANES), BF16),
            pltpu.VMEM((batch, length, total_slots), F32),
            pltpu.VMEM((batch * GROUPS, 2 * length, LANES), F32),
            pltpu.VMEM((batch * GROUPS, 2 * length, total_slots) if short else (1, 8, LANES), F32),
            pltpu.VMEM((positions, width), F32),
            pltpu.VMEM((positions, width), F32),
            flat_here, flat_here, wide_here, wide_here, flat_here, flat_here, flat_here,
            pltpu.VMEM(w_down.shape, BF16),
            pltpu.VMEM((chunks, width, width), BF16),
            square_here, square_here,
        ]
        + copied,
        anywhere=() if short else (8, 9, 10, 11),
        vmem=VMEM_SMALL if short else VMEM_LARGE,
        token=-1,
    )(
        x, normed, cotangent, queries, key_rows, value_rows, segment_column, gain_ffn,
        *keys.step(), *values.step(), w_out, w_up, w_down,
    )
    rows = [
        RowScatter("K", plan, order, outs[0], outs[1], plan.key_order),
        RowScatter("V", plan, order, outs[2], outs[3], plan.value_order),
    ]
    chains, d_flats = {"K": rows[0], "V": rows[1]}, {}
    for name, (send, keep) in (("A0", outs[4:6]), ("A1", outs[6:8])):
        chains[name] = Part(name, plan, order, bits[name], send, keep, *layouts[name])

    def make(name, kernel, outs, scratch, operands, extra=0):
        total = half_rows(name) + extra
        send, keep, *others = order.call(
            functools.partial(kernel, plan, bits[name]),
            kernel.__name__,
            [((total, width), BF16)] * 2 + outs,
            scratch=scratch,
        )(*operands)
        chains[name] = Part(name, plan, order, bits[name], send, keep, *layouts[name], extra)
        return others

    for event in EVENTS:
        if event in ("TK", "TV"):
            number = 0 if event == "TK" else 1
            row = rows[number]
            while row.bits:
                row.step()
            d_flat, = make(
                f"B{number}", conv_grad_kernel, [flat], [conv_here],
                (
                    segment_column, row.keep, (key_rows, value_rows)[number],
                    (d_key_own, d_value_own)[number], later[number],
                ),
            )
            d_flats[event] = d_flat
        elif event == "T3":
            grad_tokens, = make(
                "B2", tail_kernel, [(tokens.shape, BF16)], [square_here, square_here],
                (
                    normed, x, gain_attn, d_query, d_flats["TK"], d_flats["TV"], d_hidden,
                    gain_ffn_grad, *later[2:],
                ),
                EXTRA_ROWS,
            )
        elif event == "Af":
            grads, gains = finish(
                plan, order, "finish", [chains["A0"], chains["A1"]], (0, 1), (), chains["B2"].sums
            )
            grad_down, grad_out, grad_up, grad_query = grads
        elif event in ("Bn", "Bf"):
            chosen = [chains[name] for name in ("B0", "B1", "B2")]
            previous = () if event == "Bn" else results
            results, _ = finish(plan, order, "finish", chosen, (int(event == "Bf"),), previous)
        else:
            name, _, cost = event.partition(":")
            chains[name].step(float(cost or EACH))
    grad_conv_key, grad_conv_value, grad_key, grad_value = results
    return (
        layer_out, grad_tokens, gains[0], grad_query, grad_key, grad_value,
        grad_conv_key, grad_conv_value, grad_out, gains[1], grad_up, grad_down,
    )


def solution(mesh):
    packed = P(None, "rows", "seq", None)
    in_specs = (packed, P(None, "rows", "seq"), packed) + (P(),) * 10
    out_specs = (packed, packed) + (P(),) * 10
    return jax.shard_map(
        functools.partial(body, Plan(mesh)),
        mesh=mesh, in_specs=in_specs, out_specs=out_specs, check_vma=False,
    )
```

```python
import functools

import jax
import jax.numpy as jnp
from jax import lax
from jax.experimental import pallas as pl
from jax.experimental.pallas import tpu as pltpu
from jax.sharding import PartitionSpec as P

HEADS = 8
HEAD_DIM = 64
LANES = 128
GROUPS = HEADS * HEAD_DIM // LANES
EPSILON = 1e-05
MASKED_OUT = -1e30
SCALE = HEAD_DIM ** (-0.5)
GELU_SCALE = 0.7978845608028654
GELU_CUBIC = 0.044715
SCATTER_BITS = 5
EXTRA_ROWS = 16
VMEM_SMALL = 28 * 1024 * 1024
VMEM_LARGE = 62 * 1024 * 1024
SHORT_ROW = 768
BYTES_MICROSECOND = 3_690_000
EACH = 5

EVENTS = (
    "A0", "A1", "K", "V", "V:0", "K:0", "A1:0", "A0", "K", "V", "TK", "TV", "T3", "B0", "B1",
    "A0", "A1", "B2", "A0", "A1", "B1", "B0", "B2", "A1", "A0", "A1", "B1", "B2", "A0", "A1",
    "B0", "B2", "B1", "A0", "A1", "B0", "B2", "B1", "A0", "B0", "B2", "B1", "B0", "A1", "B2",
    "B1", "B0", "A0", "B2", "B0", "B1", "B2", "Af", "B0", "B1", "Bn", "Bf",
)

BF16 = jnp.bfloat16
F32 = jnp.float32


def dot(left, right):
    return jnp.dot(left, right, preferred_element_type=F32)


def dot_nt(left, right):
    return lax.dot_general(left, right, (((1,), (1,)), ((), ())), preferred_element_type=F32)


def dot_tn(left, right):
    return lax.dot_general(left, right, (((0,), (0,)), ((), ())), preferred_element_type=F32)


def normalize(values):
    average = jnp.mean(values, axis=-1, keepdims=True)
    centred = values - average
    variance = jnp.mean(centred * centred, axis=-1, keepdims=True)
    inverse_dev = lax.rsqrt(variance + EPSILON)
    return centred * inverse_dev, inverse_dev


def normalize_back(grad_normed, unit, inverse_dev, gain):
    grad_unit = grad_normed * gain
    first_mean = jnp.mean(grad_unit, axis=-1, keepdims=True)
    second_mean = jnp.mean(grad_unit * unit, axis=-1, keepdims=True)
    return inverse_dev * (grad_unit - first_mean - unit * second_mean)


class Plan:
    def __init__(self, mesh):
        self.n_rows = mesh.shape["rows"]
        self.n_seq = mesh.shape["seq"]
        rows = [("rows", 1 << i) for i in range(self.n_rows.bit_length() - 1)]
        seq = [("seq", 1 << i) for i in range(self.n_seq.bit_length() - 1)]
        kept = max(0, min(len(seq), SCATTER_BITS - len(rows)))
        self.seq_block = 1 << kept
        self.blocks = self.n_rows * self.seq_block
        core, others = rows[:1], rows[1:]
        low, high = seq[:1], seq[1:kept] if kept else []
        low = low[:kept]
        self.core = core[0]
        self.first = others + low
        self.second = low + others
        self.tail = high
        self.rest = seq[kept:]
        bits = [1 << i for i in range(len(seq))]
        self.key_order = bits[::-1]
        self.value_order = bits[:1] + bits[:0:-1]

    def mask(self, bit):
        axis, value = bit
        return value * self.seq_block if axis == "rows" else value

    def relative(self, order, position):
        result = 0
        for number, bit in enumerate(order):
            if position >> (len(order) - 1 - number) & 1:
                result |= self.mask(bit)
        return result

    def seq_relative(self, order, position):
        result = 0
        for number, bit in enumerate(order):
            if position >> number & 1:
                result |= bit
        return result

    def swap(self, array, bit, name):
        axis, value = bit
        size = self.n_rows if axis == "rows" else self.n_seq
        with jax.named_scope(f"swap_{name}"):
            return lax.ppermute(array, axis, [(i, i ^ value) for i in range(size)])


def order_matrix(length, transposed):
    slots = length // 3
    rows = lax.broadcasted_iota(jnp.int32, (length, length), 1 if transposed else 0)
    columns = lax.broadcasted_iota(jnp.int32, (length, length), 0 if transposed else 1)
    tap = (rows >= slots).astype(jnp.int32) + (rows >= 2 * slots).astype(jnp.int32)
    return (columns == 3 * (rows - tap * slots) + tap).astype(BF16)


def window_masks(segment_column, slots):
    last = segment_column[2 * slots :]
    return [(segment_column[i * slots : (i + 1) * slots] == last).astype(F32) for i in range(3)]


def fetch_all(pairs, arrived):
    copies = [
        pltpu.make_async_copy(source, target, arrived.at[number])
        for number, (source, target) in enumerate(pairs)
    ]
    for copy in copies:
        copy.start()

    def ready(number):
        copies[number].wait()
        return pairs[number][1]

    return ready


class Order:
    def __init__(self):
        self.last = ()

    def call(
        self, kernel, name, outs, scratch=(), anywhere=(), out_anywhere=(), aliases=None,
        vmem=VMEM_SMALL, microseconds=EACH, token=0,
    ):
        def spec(number, places):
            return pl.BlockSpec(memory_space=pl.ANY if number in places else pltpu.VMEM)

        def run(*operands):
            count, last = len(operands), self.last

            def without_last(*refs):
                kernel(*refs[:count], *refs[count + len(last) :])

            operands = [
                pltpu.with_memory_space_constraint(operand, pltpu.HBM)
                if number in anywhere and not aliases
                else operand
                for number, operand in enumerate(operands)
            ]
            results = pl.pallas_call(
                without_last,
                name=name,
                out_shape=[
                    pltpu.HBM(shape, dtype)
                    if number in out_anywhere
                    else jax.ShapeDtypeStruct(shape, dtype)
                    for number, (shape, dtype) in enumerate(outs)
                ],
                in_specs=[spec(number, anywhere) for number in range(count)]
                + [pl.BlockSpec(memory_space=pl.ANY)] * len(last),
                out_specs=[spec(number, out_anywhere) for number in range(len(outs))],
                scratch_shapes=list(scratch),
                input_output_aliases=aliases or {},
                compiler_params=pltpu.CompilerParams(vmem_limit_bytes=vmem),
                cost_estimate=pl.CostEstimate(
                    flops=1 + int(microseconds * 1_150_000_000), bytes_accessed=1 + int(microseconds * BYTES_MICROSECOND), transcendentals=0
                ),
            )(*operands, *last)
            self.last = (results[token],)
            return results

        return run

    def combine(self, name, inputs, outs, microseconds=EACH):
        width = inputs[0].shape[1]

        def kernel(*refs):
            sources, targets = refs[: len(inputs)], refs[len(inputs) :]
            for target, pieces in zip(targets, outs):
                offset = 0
                for number, start, rows, *other in pieces:
                    part = sources[number][start : start + rows, :]
                    if other:
                        added = sources[other[0]][other[1] : other[1] + rows, :]
                        part = (part.astype(F32) + added.astype(F32)).astype(BF16)
                    target[offset : offset + rows, :] = part
                    offset += rows

        shapes = [((sum(piece[2] for piece in pieces), width), BF16) for pieces in outs]
        return self.call(kernel, name, shapes, microseconds=microseconds)(*inputs)


def own_places(plan):
    seq = lax.axis_index("seq")
    return seq, lax.axis_index("rows") * plan.seq_block + lax.rem(seq, plan.seq_block)


def read_segments(order, segments, batch):
    length = order.shape[0]
    rows = [segments[b].astype(F32) for b in range(batch)]
    rows = jnp.concatenate(rows + [jnp.zeros((EXTRA_ROWS - batch, length), F32)], axis=0)
    columns = dot_nt(order, rows.astype(BF16))
    return rows, [columns[:, b : b + 1] for b in range(batch)]


def project_kernel(
    tokens_far, gain_far, segments_far, w_query, w_key, w_value, conv_key, conv_value,
    x_out, normed_out, query_out, key_out, value_out, segment_out, packed_key, packed_value,
    conv_key_here, conv_value_here, query_here, key_here, value_here, tokens, gain, segments,
    arrived,
):
    ready = fetch_all(
        [
            (tokens_far, tokens), (segments_far, segments), (gain_far, gain), (w_key, key_here), (conv_key, conv_key_here), (w_value, value_here),
            (conv_value, conv_value_here), (w_query, query_here),
        ],
        arrived,
    )
    batch, _, length, width = tokens.shape
    slots = length // 3
    order = order_matrix(length, False)
    for number in range(3):
        ready(number)
    rows = [dot(order, tokens[b, 0]) for b in range(batch)]
    segment_rows, segment_columns = read_segments(order, segments, batch)
    x = jnp.concatenate(rows, axis=0)
    x_out[...] = x
    for b in range(batch):
        segment_out[b] = segment_columns[b]
    last = lax.broadcasted_iota(jnp.int32, (length, width), 0)
    slot = lax.broadcasted_iota(jnp.int32, (length, width), 1)
    extra = dot(segment_rows.astype(BF16), (last == 3 * slot + 2).astype(BF16)).astype(BF16)
    unit, _ = normalize(x)
    normed = (unit * gain[...].astype(F32).reshape(1, width)).astype(BF16)

    normed_out[...] = normed
    for number, flat_out, packed_out in ((3, key_out, packed_key), (5, value_out, packed_value)):
        flat = dot(normed, ready(number)[...]).astype(BF16)
        flat_out[...] = flat
        taps = [[], [], []]
        for b in range(batch):
            masks = window_masks(segment_columns[b], slots)
            for i in range(3):
                start = b * length + i * slots
                part = flat[start : start + slots].astype(F32) * masks[i]
                taps[i].append(part.astype(BF16))
        conv = ready(number + 1)
        total = None
        for i in range(3):
            term = dot(jnp.concatenate(taps[i], axis=0), conv[i * width : (i + 1) * width, :])
            total = term if total is None else total + term
        packed_out[0 : batch * slots, :] = total.astype(BF16)
    packed_key[batch * slots :, :] = extra
    query_out[...] = dot(normed, ready(7)[...]).astype(BF16)


def layer_kernel(
    plan, short, down_order, up_order,
    x_in, normed_in, cotangent, query_in, key_in, value_in, segment_column, gain_ffn,
    keys_near, keys_far, values_near, values_far, w_out, w_up, w_down,
    layer_out, d_hidden_out, d_query_out, d_key_own, d_value_own,
    d_key_keep, d_key_send, d_value_keep, d_value_send,
    down_send, down_keep, up_send, up_keep, gain_grad,
    all_keys, all_values, all_extra, bias, statistics, prob_keep, expanded_sum, d_normed_sum,
    d_attended, normed_ffn_out, activated_out, d_expanded_out, cotangent_out, attended_out,
    d_branch_out, down_rows, up_rows, out_rows, query_rows, *copied,
):
    batch, _, length, width = cotangent.shape
    slots = length // 3
    n_seq = plan.n_seq
    half = n_seq // 2
    total_slots = slots * n_seq
    own_place = lax.axis_index("seq")
    key_position = {plan.seq_relative(plan.key_order, p): p for p in range(n_seq)}
    packed_rows = batch * slots
    payload = packed_rows + EXTRA_ROWS
    copies = []

    def put(source, start, rows, target, lanes=slice(None)):
        if short:
            target[...] = source[start : start + rows, lanes]
            return
        copies.append(
            pltpu.make_async_copy(
                source.at[pl.ds(start, rows), lanes], target, copied[0].at[len(copies)]
            )
        )
        copies[-1].start()

    for p in range(n_seq):
        keys, values = (keys_near, values_near) if p < half else (keys_far, values_far)
        place = p % half
        q = key_position[plan.seq_relative(plan.value_order, p)]
        put(
            keys, place * payload + packed_rows, EXTRA_ROWS, all_extra.at[p], slice(0, LANES)
        )
        for b in range(batch):
            put(
                keys, place * payload + b * slots, slots,
                all_keys.at[b, pl.ds(p * slots, slots), :],
            )
            put(
                values, place * packed_rows + b * slots, slots,
                all_values.at[b, pl.ds(q * slots, slots), :],
            )
    for copy in copies:
        copy.wait()

    segment_rows = jnp.zeros((EXTRA_ROWS, total_slots), F32)
    slot_lane = lax.broadcasted_iota(jnp.int32, (1, total_slots), 1)
    slot_end = jnp.zeros((1, total_slots), jnp.int32)
    select_row = lax.broadcasted_iota(jnp.int32, (LANES, total_slots), 0)
    select_lane = lax.broadcasted_iota(jnp.int32, (LANES, total_slots), 1)
    for p in range(n_seq):
        selected = (select_lane == select_row + p * slots) & (select_row < slots)
        segment_rows += dot(all_extra[p], selected.astype(BF16))
        owner = plan.seq_relative(plan.key_order, p) ^ own_place
        here = (slot_lane >= p * slots) & (slot_lane < (p + 1) * slots)
        slot_end = jnp.where(here, length * owner - length * p + 3 * slot_lane + 2, slot_end)
    row = lax.broadcasted_iota(jnp.int32, (length, 1), 0)
    tap = (row >= slots).astype(jnp.int32) + (row >= 2 * slots).astype(jnp.int32)
    query_place = length * own_place + 3 * (row - tap * slots) + tap
    causal = slot_end <= query_place
    for b in range(batch):
        matching = segment_rows[b : b + 1, :] == segment_column[b]
        bias[b] = jnp.where(causal & matching, 0.0, MASKED_OUT)

    low_lane = lax.broadcasted_iota(jnp.int32, (length, LANES), 1) < HEAD_DIM

    def stacked(part):
        zero = jnp.zeros_like(part)
        return jnp.concatenate(
            [jnp.where(low_lane, part, zero), jnp.where(low_lane, zero, part)], axis=0
        )

    def twice(part):
        return jnp.concatenate([part, part], axis=0)

    def merged(part):
        return jnp.where(low_lane, part[:length], part[length:])

    def lanes_of(g):
        return pl.ds(pl.multiple_of(g * LANES, LANES), LANES)

    def place_of(number):
        b, g = number // GROUPS, number % GROUPS
        if short:
            return b, slice(b * length, (b + 1) * length), slice(g * LANES, (g + 1) * LANES)
        return b, pl.ds(pl.multiple_of(b * length, 16), length), lanes_of(g)

    def each(step):
        if short:
            for number in range(batch * GROUPS):
                step(number)
        else:
            lax.fori_loop(0, batch * GROUPS, lambda number, carry: (step(number), carry)[1], 0)

    def scaled_queries(rows, lanes):
        part = query_in[rows, lanes].astype(F32) * SCALE
        return stacked(part).astype(BF16)

    def attend(number):
        b, rows, lanes = place_of(number)
        queries = scaled_queries(rows, lanes)
        own_key = twice(key_in[rows, lanes].astype(F32))
        scores = dot_nt(queries, all_keys[b, :, lanes]) + twice(bias[b])
        own_score = jnp.sum(queries.astype(F32) * own_key, axis=-1, keepdims=True)
        top = jnp.maximum(own_score, jnp.max(scores, axis=-1, keepdims=True))
        raised = jnp.exp(scores - top)
        own_raised = jnp.exp(own_score - top)
        inverse = 1.0 / (own_raised + jnp.sum(raised, axis=-1, keepdims=True))
        prob = raised * inverse
        own_prob = own_raised * inverse
        if short:
            prob_keep[number] = prob
        statistics[number, :, 0:1] = own_prob
        statistics[number, :, 1:2] = top - jnp.log(inverse)
        result = dot(prob.astype(BF16), all_values[b, :, lanes])
        own_value = twice(value_in[rows, lanes].astype(F32))
        result += own_prob.astype(BF16).astype(F32) * own_value
        attended_out[rows, lanes] = merged(result).astype(BF16)

    each(attend)

    x = x_in[...]
    hidden = x + dot(attended_out[...], w_out[...])
    unit, inverse_dev = normalize(hidden)
    gain = gain_ffn[...].astype(F32).reshape(1, width)
    normed_ffn_out[...] = (unit * gain).astype(BF16)
    order = order_matrix(length, False)
    for b in range(batch):
        cotangent_out[b * length : (b + 1) * length, :] = dot(order, cotangent[b, 0]).astype(BF16)
    expanded_sum[...] = hidden
    d_normed_sum[...] = jnp.zeros_like(d_normed_sum)
    chunk = width
    total_width = w_up.shape[1]

    def feed(number, carry):
        columns = pl.ds(pl.multiple_of(number * chunk, chunk), chunk)
        expanded = dot(normed_ffn_out[...], w_up[:, columns])
        square = expanded * expanded
        curve = jnp.tanh(GELU_SCALE * expanded * (1.0 + GELU_CUBIC * square))
        activated = (0.5 * expanded * (1.0 + curve)).astype(BF16)
        activated_out[:, columns] = activated
        slope = 0.5 * (1.0 + curve) + 0.5 * expanded * (1.0 - curve * curve) * (
            GELU_SCALE * (1.0 + 3.0 * GELU_CUBIC * square)
        )
        expanded_sum[...] += dot(activated, w_down[columns, :])
        d_activated = dot_nt(cotangent_out[...], w_down[columns, :])
        d_expanded = (d_activated * slope).astype(BF16)
        d_expanded_out[:, columns] = d_expanded
        d_normed_sum[...] += dot_nt(d_expanded, w_up[:, columns])
        return carry

    lax.fori_loop(0, total_width // chunk, feed, 0, unroll=short)

    unorder = order_matrix(length, True)
    for b in range(batch):
        part = expanded_sum[b * length : (b + 1) * length, :].astype(BF16)
        layer_out[b, 0] = dot(unorder, part).astype(BF16)
    d_normed = d_normed_sum[...]
    gain_grad[...] = jnp.sum(d_normed * unit, axis=0, keepdims=True)
    d_hidden = cotangent_out[...].astype(F32) + normalize_back(d_normed, unit, inverse_dev, gain)
    d_hidden_out[...] = d_hidden
    d_branch = d_hidden.astype(BF16)
    d_branch_out[...] = d_branch
    d_attended[...] = dot_nt(d_branch, w_out[...]).astype(BF16)

    value_spot = [key_position[plan.seq_relative(plan.value_order, p)] for p in range(n_seq)]

    def attend_back(number):
        b, rows, lanes = place_of(number)
        queries = scaled_queries(rows, lanes)
        own_prob = statistics[number, :, 0:1]
        if short:
            prob = prob_keep[number]
        else:
            scores = dot_nt(queries, all_keys[b, :, lanes]) + twice(bias[b])
            prob = jnp.exp(scores - statistics[number, :, 1:2])
        grads = stacked(d_attended[rows, lanes])
        own_value = twice(value_in[rows, lanes].astype(F32))
        own_key = twice(key_in[rows, lanes].astype(F32))
        prob_grad = dot_nt(grads, all_values[b, :, lanes])
        own_prob_grad = jnp.sum(grads.astype(F32) * own_value, axis=-1, keepdims=True)
        delta = own_prob * own_prob_grad + jnp.sum(prob * prob_grad, axis=-1, keepdims=True)
        d_score = (prob * (prob_grad - delta)).astype(BF16)
        d_own = (own_prob * (own_prob_grad - delta)).astype(BF16).astype(F32)
        own_low = own_prob.astype(BF16).astype(F32)
        d_query = merged(dot(d_score, all_keys[b, :, lanes]) + d_own * own_key) * SCALE
        d_query_out[rows, lanes] = d_query.astype(BF16)
        d_key_own[rows, lanes] = merged(d_own * queries.astype(F32))
        d_value_own[rows, lanes] = merged(own_low * grads.astype(F32))
        key_sums = dot_tn(d_score, queries).astype(BF16)
        value_sums = dot_tn(prob.astype(BF16), grads).astype(BF16)
        for p in range(n_seq):
            spot = pl.ds(p % half * packed_rows + b * slots, slots)
            key_target, value_target = (
                (d_key_keep, d_value_keep) if p < half else (d_key_send, d_value_send)
            )
            key_target[spot, lanes] = key_sums[p * slots : (p + 1) * slots]
            q = value_spot[p]
            value_target[spot, lanes] = value_sums[q * slots : (q + 1) * slots]

    def weight_piece(number):
        c = number // 2
        columns = slice(c * chunk, (c + 1) * chunk)
        if c == total_width // chunk:
            out_rows[...] = dot_tn(attended_out[...], d_branch_out[...]).astype(BF16)
        elif number % 2 == 0:
            product = dot_tn(activated_out[:, columns], cotangent_out[...])
            down_rows[columns, :] = product.astype(BF16)
        else:
            up_rows[c] = dot_tn(normed_ffn_out[...], d_expanded_out[:, columns]).astype(BF16)

    pieces = list(range(2 * (total_width // chunk) + 1))

    def attend_back_and_weigh(number):
        attend_back(number)
        if short and pieces:
            weight_piece(pieces.pop(0))

    each(attend_back_and_weigh)
    while pieces:
        weight_piece(pieces.pop(0))
    query_rows[...] = dot_tn(normed_in[...], d_query_out[...]).astype(BF16)
    _, mine = own_places(plan)
    thin = width // plan.blocks
    parts = ((down_rows, total_width // plan.blocks), (out_rows, thin))
    spread(plan, mine, down_order, parts, down_send, down_keep)
    parts = tuple((up_rows.at[c], thin) for c in range(total_width // chunk))
    spread(plan, mine, up_order, parts + ((query_rows, thin),), up_send, up_keep)


def spread(plan, place, order, parts, send, keep):
    half = plan.blocks // 2
    for target, core in ((send, 1), (keep, 0)):
        start = 0
        for p in range(half):
            block = plan.relative(order, core * half + p) ^ place
            for source, rows in parts:
                target[start : start + rows, :] = source[
                    pl.ds(pl.multiple_of(block * rows, 16), rows), :
                ]
                start += rows


def conv_grad_kernel(
    plan, order, segment_column, d_packed, flat, own, conv, send, keep, d_flat_out, conv_rows
):
    batch, length, _ = segment_column.shape
    width = conv.shape[1]
    slots = length // 3
    masks = [window_masks(segment_column[b], slots) for b in range(batch)]
    back = d_packed[...]
    for i in range(3):
        taps = []
        for b in range(batch):
            start = b * length + i * slots
            part = flat[start : start + slots, :].astype(F32) * masks[b][i]
            taps.append(part.astype(BF16))
        window = jnp.concatenate(taps, axis=0)
        conv_rows[i * width : (i + 1) * width, :] = dot_tn(window, back).astype(BF16)
    _, mine = own_places(plan)
    spread(plan, mine, order, ((conv_rows, 3 * width // plan.blocks),), send, keep)
    for i in range(3):
        from_tap = dot_nt(back, conv[i * width : (i + 1) * width, :])
        for b in range(batch):
            start = b * length + i * slots
            part = from_tap[b * slots : (b + 1) * slots] * masks[b][i]
            d_flat_out[start : start + slots, :] = (part + own[start : start + slots, :]).astype(BF16)


def tail_kernel(
    plan, order, normed, x_in, gain, d_query, d_keys, d_values, d_hidden, gain_ffn_grad,
    w_query, w_key, w_value,
    send, keep, grad_tokens, key_rows, value_rows,
):
    batch, _, length, width = grad_tokens.shape
    key_rows[...] = dot_tn(normed[...], d_keys[...]).astype(BF16)
    value_rows[...] = dot_tn(normed[...], d_values[...]).astype(BF16)
    _, mine = own_places(plan)
    thin = width // plan.blocks
    spread(plan, mine, order, ((key_rows, thin), (value_rows, thin)), send, keep)
    d_normed = (
        dot_nt(d_query[...], w_query[...])
        + dot_nt(d_keys[...], w_key[...])
        + dot_nt(d_values[...], w_value[...])
    )
    unit, inverse_dev = normalize(x_in[...])
    gain_grad = jnp.sum(d_normed * unit, axis=0, keepdims=True)
    d_input = normalize_back(d_normed, unit, inverse_dev, gain[...].astype(F32).reshape(1, width))
    result = (d_hidden[...] + d_input).astype(BF16)
    unorder = order_matrix(length, True)
    for b in range(batch):
        part = result[b * length : (b + 1) * length, :]
        grad_tokens[b, 0] = dot(unorder, part).astype(BF16)
    row = lax.broadcasted_iota(jnp.int32, (EXTRA_ROWS, width), 0)
    gains = jnp.where(row == 0, gain_grad, jnp.where(row == 1, gain_ffn_grad[...], 0.0))
    send[send.shape[0] - EXTRA_ROWS :, :] = gains.astype(BF16)
    keep[keep.shape[0] - EXTRA_ROWS :, :] = gains.astype(BF16)


def finish_kernel(plan, items, count, aliased, n_gains, *refs):
    blocks, refs = refs[: len(items)], refs[len(items) :]
    gains, refs = refs[: min(n_gains, 1)], refs[min(n_gains, 1) + (count if aliased else 0) :]
    targets, token, refs = refs[:count], refs[count], refs[count + 1 :]
    gain_targets, (sent, *stages) = refs[:n_gains], refs[n_gains:]
    token[...] = jnp.zeros_like(token)
    for row, target in enumerate(gain_targets):
        target[...] = gains[0][...].astype(F32)[row : row + 1, :].reshape(-1)
    _, mine = own_places(plan)
    half = plan.blocks // 2
    copies = []
    for source, stage, (layout, parts, core) in zip(blocks, stages, items):
        start = 0
        for p in range(half):
            block = plan.relative(layout, core * half + p) ^ mine
            for rows, target, columns in parts:
                stage[start : start + rows, :] = source[start : start + rows, :].astype(F32)
                spot = pl.ds(pl.multiple_of(block * rows, 16), rows)
                copy = pltpu.make_async_copy(
                    stage.at[pl.ds(start, rows), :],
                    targets[target].at[spot, columns],
                    sent.at[len(copies)],
                )
                copy.start()
                copies.append(copy)
                start += rows
    for copy in copies:
        copy.wait()


def finish(plan, order, name, chosen, cores, targets=(), gains=()):
    items, blocks, shapes = [], [], []
    for part, halves in zip(chosen, cores):
        for core in halves:
            parts = [(rows, len(shapes) + target, columns) for rows, target, columns in part.parts]
            items.append((part.bits, parts, core))
            blocks.append(part.far if core else part.held)
        shapes += part.shapes
    count = len(shapes)
    everywhere = tuple(range(count))
    copies = sum(plan.blocks // 2 * len(parts) for _, parts, _ in items)
    n_gains = 2 * len(gains)
    results = order.call(
        functools.partial(finish_kernel, plan, items, count, bool(targets), n_gains),
        name,
        [(shape, F32) for shape in shapes] + [((8, LANES), F32)]
        + [((array.shape[1],), F32) for array in gains] * 2,
        [pltpu.SemaphoreType.DMA((copies,))] + [pltpu.VMEM(array.shape, F32) for array in blocks],
        anywhere=tuple(range(len(items), len(items) + count)) if targets else (),
        out_anywhere=everywhere,
        aliases={len(items) + number: number for number in everywhere} if targets else None,
        token=count,
    )(*blocks, *gains, *targets)
    return results[:count], results[count + 1 :]


class RowGather:
    def __init__(self, name, plan, order, array, bits):
        self.name, self.plan, self.order = name, plan, order
        self.held, self.bits = array, list(bits)

    def step(self):
        arrived = self.plan.swap(self.held, ("seq", self.bits.pop(0)), self.name)
        if not self.bits:
            return [self.held, arrived]
        rows = self.held.shape[0]
        self.held, = self.order.combine(
            "gather_row", [self.held, arrived], [[(0, 0, rows), (1, 0, rows)]]
        )


class RowScatter:
    def __init__(self, name, plan, order, keep, send, bits):
        self.name, self.plan, self.order, self.keep, self.send = name, plan, order, keep, send
        self.bits = list(bits)

    def step(self, microseconds=EACH):
        if not self.bits:
            return
        arrived = self.plan.swap(self.send, ("seq", self.bits.pop()), self.name)
        rows = self.keep.shape[0]
        half = rows // 2
        outs = [(0, rows)] if not self.bits else [(0, half), (half, half)]
        self.keep, *send = self.order.combine(
            "scatter_row", [self.keep, arrived],
            [[(0, start, size, 1, start)] for start, size in outs], microseconds,
        )
        self.send = send[0] if send else None


class Part:
    def __init__(self, name, plan, order, bits, send, keep, shapes, parts, extra=0):
        self.name, self.plan, self.order, self.bits, self.extra = name, plan, order, bits, extra
        self.send, self.keep = send, keep
        self.shapes, self.parts = shapes, parts
        self.done = 0

    def step(self, microseconds):
        if self.done < len(self.bits):
            self.scatter(self.bits[self.done], microseconds)
        else:
            self.gather(self.bits[2 * len(self.bits) - 1 - self.done], microseconds)
        self.done += 1

    def scatter(self, bit, microseconds):
        arrived = self.plan.swap(self.send, bit, self.name)
        extra = self.extra
        rows = self.keep.shape[0] - extra
        last = [(0, rows, extra, 1, rows)]
        if self.done < len(self.bits) - 1:
            half = rows // 2
            outs = [[(0, start, half, 1, start)] + (last if extra else []) for start in (0, half)]
            self.keep, self.send = self.order.combine(
                "scatter", [self.keep, arrived], outs, microseconds
            )
            return
        outs = [[(0, 0, rows, 1, 0)]] + ([last] if extra else [])
        self.held, *self.sums = self.order.combine(
            "scatter", [self.keep, arrived], outs, microseconds
        )
        for bit in self.plan.rest:
            arrays = [self.held] + self.sums
            arrived = [self.plan.swap(array, bit, self.name) for array in arrays]
            self.held, *self.sums = self.order.combine(
                "scatter_rest", arrays + arrived,
                [
                    [(i, 0, array.shape[0], i + len(arrays), 0)]
                    for i, array in enumerate(arrays)
                ],
            )

    def gather(self, bit, microseconds=EACH):
        arrived = self.plan.swap(self.held, bit, self.name)
        rows = self.held.shape[0]
        self.held, = self.order.combine(
            "gather", [self.held, arrived], [[(0, 0, rows), (1, 0, rows)]], microseconds
        )
        if self.done == 2 * len(self.bits) - 2:
            self.far = self.plan.swap(self.held, self.plan.core, self.name)


def body(
    plan, tokens, segments, cotangent, gain_attn, w_query, w_key, w_value, conv_key, conv_value,
    w_out, gain_ffn, w_up, w_down,
):
    batch, _, length, width = tokens.shape
    slots = length // 3
    square = (width, width)
    positions = batch * length
    flat, flat32 = ((positions, width), BF16), ((positions, width), F32)
    square_here = pltpu.VMEM(square, BF16)
    conv_here = pltpu.VMEM(conv_key.shape, BF16)
    order = Order()
    later = [conv_key, conv_value, w_query, w_key, w_value]
    short = slots * plan.n_seq <= SHORT_ROW
    (
        x, normed, queries, key_rows, value_rows, segment_column, packed_key, packed_value, *here,
    ) = order.call(
        project_kernel,
        "project",
        [flat32] + [flat] * 4 + [((batch, length, 1), F32)]
        + [((batch * slots + EXTRA_ROWS, width), BF16), ((batch * slots, width), BF16)]
        + ([(array.shape, BF16) for array in later] if short else []),
        scratch=([] if short else [conv_here] * 2 + [square_here] * 3)
        + [
            pltpu.VMEM(tokens.shape, BF16), pltpu.VMEM(gain_attn.shape, BF16),
            pltpu.VMEM(segments.shape, jnp.int32), pltpu.SemaphoreType.DMA((8,)),
        ],
        anywhere=tuple(range(8)),
        token=5,
    )(tokens, gain_attn, segments, w_query, w_key, w_value, conv_key, conv_value)

    later = here or later
    steps = len(plan.key_order)
    keys = RowGather("gather_keys", plan, order, packed_key, plan.key_order)
    values = RowGather("gather_values", plan, order, packed_value, plan.value_order)
    for number in range(steps - 1):
        keys.step()
        values.step()

    core = [plan.core]
    x_first, y_first = core + plan.first + plan.tail, core + plan.second + plan.tail
    z_first = core + plan.tail[:1] + plan.first + plan.tail[1:]
    bits = {"A0": y_first, "A1": x_first, "B0": y_first, "B1": x_first, "B2": z_first}
    half = plan.blocks // 2
    thin, down_block, conv_block = (
        rows // plan.blocks for rows in (width, w_down.shape[0], conv_key.shape[0])
    )
    chunks = w_up.shape[1] // width
    everything = slice(None)
    ups = [(thin, 0, slice(c * width, (c + 1) * width)) for c in range(chunks)]
    layouts = {
        "A0": ([w_down.shape, square], [(down_block, 0, everything), (thin, 1, everything)]),
        "A1": ([w_up.shape, square], ups + [(thin, 1, everything)]),
        "B0": ([conv_key.shape], [(conv_block, 0, everything)]),
        "B1": ([conv_value.shape], [(conv_block, 0, everything)]),
        "B2": ([square, square], [(thin, 0, everything), (thin, 1, everything)]),
    }

    def half_rows(name):
        return half * sum(part[0] for part in layouts[name][1])

    total_slots = slots * plan.n_seq
    half_packed = ((batch * total_slots // 2, width), BF16)
    halves = [((half_rows(name), width), BF16) for name in ("A0", "A0", "A1", "A1")]
    flat_here = pltpu.VMEM((positions, width), BF16)
    wide_here = pltpu.VMEM((positions, w_up.shape[1]), BF16)
    copied = [] if short else [pltpu.SemaphoreType.DMA((plan.n_seq * (1 + 2 * batch),))]
    layer_out, d_hidden, d_query, d_key_own, d_value_own, *outs, gain_ffn_grad = order.call(
        functools.partial(layer_kernel, plan, short, bits["A0"], bits["A1"]),
        "layer",
        [(tokens.shape, BF16), flat32, flat, flat32, flat32] + [half_packed] * 4 + halves
        + [((1, width), F32)],
        scratch=[
            pltpu.VMEM((batch, total_slots, width), BF16),
            pltpu.VMEM((batch, total_slots, width), BF16),
            pltpu.VMEM((plan.n_seq, EXTRA_ROWS, LANES), BF16),
            pltpu.VMEM((batch, length, total_slots), F32),
            pltpu.VMEM((batch * GROUPS, 2 * length, LANES), F32),
            pltpu.VMEM((batch * GROUPS, 2 * length, total_slots) if short else (1, 8, LANES), F32),
            pltpu.VMEM((positions, width), F32),
            pltpu.VMEM((positions, width), F32),
            flat_here, flat_here, wide_here, wide_here, flat_here, flat_here, flat_here,
            pltpu.VMEM(w_down.shape, BF16),
            pltpu.VMEM((chunks, width, width), BF16),
            square_here, square_here,
        ]
        + copied,
        anywhere=() if short else (8, 9, 10, 11),
        vmem=VMEM_SMALL if short else VMEM_LARGE,
        token=-1,
    )(
        x, normed, cotangent, queries, key_rows, value_rows, segment_column, gain_ffn,
        *keys.step(), *values.step(), w_out, w_up, w_down,
    )
    rows = [
        RowScatter("K", plan, order, outs[0], outs[1], plan.key_order),
        RowScatter("V", plan, order, outs[2], outs[3], plan.value_order),
    ]
    chains, d_flats = {"K": rows[0], "V": rows[1]}, {}
    for name, (send, keep) in (("A0", outs[4:6]), ("A1", outs[6:8])):
        chains[name] = Part(name, plan, order, bits[name], send, keep, *layouts[name])

    def make(name, kernel, outs, scratch, operands, extra=0):
        total = half_rows(name) + extra
        send, keep, *others = order.call(
            functools.partial(kernel, plan, bits[name]),
            kernel.__name__,
            [((total, width), BF16)] * 2 + outs,
            scratch=scratch,
        )(*operands)
        chains[name] = Part(name, plan, order, bits[name], send, keep, *layouts[name], extra)
        return others

    for event in EVENTS:
        if event in ("TK", "TV"):
            number = 0 if event == "TK" else 1
            row = rows[number]
            while row.bits:
                row.step()
            d_flat, = make(
                f"B{number}", conv_grad_kernel, [flat], [conv_here],
                (
                    segment_column, row.keep, (key_rows, value_rows)[number],
                    (d_key_own, d_value_own)[number], later[number],
                ),
            )
            d_flats[event] = d_flat
        elif event == "T3":
            grad_tokens, = make(
                "B2", tail_kernel, [(tokens.shape, BF16)], [square_here, square_here],
                (
                    normed, x, gain_attn, d_query, d_flats["TK"], d_flats["TV"], d_hidden,
                    gain_ffn_grad, *later[2:],
                ),
                EXTRA_ROWS,
            )
        elif event == "Af":
            grads, gains = finish(
                plan, order, "finish", [chains["A0"], chains["A1"]], [(0, 1)] * 2, (),
                chains["B2"].sums,
            )
            grad_down, grad_out, grad_up, grad_query = grads
        elif event in ("Bn", "Bf"):
            chosen = [chains[name] for name in ("B0", "B1", "B2")]
            previous = () if event == "Bn" else results
            cores = [(0,), (0,), (0, 1)] if event == "Bn" else [(1,), (1,), ()]
            results, _ = finish(plan, order, "finish", chosen, cores, previous)
        else:
            name, _, cost = event.partition(":")
            chains[name].step(float(cost or EACH))
    grad_conv_key, grad_conv_value, grad_key, grad_value = results
    return (
        layer_out, grad_tokens, gains[0], grad_query, grad_key, grad_value,
        grad_conv_key, grad_conv_value, grad_out, gains[1], grad_up, grad_down,
    )


def solution(mesh):
    packed = P(None, "rows", "seq", None)
    in_specs = (packed, P(None, "rows", "seq"), packed) + (P(),) * 10
    out_specs = (packed, packed) + (P(),) * 10
    return jax.shard_map(
        functools.partial(body, Plan(mesh)),
        mesh=mesh, in_specs=in_specs, out_specs=out_specs, check_vma=False,
    )
```
